32 devices in a mesh: expert: 4 (over y, x), fsdp: 8 (over z, core).
Axes of the slice: x: 2, y: 2, z: 4, core: 2. Of those that a mesh axis runs over, the one named last changes fastest.
Arguments:
- branch_wo: bfloat16 [4, 4096, 4096], P('expert', 'fsdp'), may hold values from -3 to 3
- context: bfloat16 [1024, 4096], P('fsdp', 'expert'), may hold values from -6 to 6
- residual: bfloat16 [1024, 4096], P('fsdp', 'expert'), may hold values from -160 to 160
- norm_gain: bfloat16 [4096], P('expert'), may hold values from 0.25 to 1.75
- router_w: bfloat16 [4096, 4], P('expert'), may hold values from -0.1875 to 0.1875
- gate_w: bfloat16 [4, 4096, 8192], P('expert', None, 'fsdp'), may hold values from -0.09375 to 0.09375
- up_w: bfloat16 [4, 4096, 8192], P('expert', None, 'fsdp'), may hold values from -0.09375 to 0.09375
- expert_ids: int32 [1024, 2], P('fsdp'), may hold values from 0 to 3, as said below
- slot_ids: int32 [1024, 2], P('fsdp'), may hold values from 0 to 95, as said below
- cot_hidden: bfloat16 [4, 768, 8192], P('expert', None, 'fsdp'), may hold values from -1.1953125 to 1.1953125
Outputs:
- merged_wo: bfloat16 [4096, 4096], P('fsdp', 'expert')
- hidden: bfloat16 [4, 768, 8192], P('expert', None, 'fsdp')
- grad_gate: bfloat16 [4, 4096, 8192], P('expert', None, 'fsdp')
- grad_up: bfloat16 [4, 4096, 8192], P('expert', None, 'fsdp')
The draws below stay inside these ranges and needn't reach their ends.
Inputs may be any that keep to these rules, and one draw needn't show every extreme that they name: expert_ids[t, 0] and expert_ids[t, 1] differ. Within each aligned block of 128 tokens (the tokens of one index of fsdp) no expert is named more than 96 times, and some expert is named exactly 96 times in every block. Within each aligned block of 128 tokens the pairs (expert_ids[t, k], slot_ids[t, k]) are all different, and an expert named c times in the block uses exactly the slots 0 to c - 1.
All inputs are finite; a program needn't handle non-finite values.
Results may differ from the reference program's by a relative error of at most 0.015.
Values may be sent and summed in bfloat16 or wider, within the bound.
No kernel may reach another device: no remote copies, remote signals or barrier semaphores. Data moves between devices by JAX's collectives and lax.ppermute only.
A program may use at most 128 MiB of HBM per device.

```python
import math
import jax
import jax.numpy as jnp
from jax import lax

D = 4096
FF = 8192
TOK_DEV = 128
EXPERTS = 4
TOKENS = 1024
CAP = 96
ROWS = 768


def route_tables(key):
    blocks = TOKENS // TOK_DEV
    mean_load = 2 * TOK_DEV // EXPERTS
    key_busy, key_perm, key_extra, key_order, key_swap = jax.random.split(key, 5)
    busiest = jax.random.randint(key_busy, (), 0, EXPERTS)
    perms = jax.vmap(lambda single: jax.random.permutation(single, EXPERTS))(jax.random.split(key_perm, blocks))
    scores = jnp.where(jnp.arange(EXPERTS)[None, :] == busiest, EXPERTS, perms)
    order = jnp.argsort(-scores, axis=1, stable=True).astype(jnp.int32)
    extra = jax.random.randint(key_extra, (blocks, EXPERTS - 1), 0, mean_load // 4 + 1)
    shifted = jnp.roll(extra, 1, axis=1)
    base = jnp.concatenate([jnp.full((1,), CAP, jnp.int32), jnp.full((EXPERTS - 3,), mean_load, jnp.int32), jnp.full((2,), 3 * mean_load // 4, jnp.int32)])
    change = jnp.concatenate([jnp.zeros((blocks, 1), jnp.int32), (extra - shifted).astype(jnp.int32)], axis=1)
    counts = base[None, :] + change
    ends = jnp.cumsum(counts, axis=1)
    starts = ends - counts
    places = jnp.arange(2 * TOK_DEV, dtype=jnp.int32)
    ranks = jnp.sum((places[None, :, None] >= ends[:, None, :]).astype(jnp.int32), axis=2)
    labels = jnp.take_along_axis(order, ranks, axis=1)
    slots = places[None, :] - jnp.take_along_axis(starts, ranks, axis=1)
    shuffle = jax.vmap(lambda single: jax.random.permutation(single, TOK_DEV))(jax.random.split(key_order, blocks)).astype(jnp.int32)
    first_id = jnp.take_along_axis(labels, shuffle, axis=1)
    second_id = jnp.take_along_axis(labels, shuffle + TOK_DEV, axis=1)
    first_slot = jnp.take_along_axis(slots, shuffle, axis=1)
    second_slot = jnp.take_along_axis(slots, shuffle + TOK_DEV, axis=1)
    swapped = jax.random.randint(key_swap, (blocks, TOK_DEV), 0, 2) == 1
    ids_pair = jnp.stack([jnp.where(swapped, second_id, first_id), jnp.where(swapped, first_id, second_id)], axis=2)
    slot_pair = jnp.stack([jnp.where(swapped, second_slot, first_slot), jnp.where(swapped, first_slot, second_slot)], axis=2)
    return (ids_pair.reshape(TOKENS, 2).astype(jnp.int32), slot_pair.reshape(TOKENS, 2).astype(jnp.int32))


def draw_expert_ids(key, part):
    return route_tables(jax.random.fold_in(key, 11))[0]


def draw_slot_ids(key, part):
    return route_tables(jax.random.fold_in(key, 11))[1]


def context_values(key):
    values = jnp.clip(jax.random.normal(key, (TOKENS, D), jnp.float32), -6.0, 6.0)
    return values


def draw_context(key, part):
    return context_values(jax.random.fold_in(key, 23)).astype(jnp.bfloat16)


def draw_branch_wo(key, part):
    key_values = jax.random.fold_in(key, 31)
    spread_std = (EXPERTS / D) ** 0.5
    values = jnp.clip(jax.random.normal(key_values, (EXPERTS, D, D), jnp.float32), -6.0, 6.0)
    row_pos = jnp.arange(D, dtype=jnp.int32)[:, None]
    col_pos = jnp.arange(D, dtype=jnp.int32)[None, :]
    diagonal = jnp.where(row_pos == col_pos, 0.4, 0.0).astype(jnp.float32)
    return (values * spread_std + diagonal[None, :, :]).astype(jnp.bfloat16)


def draw_residual(key, part):
    shared = context_values(jax.random.fold_in(key, 23))
    key_base = jax.random.fold_in(jax.random.fold_in(key, 29), 0)
    key_cols = jax.random.fold_in(jax.random.fold_in(key, 29), 1)
    key_rows = jax.random.fold_in(jax.random.fold_in(key, 29), 2)
    key_align = jax.random.fold_in(jax.random.fold_in(key, 29), 4)
    position = jnp.arange(D, dtype=jnp.float32) / D
    column_scale = jnp.exp(math.log(3.0) * position) * jax.random.uniform(key_cols, (D,), jnp.float32, 0.7, 1.4)
    row_scale = jnp.exp(jax.random.uniform(key_rows, (TOKENS, 1), jnp.float32, math.log(0.5), math.log(5.0)))
    values = jax.random.normal(key_base, (TOKENS, D), jnp.float32)
    values = jnp.clip(values, -6.0, 6.0)
    align = jax.random.uniform(key_align, (TOKENS, 1), jnp.float32, -2.5, 2.5)
    total = values * column_scale[None, :] * row_scale + align * shared
    return jnp.clip(total, -160.0, 160.0).astype(jnp.bfloat16)


def shard_levels(rng, shape, shards, low, largest):
    def one(dim, shards_of):
        steps = jax.random.uniform(jax.random.fold_in(jax.random.fold_in(rng, 6), dim), (shards_of,), jnp.float32, low / len(shards), largest / len(shards))
        return jnp.repeat(jnp.exp(steps), shape[dim] // shards_of).reshape((-1,) + (1,) * (len(shape) - dim - 1))

    factor_of = one(*shards[0])
    for cut in shards[1:]:
        factor_of = factor_of * one(*cut)
    return factor_of


def normal_values(rng, shape, width, bound, shards=(), kind=jnp.bfloat16):
    entries = jax.random.normal(rng, shape, jnp.float32) * width
    if len(shards) > 0:
        entries = shard_levels(rng, shape, shards, -0.22, 0.18) * entries
    return jnp.clip(entries, min=-bound, max=bound).astype(kind)


def setup_inputs(seed: int = 0) -> dict:
    seeds = jax.random.split(jax.random.key(seed), 11)
    return {
        "branch_wo": draw_branch_wo(jax.random.fold_in(seeds[10], 71), 0),
        "context": draw_context(jax.random.fold_in(seeds[10], 71), 0),
        "residual": draw_residual(jax.random.fold_in(seeds[10], 71), 0),
        "norm_gain": jnp.clip(1.0 + 0.15 * jax.random.normal(seeds[3], (D,), jnp.float32), 0.25, 1.75).astype(jnp.bfloat16),
        "router_w": normal_values(seeds[4], (D, EXPERTS), (D // 4) ** -0.5, 0.1875, ((0, 4),)),
        "gate_w": normal_values(seeds[5], (EXPERTS, D, FF), D ** -0.5, 0.09375, ((0, 4), (2, 8))),
        "up_w": normal_values(seeds[6], (EXPERTS, D, FF), D ** -0.5, 0.09375, ((0, 4), (2, 8))),
        "expert_ids": draw_expert_ids(jax.random.fold_in(seeds[10], 71), 0),
        "slot_ids": draw_slot_ids(jax.random.fold_in(seeds[10], 71), 0),
        "cot_hidden": normal_values(seeds[9], (EXPERTS, ROWS, FF), 0.2, 1.1953125, ((0, 4), (2, 8))),
    }


def expert_step(items):
    rows, slot_weight, gate_weight, up_weight, cotangent = items
    gate_pre = jnp.dot(rows, gate_weight, preferred_element_type=jnp.float32)
    up_pre = jnp.dot(rows, up_weight, preferred_element_type=jnp.float32)
    sig_gate = jax.nn.sigmoid(gate_pre)
    act_gate = gate_pre * sig_gate
    weight_col = slot_weight.astype(jnp.float32)[:, None]
    hidden = (weight_col * act_gate * up_pre).astype(jnp.bfloat16)
    d_pre = cotangent.astype(jnp.float32) * weight_col
    d_gate = (d_pre * up_pre * sig_gate * (1.0 + gate_pre * (1.0 - sig_gate))).astype(jnp.bfloat16)
    d_up = (d_pre * act_gate).astype(jnp.bfloat16)
    grad_gate = jnp.dot(rows.T, d_gate, preferred_element_type=jnp.float32).astype(jnp.bfloat16)
    grad_up = jnp.dot(rows.T, d_up, preferred_element_type=jnp.float32).astype(jnp.bfloat16)
    return (hidden, grad_gate, grad_up)

def reference(branch_wo, context, residual, norm_gain, router_w, gate_w, up_w, expert_ids, slot_ids, cot_hidden):
    summed = lax.optimization_barrier(jnp.sum(branch_wo.astype(jnp.float32), axis=0))
    merged_wo = (summed / EXPERTS).astype(jnp.bfloat16)
    attention = jnp.dot(context, merged_wo, preferred_element_type=jnp.float32)
    hstate = residual.astype(jnp.float32) + attention
    scaled = hstate * norm_gain.astype(jnp.float32)
    inverse = lax.rsqrt(lax.optimization_barrier(jnp.mean(hstate * hstate, axis=1)) + 1e-05)
    normed = (scaled * inverse[:, None]).astype(jnp.bfloat16)
    logits = inverse[:, None] * jnp.dot(scaled, router_w.astype(jnp.float32), precision=lax.Precision.HIGHEST)
    picked = jnp.take_along_axis(logits, expert_ids, axis=1)
    probs = jax.nn.sigmoid(picked - picked[:, ::-1]).astype(jnp.bfloat16)
    block_index = (jnp.arange(TOKENS) // TOK_DEV).astype(jnp.int32)
    row_index = (block_index[:, None] * CAP + slot_ids).astype(jnp.int32)
    spread = jnp.broadcast_to(normed[:, None, :], (TOKENS, 2, D))
    dispatched = jnp.zeros((EXPERTS, ROWS, D), jnp.bfloat16).at[expert_ids, row_index].set(spread)
    slot_weight = jnp.zeros((EXPERTS, ROWS), jnp.bfloat16).at[expert_ids, row_index].set(probs)
    hidden, grad_gate, grad_up = lax.map(expert_step, (dispatched, slot_weight, gate_w, up_w, cot_hidden))
    return (merged_wo, hidden, grad_gate, grad_up)
```

```python
import jax
import jax.numpy as jnp
from jax import lax
from jax.sharding import PartitionSpec as P


def exchange(value, axis, offset):
    size = lax.axis_size(axis)
    return lax.ppermute(value, axis, [(i, i ^ offset) for i in range(size)])


def pick(value, index, axis):
    return lax.dynamic_index_in_dim(value, index, axis, keepdims=False)


def per_device(
    branch_wo,
    context,
    residual,
    norm_gain,
    router_w,
    gate_w,
    up_w,
    expert_ids,
    slot_ids,
    cot_hidden,
):
    experts = lax.axis_size("expert")
    blocks = lax.axis_size("fsdp")
    planes = blocks // 2
    expert = lax.axis_index("expert")
    block = lax.axis_index("fsdp")
    plane, core = block // 2, block % 2
    tokens, columns = context.shape
    width = columns * experts
    capacity = cot_hidden.shape[1] // blocks

    branch = branch_wo[0]

    def branch_columns(offset):
        return lax.dynamic_slice_in_dim(branch, (expert ^ offset) * columns, columns, 1)

    received = [exchange(branch_columns(k), "expert", k) for k in range(1, experts)]

    full_context = lax.all_gather(context, "expert", axis=1, tiled=True)
    features = width // blocks
    context_rows = lax.all_to_all(full_context, "fsdp", split_axis=1, concat_axis=0, tiled=True)
    context_rows = context_rows.reshape(planes, 2, tokens, features)
    ids_all = lax.all_gather(jnp.concatenate([expert_ids, slot_ids], axis=1), "fsdp", axis=0)

    summed = branch_columns(0).astype(jnp.float32)
    for part in received:
        summed = summed + part.astype(jnp.float32)
    merged = (summed / experts).astype(jnp.bfloat16)

    def attend(which):
        rows = pick(context_rows, which, 1).reshape(planes * tokens, features)
        out = jnp.dot(rows, merged, preferred_element_type=jnp.float32)
        return out.reshape(planes, tokens, columns)

    swapped = exchange(attend(1 - core).astype(jnp.bfloat16), "fsdp", 1)
    pair = attend(core) + swapped.astype(jnp.float32)
    pair_sent = pair.astype(jnp.bfloat16)
    arrived = [
        exchange(pick(pair_sent, plane ^ k, 0), "fsdp", 2 * k) for k in range(1, planes)
    ]
    hstate = residual.astype(jnp.float32) + pick(pair, plane, 0)
    for part in arrived:
        hstate = hstate + part.astype(jnp.float32)
    scaled = hstate * norm_gain.astype(jnp.float32)
    sent_tokens = scaled.astype(jnp.bfloat16)
    all_tokens = lax.all_gather(sent_tokens, "fsdp", axis=0).reshape(planes, 2, tokens, columns)
    own_tokens = pick(all_tokens, core, 1)

    partial_logits = jnp.dot(scaled, router_w.astype(jnp.float32), precision=lax.Precision.HIGHEST)
    squares, logits = lax.psum((jnp.sum(hstate * hstate, axis=1), partial_logits), "expert")
    inverse = lax.rsqrt(squares / width + 1e-05)
    logits = logits * inverse[:, None]
    expert_range = jnp.arange(experts, dtype=jnp.int32)
    selected = (expert_ids[:, :, None] == expert_range[None, None, :]).astype(jnp.float32)
    picked = jnp.sum(selected * logits[:, None, :], axis=2)
    probs = jax.nn.sigmoid(picked - picked[:, ::-1])
    own_slots = expert * capacity + jnp.arange(capacity, dtype=jnp.int32)
    codes_here = expert_ids * capacity + slot_ids
    matches = codes_here[None, :, :] == own_slots[:, None, None]
    slot_prob = jnp.sum(jnp.where(matches, probs[None, :, :], 0.0), axis=(1, 2))
    slot_inverse = jnp.sum(jnp.where(matches, inverse[None, :, None], 0.0), axis=(1, 2))
    slot_prob = slot_prob.astype(jnp.bfloat16).astype(jnp.float32)
    slot_all = lax.all_gather(jnp.stack([slot_prob, slot_inverse]), "fsdp", axis=0)
    weight_col = slot_all[:, 0].reshape(-1, 1)
    inverse_col = slot_all[:, 1].reshape(-1, 1)

    own_ids = pick(ids_all.reshape(planes, 2, tokens, 4), core, 1)
    codes = own_ids[..., :2] * capacity + own_ids[..., 2:]

    def slots_of(which):
        targets = which * capacity + jnp.arange(capacity, dtype=jnp.int32)
        one_hot = jnp.any(codes[:, None] == targets[None, :, None, None], axis=3)
        return lax.dot_general(
            one_hot.astype(jnp.bfloat16),
            own_tokens,
            (((2,), (1,)), ((0,), (0,))),
            preferred_element_type=jnp.float32,
        ).astype(jnp.bfloat16)

    rows_half = jnp.zeros((planes, capacity, width), jnp.bfloat16)
    for k in range(experts):
        piece = slots_of(expert ^ k)
        if k > 0:
            piece = exchange(piece, "expert", k)
        rows_half = lax.dynamic_update_slice_in_dim(rows_half, piece, (expert ^ k) * columns, 2)
    rows_other = exchange(rows_half, "fsdp", 1)
    first = jnp.where(core == 0, rows_half, rows_other)
    second = jnp.where(core == 0, rows_other, rows_half)
    all_rows = jnp.stack([first, second], axis=1).reshape(-1, width)

    gate_pre = inverse_col * jnp.dot(all_rows, gate_w[0], preferred_element_type=jnp.float32)
    up_pre = inverse_col * jnp.dot(all_rows, up_w[0], preferred_element_type=jnp.float32)
    sig_gate = jax.nn.sigmoid(gate_pre)
    act_gate = gate_pre * sig_gate
    hidden = (weight_col * act_gate * up_pre).astype(jnp.bfloat16)
    d_pre = cot_hidden[0].astype(jnp.float32) * (weight_col * inverse_col)
    d_gate = (d_pre * up_pre * sig_gate * (1.0 + gate_pre * (1.0 - sig_gate))).astype(jnp.bfloat16)
    d_up = (d_pre * act_gate).astype(jnp.bfloat16)
    contract = (((0,), (0,)), ((), ()))
    grad_gate = lax.dot_general(all_rows, d_gate, contract, preferred_element_type=jnp.float32)
    grad_up = lax.dot_general(all_rows, d_up, contract, preferred_element_type=jnp.float32)
    return (
        merged,
        hidden[None],
        grad_gate.astype(jnp.bfloat16)[None],
        grad_up.astype(jnp.bfloat16)[None],
    )


def solution(mesh):
    placed = (
        P("expert", "fsdp", None),
        P("fsdp", "expert"),
        P("fsdp", "expert"),
        P("expert"),
        P("expert", None),
        P("expert", None, "fsdp"),
        P("expert", None, "fsdp"),
        P("fsdp", None),
        P("fsdp", None),
        P("expert", None, "fsdp"),
    )
    return jax.shard_map(
        per_device,
        mesh=mesh,
        in_specs=placed,
        out_specs=(
            P("fsdp", "expert"),
            P("expert", None, "fsdp"),
            P("expert", None, "fsdp"),
            P("expert", None, "fsdp"),
        ),
        check_vma=False,
    )
```

```python
import jax
import jax.numpy as jnp
from jax import lax
from jax.sharding import PartitionSpec as P

CHUNKS = 2


def exchange(value, axis, offset):
    size = lax.axis_size(axis)
    return lax.ppermute(value, axis, [(i, i ^ offset) for i in range(size)])


def pick(value, index, axis):
    return lax.dynamic_index_in_dim(value, index, axis, keepdims=False)


def pad_rows(value, multiple):
    return jnp.pad(value, ((0, -value.shape[0] % multiple), (0, 0)))


def branch_sum(branch, expert, experts, columns, start, count):
    half = branch.shape[0] // 2
    bits = [1 << i for i in range(experts.bit_length() - 1)]
    halves = []
    for rows, order in ((branch[:half], bits), (branch[half:], bits[::-1])):
        held = {
            k: lax.dynamic_slice_in_dim(rows, (expert ^ k) * columns + start, count, 1)
            for k in range(experts)
        }
        for bit in order:
            away = [k for k in held if k & bit]
            sent = jnp.stack([held[k].astype(jnp.bfloat16) for k in away])
            got = exchange(sent, "expert", bit)
            held = {
                k ^ bit: held[k ^ bit].astype(jnp.float32) + got[i].astype(jnp.float32)
                for i, k in enumerate(away)
            }
        halves.append(held[0])
    return jnp.concatenate(halves)


def per_device(
    branch_wo,
    context,
    residual,
    norm_gain,
    router_w,
    gate_w,
    up_w,
    expert_ids,
    slot_ids,
    cot_hidden,
):
    experts = lax.axis_size("expert")
    blocks = lax.axis_size("fsdp")
    planes = blocks // 2
    expert = lax.axis_index("expert")
    block = lax.axis_index("fsdp")
    plane, core = block // 2, block % 2
    tokens, columns = context.shape
    width = columns * experts
    features = width // blocks
    capacity = cot_hidden.shape[1] // blocks
    hidden_units = cot_hidden.shape[2]
    part = columns // CHUNKS

    extra = jnp.concatenate([norm_gain[None], router_w.T])
    packed = pad_rows(jnp.concatenate([context, extra]), 16)
    full = jnp.zeros((packed.shape[0], width), jnp.bfloat16)
    for k in range(experts):
        piece = exchange(packed, "expert", k) if k else packed
        full = lax.dynamic_update_slice_in_dim(full, piece, (expert ^ k) * columns, 1)
    gain_all = full[tokens].astype(jnp.float32)
    router_all = full[tokens + 1 : tokens + 1 + experts]

    ids = jnp.concatenate([expert_ids, slot_ids], axis=1).astype(jnp.bfloat16)
    id_rows = ids.size // features
    to_blocks = jnp.concatenate(
        [
            full[:tokens].reshape(tokens, blocks, features).transpose(1, 0, 2),
            jnp.broadcast_to(ids.reshape(1, id_rows, features), (blocks, id_rows, features)),
        ],
        axis=1,
    )
    to_blocks = jnp.pad(to_blocks, ((0, 0), (0, -to_blocks.shape[1] % 16), (0, 0)))
    from_blocks = lax.all_to_all(to_blocks, "fsdp", split_axis=0, concat_axis=0, tiled=True)
    context_rows = from_blocks[:, :tokens].reshape(planes, 2, tokens, features)
    ids_all = from_blocks[:, tokens : tokens + id_rows].reshape(planes, 2, tokens, 2, 2)
    ids_all = jnp.stack([pick(ids_all, plane ^ k, 0) for k in range(planes)])
    ids_all = ids_all.astype(jnp.int32)
    expert_of, slot_of = ids_all[:, :, :, 0], ids_all[:, :, :, 1]
    context_sides = [
        pick(context_rows, side, 1).reshape(planes * tokens, features) for side in (core, 1 - core)
    ]
    codes = pick(expert_of * capacity + slot_of, core, 1)

    def slot_choice(which):
        targets = which * capacity + jnp.arange(capacity, dtype=jnp.int32)
        one_hot = jnp.any(codes[:, None] == targets[None, :, None, None], axis=3)
        return one_hot.astype(jnp.bfloat16)

    choices = [slot_choice(expert ^ k) for k in range(experts)]

    own_slots = jnp.arange(capacity, dtype=jnp.int32)
    hits = (slot_of[:, :, None] == own_slots[:, None, None]) & (expert_of[:, :, None] == expert)
    expert_range = jnp.arange(experts, dtype=jnp.int32)
    chosen = (expert_of[..., None] == expert_range).astype(jnp.float32)
    signs = chosen - chosen[:, :, :, ::-1]
    signs = jnp.einsum("pcstk,pctke->pcse", hits.astype(jnp.float32), signs).reshape(-1, experts)
    filled = jnp.any(hits, axis=(3, 4)).reshape(-1, 1)

    merged_parts = []
    row_parts = []
    for c in range(CHUNKS):
        span = slice(c * part, (c + 1) * part)
        summed = branch_sum(branch_wo[0], expert, experts, columns, c * part, part)
        merged = (summed / experts).astype(jnp.bfloat16)
        merged_parts.append(merged)

        def attend(rows):
            out = jnp.dot(rows, merged, preferred_element_type=jnp.float32)
            return out.reshape(planes, tokens, part)

        swapped = exchange(attend(context_sides[1]).astype(jnp.bfloat16), "fsdp", 1)
        pair = attend(context_sides[0]) + swapped.astype(jnp.float32)
        pair_sent = pair.astype(jnp.bfloat16)
        hstate = residual[:, span].astype(jnp.float32) + pick(pair, plane, 0)
        for k in range(1, planes):
            arrived = exchange(pick(pair_sent, plane ^ k, 0), "fsdp", 2 * k)
            hstate = hstate + arrived.astype(jnp.float32)
        scaled = (hstate * norm_gain[span].astype(jnp.float32)).astype(jnp.bfloat16)
        own_tokens = jnp.stack(
            [exchange(scaled, "fsdp", 2 * k) if k else scaled for k in range(planes)]
        )

        rows_half = jnp.zeros((planes, capacity, experts * part), jnp.bfloat16)
        for k in range(experts):
            piece = lax.dot_general(
                choices[k],
                own_tokens,
                (((2,), (1,)), ((0,), (0,))),
                preferred_element_type=jnp.float32,
            ).astype(jnp.bfloat16)
            if k > 0:
                piece = exchange(piece, "expert", k)
            rows_half = lax.dynamic_update_slice_in_dim(rows_half, piece, (expert ^ k) * part, 2)
        rows_other = exchange(rows_half, "fsdp", 1)
        first = jnp.where(core == 0, rows_half, rows_other)
        second = jnp.where(core == 0, rows_other, rows_half)
        row_parts.append(jnp.stack([first, second], axis=1).reshape(-1, experts, part))

    by_part = lambda value: value.reshape(value.shape[:-1] + (experts, CHUNKS, part))
    gains = by_part(gain_all)
    routers = by_part(router_all)
    gate_by_part = gate_w[0].reshape(experts, CHUNKS, part, hidden_units)
    up_by_part = up_w[0].reshape(experts, CHUNKS, part, hidden_units)
    squares = logits = gate_pre = up_pre = 0.0
    for c in range(CHUNKS):
        rows = row_parts[c]
        squares += jnp.sum((rows.astype(jnp.float32) / gains[:, c]) ** 2, axis=(1, 2))
        logits += jnp.einsum(
            "rep,kep->rk", rows, routers[:, :, c], preferred_element_type=jnp.float32
        )
        for k in range(experts):
            gate_pre += jnp.dot(rows[:, k], gate_by_part[k, c], preferred_element_type=jnp.float32)
            up_pre += jnp.dot(rows[:, k], up_by_part[k, c], preferred_element_type=jnp.float32)
    inverse_col = lax.rsqrt(squares[:, None] / width + 1e-05)
    margin = jnp.sum(logits * signs, axis=1, keepdims=True) * inverse_col
    weight_col = jnp.where(filled, jax.nn.sigmoid(margin), 0.0)
    weight_col = weight_col.astype(jnp.bfloat16).astype(jnp.float32)

    def reorder(value):
        value = value.reshape(planes, -1, hidden_units)
        return jnp.stack([pick(value, plane ^ k, 0) for k in range(planes)]).reshape(-1, hidden_units)

    gate_pre = inverse_col * gate_pre
    up_pre = inverse_col * up_pre
    sig_gate = jax.nn.sigmoid(gate_pre)
    act_gate = gate_pre * sig_gate
    hidden = reorder((weight_col * act_gate * up_pre).astype(jnp.bfloat16))
    d_pre = reorder(cot_hidden[0]).astype(jnp.float32) * (weight_col * inverse_col)
    d_gate = (d_pre * up_pre * sig_gate * (1.0 + gate_pre * (1.0 - sig_gate))).astype(jnp.bfloat16)
    d_up = (d_pre * act_gate).astype(jnp.bfloat16)
    all_rows = jnp.stack(row_parts, axis=2).reshape(-1, width)
    contract = (((0,), (0,)), ((), ()))
    grad_gate = lax.dot_general(all_rows, d_gate, contract, preferred_element_type=jnp.float32)
    grad_up = lax.dot_general(all_rows, d_up, contract, preferred_element_type=jnp.float32)
    return (
        jnp.concatenate(merged_parts, axis=1),
        hidden[None],
        grad_gate.astype(jnp.bfloat16)[None],
        grad_up.astype(jnp.bfloat16)[None],
    )


def solution(mesh):
    placed = (
        P("expert", "fsdp", None),
        P("fsdp", "expert"),
        P("fsdp", "expert"),
        P("expert"),
        P("expert", None),
        P("expert", None, "fsdp"),
        P("expert", None, "fsdp"),
        P("fsdp", None),
        P("fsdp", None),
        P("expert", None, "fsdp"),
    )
    return jax.shard_map(
        per_device,
        mesh=mesh,
        in_specs=placed,
        out_specs=(
            P("fsdp", "expert"),
            P("expert", None, "fsdp"),
            P("expert", None, "fsdp"),
            P("expert", None, "fsdp"),
        ),
        check_vma=False,
    )
```

```python
import functools

import jax
import jax.numpy as jnp
from jax import lax
from jax.experimental import pallas as pl
from jax.experimental.pallas import tpu as pltpu
from jax.sharding import PartitionSpec as P

CHUNKS = 2
VMEM_LIMIT = 50 * 1024 * 1024


def exchange(value, axis, offset):
    size = lax.axis_size(axis)
    return lax.ppermute(value, axis, [(i, i ^ offset) for i in range(size)])


def pick(value, index, axis):
    return lax.dynamic_index_in_dim(value, index, axis, keepdims=False)


def bits_of(size):
    return size.bit_length() - 1


def whole(shape):
    return pl.BlockSpec(shape, lambda *_: (0,) * len(shape))


def smem():
    return pl.BlockSpec(memory_space=pltpu.SMEM)


def params():
    return pltpu.CompilerParams(vmem_limit_bytes=VMEM_LIMIT)


def signs_kernel(experts, position_ref, ids_ref, out_ref):
    blocks, capacity, lanes = out_ref.shape
    tokens = ids_ref.shape[2]
    expert = position_ref[0]
    slots = lax.broadcasted_iota(jnp.int32, (capacity, tokens), 0)
    rows = lax.broadcasted_iota(jnp.int32, (lanes, tokens), 0)
    last = lax.broadcasted_iota(jnp.int32, (capacity, lanes), 1) == lanes - 1
    for b in range(blocks):
        ids = ids_ref[b]
        e0, e1, s0, s1 = ids[0:1], ids[1:2], ids[2:3], ids[3:4]
        hit0 = jnp.where((e0 == expert) & (s0 == slots), 1.0, 0.0)
        hit1 = jnp.where((e1 == expert) & (s1 == slots), 1.0, 0.0)
        table = jnp.where(e0 == rows - 1, 1.0, 0.0) - jnp.where(e1 == rows - 1, 1.0, 0.0)
        signs = lax.dot_general(
            (hit0 - hit1).astype(jnp.bfloat16),
            table.astype(jnp.bfloat16),
            (((1,), (1,)), ((), ())),
            preferred_element_type=jnp.float32,
        )
        filled = jnp.sum(hit0 + hit1, axis=1, keepdims=True)
        out_ref[b] = jnp.where(last, filled, signs)


def dispatch_kernel(position_ref, ids_ref, *refs):
    *token_refs, out_ref = refs
    experts, planes, capacity, part = out_ref.shape
    tokens = ids_ref.shape[2]
    plane, core = position_ref[1], position_ref[2]
    slots = lax.broadcasted_iota(jnp.int32, (experts * capacity, tokens), 0)
    for k in range(planes):
        source = plane ^ k
        ids = ids_ref[source * 2 + core]
        code0 = ids[0:1] * capacity + ids[2:3]
        code1 = ids[1:2] * capacity + ids[3:4]
        one_hot = jnp.where((code0 == slots) | (code1 == slots), 1.0, 0.0).astype(jnp.bfloat16)
        picked = jnp.dot(one_hot, token_refs[k][...], preferred_element_type=jnp.float32)
        out_ref[:, source] = picked.reshape(experts, capacity, part).astype(jnp.bfloat16)


def row_stats(rows, aux):
    experts, count, part = rows.shape
    squares = jnp.zeros((count, part), jnp.float32)
    logits = jnp.zeros((count, aux.shape[1]), jnp.float32)
    for e in range(experts):
        ratio = rows[e].astype(jnp.float32) / aux[e, 0:1].astype(jnp.float32)
        squares = squares + ratio * ratio
        logits = logits + lax.dot_general(
            rows[e], aux[e], (((1,), (1,)), ((), ())), preferred_element_type=jnp.float32
        )
    total = jnp.sum(squares, axis=1, keepdims=True)
    return jnp.where(lax.broadcasted_iota(jnp.int32, logits.shape, 1) == 0, total, logits)


def products(rows_ref, weight_ref):
    total = None
    for e in range(rows_ref.shape[0]):
        term = jnp.dot(rows_ref[e], weight_ref[e, 0], preferred_element_type=jnp.float32)
        total = term if total is None else total + term
    return total


def early_kernel(own_ref, other_ref, aux_ref, gate_ref, up_ref, gate_out, up_out, stats_out):
    for side, rows_ref in enumerate((own_ref, other_ref)):
        gate_out[side] = products(rows_ref, gate_ref)
        up_out[side] = products(rows_ref, up_ref)

    @pl.when(pl.program_id(0) == 0)
    def _():
        for side, rows_ref in enumerate((own_ref, other_ref)):
            stats_out[side] = row_stats(rows_ref[...], aux_ref[...])


def late_kernel(
    width,
    tiles,
    position_ref,
    own0_ref,
    other0_ref,
    own1_ref,
    other1_ref,
    aux_ref,
    gate_ref,
    up_ref,
    gate_acc,
    up_acc,
    stats_ref,
    signs_ref,
    cot_ref,
    hidden_out,
    grad_gate_out,
    grad_up_out,
    scale_scratch,
    weight_scratch,
    d_gate_scratch,
    d_up_scratch,
    turned_scratch,
):
    step = pl.program_id(0)
    core = position_ref[2]
    planes, _, capacity, tile = hidden_out.shape
    count = planes * capacity
    experts = own0_ref.shape[0]
    lanes = stats_ref.shape[2]

    @pl.when(step == 0)
    def _():
        for side, rows_ref in enumerate((own1_ref, other1_ref)):
            stats = stats_ref[side] + row_stats(rows_ref[...], aux_ref[...])
            inverse = lax.rsqrt(stats[:, 0:1] / width + 1e-05)
            signs = signs_ref[:, pl.ds(core ^ side, 1)].reshape(count, lanes)
            filled = signs[:, lanes - 1 :]
            column = lax.broadcasted_iota(jnp.int32, stats.shape, 1)
            router = (column >= 1) & (column <= experts)
            margin = jnp.sum(jnp.where(router, stats * signs, 0.0), axis=1, keepdims=True)
            prob = jax.nn.sigmoid(margin * inverse).astype(jnp.bfloat16).astype(jnp.float32)
            scale_scratch[side] = inverse
            weight_scratch[side] = jnp.where(filled > 0.0, prob, 0.0)

    @pl.when(step < tiles)
    def _():
        start = pl.multiple_of(step * tile, tile)
        for side, rows_ref in enumerate((own1_ref, other1_ref)):
            inverse = scale_scratch[side]
            weight = weight_scratch[side]
            gate_pre = inverse * (gate_acc[side] + products(rows_ref, gate_ref))
            up_pre = inverse * (up_acc[side] + products(rows_ref, up_ref))
            sig_gate = jax.nn.sigmoid(gate_pre)
            act_gate = gate_pre * sig_gate
            hidden = (weight * act_gate * up_pre).astype(jnp.bfloat16)
            hidden_out[:, pl.ds(core ^ side, 1)] = hidden.reshape(planes, 1, capacity, tile)
            cot = cot_ref[:, pl.ds(core ^ side, 1)].reshape(count, tile)
            d_pre = cot.astype(jnp.float32) * (weight * inverse)
            d_gate = d_pre * up_pre * sig_gate * (1.0 + gate_pre * (1.0 - sig_gate))
            rows = pl.ds(side * count, count)
            d_gate_scratch[rows, pl.ds(start, tile)] = d_gate.astype(jnp.bfloat16)
            d_up_scratch[rows, pl.ds(start, tile)] = (d_pre * act_gate).astype(jnp.bfloat16)

    @pl.when(step >= tiles)
    def _():
        e = (step - tiles) // 2
        for c, sides in enumerate(((own0_ref, other0_ref), (own1_ref, other1_ref))):

            @pl.when((step - tiles) % 2 == c)
            def _():
                for side, rows_ref in enumerate(sides):
                    turned_scratch[:, side * count : (side + 1) * count] = rows_ref[e].T

        for t in range(tiles):
            span = slice(t * tile, (t + 1) * tile)
            for scratch, out in ((d_gate_scratch, grad_gate_out), (d_up_scratch, grad_up_out)):
                out[0, 0, :, span] = jnp.dot(
                    turned_scratch[...], scratch[:, span], preferred_element_type=jnp.float32
                ).astype(jnp.bfloat16)


def per_device(
    branch_wo,
    context,
    residual,
    norm_gain,
    router_w,
    gate_w,
    up_w,
    expert_ids,
    slot_ids,
    cot_hidden,
):
    experts = lax.axis_size("expert")
    blocks = lax.axis_size("fsdp")
    planes = blocks // 2
    expert = lax.axis_index("expert")
    block = lax.axis_index("fsdp")
    plane, core = block // 2, block % 2
    tokens, columns = context.shape
    width = columns * experts
    features = width // blocks
    capacity = cot_hidden.shape[1] // blocks
    units = cot_hidden.shape[2]
    part = columns // CHUNKS
    quarter = tokens // experts
    count = planes * capacity
    position = jnp.stack([expert, plane, core]).astype(jnp.int32)
    bits = bits_of(experts)

    extra = jnp.concatenate([norm_gain[None], router_w.T])
    lanes = experts + 2 + (-(experts + 2)) % 16
    extra = jnp.pad(extra, ((0, lanes - extra.shape[0]), (0, 0)))
    to_experts = jnp.concatenate(
        [
            context.reshape(experts, quarter, columns),
            jnp.broadcast_to(extra, (experts, lanes, columns)),
        ],
        axis=1,
    )
    shares = lax.all_to_all(to_experts, "expert", split_axis=0, concat_axis=0, tiled=True)
    aux = shares[:, quarter:]
    per_expert = blocks // experts
    spread = shares[:, :quarter].reshape(experts, quarter, per_expert, features)
    spread = spread.transpose(0, 2, 1, 3).reshape(blocks, quarter, features)
    ids = jnp.concatenate([expert_ids, slot_ids], axis=1).T.astype(jnp.bfloat16)
    id_rows = ids.size // features
    ids = jnp.pad(ids.reshape(id_rows, features), ((0, -id_rows % 16), (0, 0)))
    to_blocks = jnp.concatenate(
        [spread, jnp.broadcast_to(ids, (blocks,) + ids.shape)], axis=1
    )
    from_blocks = lax.all_to_all(to_blocks, "fsdp", split_axis=0, concat_axis=0, tiled=True)
    ids_all = from_blocks[:, quarter : quarter + id_rows].astype(jnp.int32)
    ids_all = ids_all.reshape(blocks, 4, tokens)
    share = from_blocks[:, :quarter]
    context_rows = jnp.zeros((blocks, experts, quarter, features), jnp.bfloat16)
    for k in range(experts):
        piece = exchange(share, "expert", k) if k else share
        context_rows = lax.dynamic_update_slice_in_dim(
            context_rows, piece[:, None], expert ^ k, 1
        )
    context_rows = context_rows.reshape(planes, 2, tokens, features)
    sides = [
        pick(context_rows, side, 1).reshape(planes * tokens, features) for side in (core, 1 - core)
    ]

    signs = pl.pallas_call(
        functools.partial(signs_kernel, experts),
        out_shape=jax.ShapeDtypeStruct((blocks, capacity, lanes), jnp.float32),
        in_specs=[smem(), whole(ids_all.shape)],
        out_specs=whole((blocks, capacity, lanes)),
        grid=(1,),
        compiler_params=params(),
        name="signs",
    )(position, ids_all).reshape(planes, 2, capacity, lanes)

    branch = branch_wo[0]
    half = branch.shape[0] // 2
    own_bits = [(expert >> (bits - 1 - i)) & 1 for i in range(bits)]

    def block_view(c, h):
        rows = branch[h * half : (h + 1) * half].reshape((half,) + (2,) * bits + (columns,))
        return rows[..., c * part : (c + 1) * part]

    held = {(c, h): block_view(c, h) for c in range(CHUNKS) for h in range(2)}
    remaining = {h: list(range(bits)) for h in range(2)}
    for phase in range(bits):
        before = None
        for c in range(CHUNKS):
            sends, axes = [], []
            for h in range(2):
                i = bits - 1 - phase if h == 0 else phase
                axis = 1 + sum(1 for j in remaining[h] if j < i)
                axes.append((i, axis))
                sends.append(pick(held[c, h], 1 - own_bits[i], axis).astype(jnp.bfloat16))
            if before is not None:
                sends, before = lax.optimization_barrier((sends, before))
            got = [
                exchange(sends[h], "expert", 1 << (bits - 1 - axes[h][0])) for h in range(2)
            ]
            before = got
            for h in range(2):
                kept = pick(held[c, h], own_bits[axes[h][0]], axes[h][1])
                held[c, h] = kept.astype(jnp.float32) + got[h].astype(jnp.float32)
        for h in range(2):
            remaining[h].remove(bits - 1 - phase if h == 0 else phase)

    gate_view = gate_w.reshape(experts, CHUNKS, part, units)
    up_view = up_w.reshape(experts, CHUNKS, part, units)
    tile = min(256, units)
    tiles = units // tile
    merged_parts = []
    row_parts = []
    partial = None
    for c in range(CHUNKS):
        span = slice(c * part, (c + 1) * part)
        merged = jnp.concatenate([held[c, 0], held[c, 1]]) / experts
        merged = merged.astype(jnp.bfloat16)
        merged_parts.append(merged)

        def attend(rows):
            out = jnp.dot(rows, merged, preferred_element_type=jnp.float32)
            return out.reshape(planes, tokens, part)

        swapped = exchange(attend(sides[1]).astype(jnp.bfloat16), "fsdp", 1)
        pair = attend(sides[0]) + swapped.astype(jnp.float32)
        hstate = residual[:, span].astype(jnp.float32) + pick(pair, plane, 0)
        for k in range(1, planes):
            arrived = exchange(pick(pair, plane ^ k, 0).astype(jnp.bfloat16), "fsdp", 2 * k)
            hstate = hstate + arrived.astype(jnp.float32)
        scaled = (hstate * norm_gain[span].astype(jnp.float32)).astype(jnp.bfloat16)
        own_tokens = [exchange(scaled, "fsdp", 2 * k) if k else scaled for k in range(planes)]

        slots = pl.pallas_call(
            dispatch_kernel,
            out_shape=jax.ShapeDtypeStruct((experts, planes, capacity, part), jnp.bfloat16),
            in_specs=[smem(), whole(ids_all.shape)] + [whole((tokens, part))] * planes,
            out_specs=whole((experts, planes, capacity, part)),
            grid=(1,),
            compiler_params=params(),
            name="dispatch",
        )(position, ids_all, *own_tokens)
        rows = lax.all_to_all(
            slots.reshape(experts, count, part), "expert", split_axis=0, concat_axis=0, tiled=True
        )
        other = exchange(rows, "fsdp", 1)
        row_parts.append((rows, other))

        if c == 0:
            aux_spec = pl.BlockSpec((experts, lanes, part), lambda n: (0, 0, 0))
            weight_spec = pl.BlockSpec((experts, 1, part, tile), lambda n: (0, 0, 0, n))
            sums = jax.ShapeDtypeStruct((2, count, units), jnp.float32)
            sum_spec = pl.BlockSpec((2, count, tile), lambda n: (0, 0, n))
            partial = pl.pallas_call(
                early_kernel,
                out_shape=(sums, sums, jax.ShapeDtypeStruct((2, count, lanes), jnp.float32)),
                in_specs=[whole(rows.shape)] * 2 + [aux_spec, weight_spec, weight_spec],
                out_specs=(sum_spec, sum_spec, whole((2, count, lanes))),
                grid=(tiles,),
                compiler_params=params(),
                cost_estimate=pl.CostEstimate(
                    flops=8 * count * experts * part * units,
                    bytes_accessed=4 * experts * part * units,
                    transcendentals=0,
                ),
                name="early",
            )(rows, other, aux, gate_view, up_view)

    aux_spec = pl.BlockSpec((experts, lanes, part), lambda i: (0, 0, 1))
    tile_of = lambda i: jnp.minimum(i, tiles - 1)
    weight_spec = pl.BlockSpec((experts, 1, part, tile), lambda i: (0, 1, 0, tile_of(i)))
    sum_spec = pl.BlockSpec((2, count, tile), lambda i: (0, 0, tile_of(i)))
    unit_spec = pl.BlockSpec((planes, 2, capacity, tile), lambda i: (0, 0, 0, tile_of(i)))

    def grad_index(i):
        place = jnp.maximum(i - tiles, 0)
        return (place // 2, place % 2, 0, 0)

    grad_spec = pl.BlockSpec((1, 1, part, units), grad_index)
    grad_shape = jax.ShapeDtypeStruct((experts, CHUNKS, part, units), jnp.bfloat16)
    row_spec = whole(row_parts[0][0].shape)
    hidden, grad_gate, grad_up = pl.pallas_call(
        functools.partial(late_kernel, float(width), tiles),
        out_shape=(
            jax.ShapeDtypeStruct((planes, 2, capacity, units), jnp.bfloat16),
            grad_shape,
            grad_shape,
        ),
        in_specs=[smem()]
        + [row_spec] * 4
        + [aux_spec, weight_spec, weight_spec, sum_spec, sum_spec]
        + [whole((2, count, lanes)), whole(signs.shape), unit_spec],
        out_specs=(unit_spec, grad_spec, grad_spec),
        grid=(tiles + experts * CHUNKS,),
        scratch_shapes=[
            pltpu.VMEM((2, count, 1), jnp.float32),
            pltpu.VMEM((2, count, 1), jnp.float32),
            pltpu.VMEM((2 * count, units), jnp.bfloat16),
            pltpu.VMEM((2 * count, units), jnp.bfloat16),
            pltpu.VMEM((part, 2 * count), jnp.bfloat16),
        ],
        compiler_params=params(),
        name="late",
    )(
        position,
        *row_parts[0],
        *row_parts[1],
        aux,
        gate_view,
        up_view,
        *partial,
        signs,
        cot_hidden.reshape(planes, 2, capacity, units),
    )
    return (
        jnp.concatenate(merged_parts, axis=1),
        hidden.reshape(1, -1, units),
        grad_gate.reshape(1, width, units),
        grad_up.reshape(1, width, units),
    )


def solution(mesh):
    placed = (
        P("expert", "fsdp", None),
        P("fsdp", "expert"),
        P("fsdp", "expert"),
        P("expert"),
        P("expert", None),
        P("expert", None, "fsdp"),
        P("expert", None, "fsdp"),
        P("fsdp", None),
        P("fsdp", None),
        P("expert", None, "fsdp"),
    )
    return jax.shard_map(
        per_device,
        mesh=mesh,
        in_specs=placed,
        out_specs=(
            P("fsdp", "expert"),
            P("expert", None, "fsdp"),
            P("expert", None, "fsdp"),
            P("expert", None, "fsdp"),
        ),
        check_vma=False,
    )
```

```python
import functools

import jax
import jax.numpy as jnp
from jax import lax
from jax.experimental import pallas as pl
from jax.experimental.pallas import tpu as pltpu
from jax.sharding import PartitionSpec as P

CHUNKS = 2
VMEM_LIMIT = 50 * 1024 * 1024


def exchange(value, axis, offset):
    size = lax.axis_size(axis)
    return lax.ppermute(value, axis, [(i, i ^ offset) for i in range(size)])


def pick(value, index, axis):
    return lax.dynamic_index_in_dim(value, index, axis, keepdims=False)


def bits_of(size):
    return size.bit_length() - 1


def whole(shape):
    return pl.BlockSpec(shape, lambda *_: (0,) * len(shape))


def smem():
    return pl.BlockSpec(memory_space=pltpu.SMEM)


def params():
    return pltpu.CompilerParams(vmem_limit_bytes=VMEM_LIMIT)


def signs_kernel(experts, position_ref, ids_ref, out_ref):
    blocks, capacity, lanes = out_ref.shape
    tokens = ids_ref.shape[2]
    expert = position_ref[0]
    slots = lax.broadcasted_iota(jnp.int32, (capacity, tokens), 0)
    rows = lax.broadcasted_iota(jnp.int32, (lanes, tokens), 0)
    last = lax.broadcasted_iota(jnp.int32, (capacity, lanes), 1) == lanes - 1
    for b in range(blocks):
        ids = ids_ref[b]
        e0, e1, s0, s1 = ids[0:1], ids[1:2], ids[2:3], ids[3:4]
        hit0 = jnp.where((e0 == expert) & (s0 == slots), 1.0, 0.0)
        hit1 = jnp.where((e1 == expert) & (s1 == slots), 1.0, 0.0)
        table = jnp.where(e0 == rows - 1, 1.0, 0.0) - jnp.where(e1 == rows - 1, 1.0, 0.0)
        signs = lax.dot_general(
            (hit0 - hit1).astype(jnp.bfloat16),
            table.astype(jnp.bfloat16),
            (((1,), (1,)), ((), ())),
            preferred_element_type=jnp.float32,
        )
        filled = jnp.sum(hit0 + hit1, axis=1, keepdims=True)
        out_ref[b] = jnp.where(last, filled, signs)


def pack_kernel(position_ref, low_ref, high_ref, low_out, high_out):
    low_out[0] = low_ref[...]
    high_out[0] = high_ref[...]


def pack(position, branch, c, experts):
    half = branch.shape[0] // 2
    part = branch.shape[1] // experts // CHUNKS
    others = experts // 2

    def low(j, position_ref):
        return (0, (2 * j + 1 - position_ref[0] % 2) * CHUNKS + c)

    def high(j, position_ref):
        return (1, (j + others * (1 - position_ref[0] // others)) * CHUNKS + c)

    block = pl.BlockSpec((1, half, part), lambda j, position_ref: (j, 0, 0))
    shape = jax.ShapeDtypeStruct((others, half, part), jnp.bfloat16)
    return pl.pallas_call(
        pack_kernel,
        out_shape=(shape, shape),
        grid_spec=pltpu.PrefetchScalarGridSpec(
            num_scalar_prefetch=1,
            grid=(others,),
            in_specs=[pl.BlockSpec((half, part), low), pl.BlockSpec((half, part), high)],
            out_specs=(block, block),
        ),
        compiler_params=params(),
        name="pack",
    )(position, branch, branch)


def spread_kernel(shares_ref, ids_ref, out_ref):
    experts, quarter, columns = shares_ref.shape
    blocks, _, features = out_ref.shape
    per_expert = blocks // experts
    for f in range(blocks):
        start = (f % per_expert) * features
        out_ref[f, :quarter] = shares_ref[f // per_expert, :, start : start + features]
        out_ref[f, quarter:] = ids_ref[...]


def sides_kernel(position_ref, *refs):
    *share_refs, own_ref, other_ref = refs
    quarter = own_ref.shape[2]
    for k, share_ref in enumerate(share_refs):
        place = position_ref[0] ^ k
        for side, out_ref in enumerate((own_ref, other_ref)):
            out_ref[:, place] = share_ref[:, position_ref[2] ^ side, :quarter]


def dispatch_kernel(position_ref, ids_ref, extra_ref, *refs):
    *token_refs, out_ref = refs
    planes = len(token_refs)
    experts, _, part = out_ref.shape
    lanes = extra_ref.shape[0]
    count = out_ref.shape[1] - lanes
    capacity = count // planes
    tokens = ids_ref.shape[2]
    plane, core = position_ref[1], position_ref[2]
    slots = lax.broadcasted_iota(jnp.int32, (experts * capacity, tokens), 0)
    for k in range(planes):
        source = plane ^ k
        ids = ids_ref[source * 2 + core]
        code0 = ids[0:1] * capacity + ids[2:3]
        code1 = ids[1:2] * capacity + ids[3:4]
        one_hot = jnp.where((code0 == slots) | (code1 == slots), 1.0, 0.0).astype(jnp.bfloat16)
        picked = jnp.dot(one_hot, token_refs[k][...], preferred_element_type=jnp.float32)
        rows = pl.ds(pl.multiple_of(source * capacity, 16), capacity)
        out_ref[:, rows] = picked.reshape(experts, capacity, part).astype(jnp.bfloat16)
    for e in range(experts):
        out_ref[e, count:] = extra_ref[...]


def row_stats(rows_ref, aux_ref, count):
    experts, height, part = rows_ref.shape
    squares = jnp.zeros((count, part), jnp.float32)
    logits = jnp.zeros((count, height - count), jnp.float32)
    for e in range(experts):
        rows, aux = rows_ref[e, :count], aux_ref[e, count:]
        ratio = rows.astype(jnp.float32) * (1.0 / aux[0:1].astype(jnp.float32))
        squares = squares + ratio * ratio
        logits = logits + lax.dot_general(
            rows, aux, (((1,), (1,)), ((), ())), preferred_element_type=jnp.float32
        )
    total = jnp.sum(squares, axis=1, keepdims=True)
    return jnp.where(lax.broadcasted_iota(jnp.int32, logits.shape, 1) == 0, total, logits)


def lay_flat(sides, flat_ref):
    count = flat_ref.shape[0] // 2
    part = sides[0].shape[2]
    for side, rows_ref in enumerate(sides):
        for e in range(rows_ref.shape[0]):
            flat_ref[side * count : (side + 1) * count, e * part : (e + 1) * part] = rows_ref[
                e, :count
            ]


def turn(sides, e, out_ref, at):
    count = out_ref.shape[2] // 2
    for side, rows_ref in enumerate(sides):
        out_ref[at, :, side * count : (side + 1) * count] = rows_ref[e, :count].T


def product(flat_ref, weight_ref):
    weight = weight_ref[...].reshape(flat_ref.shape[1], weight_ref.shape[3])
    return jnp.dot(flat_ref[...], weight, preferred_element_type=jnp.float32)


def early_kernel(
    own_ref, other_ref, gate_ref, up_ref, gate_out, up_out, stats_out, turned_out, flat_scratch
):
    count = flat_scratch.shape[0] // 2
    sides = (own_ref, other_ref)

    @pl.when(pl.program_id(0) == 0)
    def _():
        lay_flat(sides, flat_scratch)
        for side, rows_ref in enumerate(sides):
            stats_out[side * count : (side + 1) * count] = row_stats(rows_ref, own_ref, count)

    gate_out[...] = product(flat_scratch, gate_ref)
    up_out[...] = product(flat_scratch, up_ref)
    per_step = turned_out.shape[0]
    first = jnp.minimum(pl.program_id(0) * per_step, own_ref.shape[0] - per_step)
    for j in range(per_step):
        turn(sides, first + j, turned_out, j)


def late_kernel(
    width,
    tiles,
    position_ref,
    own_ref,
    other_ref,
    turned_ref,
    gate_ref,
    up_ref,
    gate_acc,
    up_acc,
    stats_ref,
    signs_ref,
    cot_ref,
    hidden_out,
    grad_gate_out,
    grad_up_out,
    flat_scratch,
    scale_scratch,
    weight_scratch,
    d_gate_scratch,
    d_up_scratch,
    turned_scratch,
):
    step = pl.program_id(0)
    core = position_ref[2]
    planes, _, capacity, tile = hidden_out.shape
    count = planes * capacity
    experts = own_ref.shape[0]
    lanes = stats_ref.shape[1]
    sides = (own_ref, other_ref)
    per_step = max(1, experts // tiles)

    @pl.when(step == 0)
    def _():
        lay_flat(sides, flat_scratch)
        for side, rows_ref in enumerate(sides):
            span = slice(side * count, (side + 1) * count)
            stats = stats_ref[span] + row_stats(rows_ref, own_ref, count)
            inverse = lax.rsqrt(stats[:, 0:1] / width + 1e-05)
            signs = signs_ref[:, pl.ds(core ^ side, 1)].reshape(count, lanes)
            filled = signs[:, lanes - 1 :]
            column = lax.broadcasted_iota(jnp.int32, stats.shape, 1)
            router = (column >= 1) & (column <= experts)
            margin = jnp.sum(jnp.where(router, stats * signs, 0.0), axis=1, keepdims=True)
            prob = jax.nn.sigmoid(margin * inverse).astype(jnp.bfloat16).astype(jnp.float32)
            scale_scratch[span] = inverse
            weight_scratch[span] = jnp.where(filled > 0.0, prob, 0.0)

    @pl.when(step < tiles)
    def _():
        start = pl.multiple_of(step * tile, tile)
        gate_all = gate_acc[...] + product(flat_scratch, gate_ref)
        up_all = up_acc[...] + product(flat_scratch, up_ref)
        first = jnp.minimum(step * per_step, experts - per_step)
        for j in range(per_step):
            turn(sides, first + j, turned_scratch, first + j)
        for side in range(2):
            span = slice(side * count, (side + 1) * count)
            inverse = scale_scratch[span]
            weight = weight_scratch[span]
            gate_pre = inverse * gate_all[span]
            up_pre = inverse * up_all[span]
            sig_gate = jax.nn.sigmoid(gate_pre)
            act_gate = gate_pre * sig_gate
            hidden = (weight * act_gate * up_pre).astype(jnp.bfloat16)
            hidden_out[:, pl.ds(core ^ side, 1)] = hidden.reshape(planes, 1, capacity, tile)
            cot = cot_ref[:, pl.ds(core ^ side, 1)].reshape(count, tile)
            d_pre = cot.astype(jnp.float32) * (weight * inverse)
            d_gate = d_pre * up_pre * sig_gate * (1.0 + gate_pre * (1.0 - sig_gate))
            d_gate_scratch[span, pl.ds(start, tile)] = d_gate.astype(jnp.bfloat16)
            d_up_scratch[span, pl.ds(start, tile)] = (d_pre * act_gate).astype(jnp.bfloat16)

    def gradients(turned):
        for t in range(tiles):
            span = slice(t * tile, (t + 1) * tile)
            for scratch, out in ((d_gate_scratch, grad_gate_out), (d_up_scratch, grad_up_out)):
                out[0, 0, :, span] = jnp.dot(
                    turned, scratch[:, span], preferred_element_type=jnp.float32
                ).astype(jnp.bfloat16)

    @pl.when((step >= tiles) & ((step - tiles) % 2 == 0))
    def _():
        gradients(turned_ref[0])

    @pl.when((step >= tiles) & ((step - tiles) % 2 == 1))
    def _():
        gradients(turned_scratch[(step - tiles) // 2])


def per_device(
    branch_wo,
    context,
    residual,
    norm_gain,
    router_w,
    gate_w,
    up_w,
    expert_ids,
    slot_ids,
    cot_hidden,
):
    experts = lax.axis_size("expert")
    blocks = lax.axis_size("fsdp")
    planes = blocks // 2
    expert = lax.axis_index("expert")
    block = lax.axis_index("fsdp")
    plane, core = block // 2, block % 2
    tokens, columns = context.shape
    width = columns * experts
    features = width // blocks
    capacity = cot_hidden.shape[1] // blocks
    units = cot_hidden.shape[2]
    part = columns // CHUNKS
    quarter = tokens // experts
    count = planes * capacity
    position = jnp.stack([expert, plane, core]).astype(jnp.int32)
    bits = bits_of(experts)

    lanes = experts + 2 + (-(experts + 2)) % 16
    extra = jnp.concatenate([norm_gain[None], router_w.T])
    extra = jnp.pad(extra, ((0, lanes - extra.shape[0]), (0, 0)))
    ids = jnp.concatenate([expert_ids, slot_ids], axis=1).T.astype(jnp.bfloat16)
    id_rows = ids.size // features
    ids = jnp.pad(ids.reshape(id_rows, features), ((0, -id_rows % 16), (0, 0)))

    shares = lax.all_to_all(
        context.reshape(experts, quarter, columns), "expert", split_axis=0, concat_axis=0, tiled=True
    )
    spread_shape = (blocks, quarter + ids.shape[0], features)
    to_blocks = pl.pallas_call(
        spread_kernel,
        out_shape=jax.ShapeDtypeStruct(spread_shape, jnp.bfloat16),
        in_specs=[whole(shares.shape), whole(ids.shape)],
        out_specs=whole(spread_shape),
        grid=(1,),
        compiler_params=params(),
        name="spread",
    )(shares, ids)
    from_blocks = lax.all_to_all(to_blocks, "fsdp", split_axis=0, concat_axis=0, tiled=True)
    ids_all = from_blocks[:, quarter : quarter + id_rows].astype(jnp.int32)
    ids_all = ids_all.reshape(blocks, 4, tokens)
    pieces = [
        (exchange(from_blocks, "expert", k) if k else from_blocks).reshape(
            planes, 2, spread_shape[1], features
        )
        for k in range(experts)
    ]
    side_shape = (planes, experts, quarter, features)
    sides = pl.pallas_call(
        sides_kernel,
        out_shape=(jax.ShapeDtypeStruct(side_shape, jnp.bfloat16),) * 2,
        in_specs=[smem()] + [whole(piece.shape) for piece in pieces],
        out_specs=(whole(side_shape),) * 2,
        grid=(1,),
        compiler_params=params(),
        name="sides",
    )(position, *pieces)
    sides = [side.reshape(planes * tokens, features) for side in sides]

    signs = pl.pallas_call(
        functools.partial(signs_kernel, experts),
        out_shape=jax.ShapeDtypeStruct((blocks, capacity, lanes), jnp.float32),
        in_specs=[smem(), whole(ids_all.shape)],
        out_specs=whole((blocks, capacity, lanes)),
        grid=(1,),
        compiler_params=params(),
        name="signs",
    )(position, ids_all).reshape(planes, 2, capacity, lanes)

    branch = branch_wo[0]
    half = branch.shape[0] // 2
    weights = [1 << (bits - 1 - i) for i in range(bits)]
    own_bits = [(expert // weight) % 2 for weight in weights]

    def start_sum(c, h):
        def value(chosen):
            place = sum(weight * bit for weight, bit in zip(weights, chosen))
            corner = (h * half, (place * CHUNKS + c) * part)
            return lax.dynamic_slice(branch, corner, (half, part)).astype(jnp.float32)

        return value

    def joined(value, got, axis, rest):
        def total(chosen):
            chosen = [own_bits[axis] if i == axis else bit for i, bit in enumerate(chosen)]
            place = 0
            for i in rest:
                place = 2 * place + chosen[i]
            return value(chosen) + pick(got, place, 0).astype(jnp.float32)

        return total

    held = {(c, h): start_sum(c, h) for c in range(CHUNKS) for h in range(2)}
    orders = (list(range(bits))[::-1], list(range(bits)))
    for phase in range(bits):
        before = None
        for c in range(CHUNKS):
            if phase == 0:
                sends = list(pack(position, branch, c, experts))
            else:
                sends = []
                for h, order in enumerate(orders):
                    rest = sorted(order[phase + 1 :])
                    stacked = []
                    for code in range(1 << len(rest)):
                        chosen = [own_bits[i] for i in range(bits)]
                        chosen[order[phase]] = 1 - own_bits[order[phase]]
                        for at, i in enumerate(rest):
                            chosen[i] = (code >> (len(rest) - 1 - at)) & 1
                        stacked.append(held[c, h](chosen).astype(jnp.bfloat16))
                    sends.append(stacked[0][None] if len(stacked) == 1 else jnp.stack(stacked))
            if before is not None:
                sends, before = lax.optimization_barrier((sends, before))
            got = [
                exchange(sends[h], "expert", weights[order[phase]])
                for h, order in enumerate(orders)
            ]
            before = got
            for h, order in enumerate(orders):
                held[c, h] = joined(held[c, h], got[h], order[phase], sorted(order[phase + 1 :]))
    held = {key: value(own_bits) for key, value in held.items()}

    gate_view = gate_w.reshape(experts, CHUNKS, part, units)
    up_view = up_w.reshape(experts, CHUNKS, part, units)
    tile = min(256, units)
    tiles = units // tile
    merged_parts = []
    partial = None
    for c in range(CHUNKS):
        span = slice(c * part, (c + 1) * part)
        merged = jnp.concatenate([held[c, 0], held[c, 1]]) / experts
        merged = merged.astype(jnp.bfloat16)
        merged_parts.append(merged)

        def attend(rows):
            out = jnp.dot(rows, merged, preferred_element_type=jnp.float32)
            return out.reshape(planes, tokens, part)

        swapped = exchange(attend(sides[1]).astype(jnp.bfloat16), "fsdp", 1)
        pair = attend(sides[0]) + swapped.astype(jnp.float32)
        hstate = residual[:, span].astype(jnp.float32) + pick(pair, plane, 0)
        for k in range(1, planes):
            arrived = exchange(pick(pair, plane ^ k, 0).astype(jnp.bfloat16), "fsdp", 2 * k)
            hstate = hstate + arrived.astype(jnp.float32)
        scaled = (hstate * norm_gain[span].astype(jnp.float32)).astype(jnp.bfloat16)
        own_tokens = [exchange(scaled, "fsdp", 2 * k) if k else scaled for k in range(planes)]

        height = count + lanes
        slots = pl.pallas_call(
            dispatch_kernel,
            out_shape=jax.ShapeDtypeStruct((experts, height, part), jnp.bfloat16),
            in_specs=[smem(), whole(ids_all.shape)]
            + [pl.BlockSpec((lanes, part), lambda i, c=c: (0, c))]
            + [whole((tokens, part))] * planes,
            out_specs=whole((experts, height, part)),
            grid=(1,),
            compiler_params=params(),
            name="dispatch",
        )(position, ids_all, extra, *own_tokens)
        rows = lax.all_to_all(slots, "expert", split_axis=0, concat_axis=0, tiled=True)
        if partial is not None:
            rows, partial = lax.optimization_barrier((rows, partial))
        other = exchange(rows, "fsdp", 1)

        if c == 0:
            weight_spec = pl.BlockSpec((experts, 1, part, tile), lambda n: (0, 0, 0, n))
            sums = jax.ShapeDtypeStruct((2 * count, units), jnp.float32)
            sum_spec = pl.BlockSpec((2 * count, tile), lambda n: (0, n))
            per_step = max(1, experts // tiles)
            partial = pl.pallas_call(
                early_kernel,
                out_shape=(
                    sums,
                    sums,
                    jax.ShapeDtypeStruct((2 * count, lanes), jnp.float32),
                    jax.ShapeDtypeStruct((experts, part, 2 * count), jnp.bfloat16),
                ),
                in_specs=[whole(rows.shape)] * 2 + [weight_spec, weight_spec],
                out_specs=(
                    sum_spec,
                    sum_spec,
                    whole((2 * count, lanes)),
                    pl.BlockSpec(
                        (per_step, part, 2 * count),
                        lambda n: (jnp.minimum(n, experts // per_step - 1), 0, 0),
                    ),
                ),
                grid=(tiles,),
                scratch_shapes=[pltpu.VMEM((2 * count, experts * part), jnp.bfloat16)],
                compiler_params=params(),
                cost_estimate=pl.CostEstimate(
                    flops=8 * count * experts * part * units,
                    bytes_accessed=4 * experts * part * units,
                    transcendentals=0,
                ),
                name="early",
            )(rows, other, gate_view, up_view)

    tile_of = lambda i: jnp.minimum(i, tiles - 1)
    place_of = lambda i: jnp.maximum(i - tiles, 0)
    weight_spec = pl.BlockSpec((experts, 1, part, tile), lambda i: (0, 1, 0, tile_of(i)))
    sum_spec = pl.BlockSpec((2 * count, tile), lambda i: (0, tile_of(i)))
    unit_spec = pl.BlockSpec((planes, 2, capacity, tile), lambda i: (0, 0, 0, tile_of(i)))
    grad_spec = pl.BlockSpec((1, 1, part, units), lambda i: (place_of(i) // 2, place_of(i) % 2, 0, 0))
    grad_shape = jax.ShapeDtypeStruct((experts, CHUNKS, part, units), jnp.bfloat16)
    gate_sums, up_sums, stats, turned = partial
    hidden, grad_gate, grad_up = pl.pallas_call(
        functools.partial(late_kernel, float(width), tiles),
        out_shape=(
            jax.ShapeDtypeStruct((planes, 2, capacity, units), jnp.bfloat16),
            grad_shape,
            grad_shape,
        ),
        in_specs=[smem(), whole(rows.shape), whole(rows.shape)]
        + [pl.BlockSpec((1, part, 2 * count), lambda i: (place_of(i) // 2, 0, 0))]
        + [weight_spec, weight_spec, sum_spec, sum_spec]
        + [whole(stats.shape), whole(signs.shape), unit_spec],
        out_specs=(unit_spec, grad_spec, grad_spec),
        grid=(tiles + experts * CHUNKS,),
        scratch_shapes=[
            pltpu.VMEM((2 * count, experts * part), jnp.bfloat16),
            pltpu.VMEM((2 * count, 1), jnp.float32),
            pltpu.VMEM((2 * count, 1), jnp.float32),
            pltpu.VMEM((2 * count, units), jnp.bfloat16),
            pltpu.VMEM((2 * count, units), jnp.bfloat16),
            pltpu.VMEM((experts, part, 2 * count), jnp.bfloat16),
        ],
        compiler_params=params(),
        name="late",
    )(
        position,
        rows,
        other,
        turned,
        gate_view,
        up_view,
        gate_sums,
        up_sums,
        stats,
        signs,
        cot_hidden.reshape(planes, 2, capacity, units),
    )
    return (
        jnp.concatenate(merged_parts, axis=1),
        hidden.reshape(1, -1, units),
        grad_gate.reshape(1, width, units),
        grad_up.reshape(1, width, units),
    )


def solution(mesh):
    placed = (
        P("expert", "fsdp", None),
        P("fsdp", "expert"),
        P("fsdp", "expert"),
        P("expert"),
        P("expert", None),
        P("expert", None, "fsdp"),
        P("expert", None, "fsdp"),
        P("fsdp", None),
        P("fsdp", None),
        P("expert", None, "fsdp"),
    )
    return jax.shard_map(
        per_device,
        mesh=mesh,
        in_specs=placed,
        out_specs=(
            P("fsdp", "expert"),
            P("expert", None, "fsdp"),
            P("expert", None, "fsdp"),
            P("expert", None, "fsdp"),
        ),
        check_vma=False,
    )
```

```python
import functools

import jax
import jax.numpy as jnp
from jax import lax
from jax.experimental import pallas as pl
from jax.experimental.pallas import tpu as pltpu
from jax.sharding import PartitionSpec as P

CHUNKS = 2
VMEM_LIMIT = 50 * 1024 * 1024


def exchange(value, axis, offset):
    size = lax.axis_size(axis)
    return lax.ppermute(value, axis, [(i, i ^ offset) for i in range(size)])


def pick(value, index, axis):
    return lax.dynamic_index_in_dim(value, index, axis, keepdims=False)


def after(value, *others):
    return lax.optimization_barrier((value, others))[0]


def bits_of(size):
    return size.bit_length() - 1


def whole(shape):
    return pl.BlockSpec(shape, lambda *_: (0,) * len(shape))


def smem():
    return pl.BlockSpec(memory_space=pltpu.SMEM)


def params():
    return pltpu.CompilerParams(vmem_limit_bytes=VMEM_LIMIT)


def signs_kernel(experts, position_ref, ids_ref, out_ref):
    blocks, capacity, lanes = out_ref.shape
    tokens = ids_ref.shape[2]
    expert = position_ref[0]
    slots = lax.broadcasted_iota(jnp.int32, (capacity, tokens), 0)
    rows = lax.broadcasted_iota(jnp.int32, (lanes, tokens), 0)
    last = lax.broadcasted_iota(jnp.int32, (capacity, lanes), 1) == lanes - 1
    for b in range(blocks):
        ids = ids_ref[b]
        e0, e1, s0, s1 = ids[0:1], ids[1:2], ids[2:3], ids[3:4]
        hit0 = jnp.where((e0 == expert) & (s0 == slots), 1.0, 0.0)
        hit1 = jnp.where((e1 == expert) & (s1 == slots), 1.0, 0.0)
        table = jnp.where(e0 == rows - 1, 1.0, 0.0) - jnp.where(e1 == rows - 1, 1.0, 0.0)
        signs = lax.dot_general(
            (hit0 - hit1).astype(jnp.bfloat16),
            table.astype(jnp.bfloat16),
            (((1,), (1,)), ((), ())),
            preferred_element_type=jnp.float32,
        )
        filled = jnp.sum(hit0 + hit1, axis=1, keepdims=True)
        out_ref[b] = jnp.where(last, filled, signs)


def pack_kernel(position_ref, low_ref, high_ref, low_out, high_out):
    low_out[0] = low_ref[...]
    high_out[0] = high_ref[...]


def pack(position, branch, c, experts):
    half = branch.shape[0] // 2
    part = branch.shape[1] // experts // CHUNKS
    others = experts // 2

    def low(j, position_ref):
        return (0, (2 * j + 1 - position_ref[0] % 2) * CHUNKS + c)

    def high(j, position_ref):
        return (1, (j + others * (1 - position_ref[0] // others)) * CHUNKS + c)

    block = pl.BlockSpec((1, half, part), lambda j, position_ref: (j, 0, 0))
    shape = jax.ShapeDtypeStruct((others, half, part), jnp.bfloat16)
    return pl.pallas_call(
        pack_kernel,
        out_shape=(shape, shape),
        grid_spec=pltpu.PrefetchScalarGridSpec(
            num_scalar_prefetch=1,
            grid=(others,),
            in_specs=[pl.BlockSpec((half, part), low), pl.BlockSpec((half, part), high)],
            out_specs=(block, block),
        ),
        compiler_params=params(),
        name="pack",
    )(position, branch, branch)


def join_kernel(*refs):
    *part_refs, out_ref = refs
    part = part_refs[0].shape[1]
    for c, part_ref in enumerate(part_refs):
        out_ref[:, c * part : (c + 1) * part] = part_ref[...]


def spread_kernel(shares_ref, ids_ref, out_ref):
    experts, quarter, columns = shares_ref.shape
    blocks, _, features = out_ref.shape
    per_expert = blocks // experts
    for f in range(blocks):
        start = (f % per_expert) * features
        out_ref[f, :quarter] = shares_ref[f // per_expert, :, start : start + features]
        out_ref[f, quarter:] = ids_ref[...]


def sides_kernel(position_ref, *refs):
    *share_refs, own_ref, other_ref = refs
    for k, share_ref in enumerate(share_refs):
        place = position_ref[0] ^ k
        for side, out_ref in enumerate((own_ref, other_ref)):
            out_ref[:, place] = share_ref[:, position_ref[2] ^ side]


def dispatch_kernel(position_ref, ids_ref, extra_ref, *refs):
    *token_refs, out_ref = refs
    planes = len(token_refs)
    experts, _, part = out_ref.shape
    lanes = extra_ref.shape[0]
    count = out_ref.shape[1] - lanes
    capacity = count // planes
    tokens = ids_ref.shape[2]
    plane, core = position_ref[1], position_ref[2]
    slots = lax.broadcasted_iota(jnp.int32, (experts * capacity, tokens), 0)
    for k in range(planes):
        source = plane ^ k
        ids = ids_ref[source * 2 + core]
        code0 = ids[0:1] * capacity + ids[2:3]
        code1 = ids[1:2] * capacity + ids[3:4]
        one_hot = jnp.where((code0 == slots) | (code1 == slots), 1.0, 0.0).astype(jnp.bfloat16)
        picked = jnp.dot(one_hot, token_refs[k][...], preferred_element_type=jnp.float32)
        rows = pl.ds(pl.multiple_of(source * capacity, 16), capacity)
        out_ref[:, rows] = picked.reshape(experts, capacity, part).astype(jnp.bfloat16)
    for e in range(experts):
        out_ref[e, count:] = extra_ref[...]


def row_stats(rows_ref, aux_ref, count):
    experts, height, part = rows_ref.shape
    squares = jnp.zeros((count, part), jnp.float32)
    logits = jnp.zeros((count, height - count), jnp.float32)
    for e in range(experts):
        rows, aux = rows_ref[e, :count], aux_ref[e, count:]
        ratio = rows.astype(jnp.float32) * (1.0 / aux[0:1].astype(jnp.float32))
        squares = squares + ratio * ratio
        logits = logits + lax.dot_general(
            rows, aux, (((1,), (1,)), ((), ())), preferred_element_type=jnp.float32
        )
    total = jnp.sum(squares, axis=1, keepdims=True)
    return jnp.where(lax.broadcasted_iota(jnp.int32, logits.shape, 1) == 0, total, logits)


def lay_flat(sides, flat_ref):
    count = flat_ref.shape[0] // 2
    part = sides[0].shape[2]
    for side, rows_ref in enumerate(sides):
        for e in range(rows_ref.shape[0]):
            flat_ref[side * count : (side + 1) * count, e * part : (e + 1) * part] = rows_ref[
                e, :count
            ]


def turn(sides, e, out_ref, at):
    count = out_ref.shape[2] // 2
    for side, rows_ref in enumerate(sides):
        out_ref[at, :, side * count : (side + 1) * count] = rows_ref[e, :count].T


def product(flat_ref, weight_ref):
    weight = weight_ref[...].reshape(flat_ref.shape[1], weight_ref.shape[3])
    return jnp.dot(flat_ref[...], weight, preferred_element_type=jnp.float32)


def early_kernel(
    own_ref, other_ref, gate_ref, up_ref, gate_out, up_out, stats_out, turned_out, flat_scratch
):
    count = flat_scratch.shape[0] // 2
    sides = (own_ref, other_ref)

    @pl.when(pl.program_id(0) == 0)
    def _():
        lay_flat(sides, flat_scratch)
        for side, rows_ref in enumerate(sides):
            stats_out[side * count : (side + 1) * count] = row_stats(rows_ref, own_ref, count)

    gate_out[...] = product(flat_scratch, gate_ref)
    up_out[...] = product(flat_scratch, up_ref)
    per_step = turned_out.shape[0]
    first = jnp.minimum(pl.program_id(0) * per_step, own_ref.shape[0] - per_step)
    for j in range(per_step):
        turn(sides, first + j, turned_out, j)


def late_kernel(
    width,
    tiles,
    position_ref,
    own_ref,
    other_ref,
    turned_ref,
    gate_ref,
    up_ref,
    gate_acc,
    up_acc,
    stats_ref,
    signs_ref,
    cot_ref,
    hidden_out,
    grad_gate_out,
    grad_up_out,
    flat_scratch,
    scale_scratch,
    weight_scratch,
    d_gate_scratch,
    d_up_scratch,
    turned_scratch,
):
    step = pl.program_id(0)
    core = position_ref[2]
    planes, _, capacity, tile = hidden_out.shape
    count = planes * capacity
    experts = own_ref.shape[0]
    lanes = stats_ref.shape[1]
    sides = (own_ref, other_ref)
    per_step = max(1, experts // tiles)

    @pl.when(step == 0)
    def _():
        lay_flat(sides, flat_scratch)
        for side, rows_ref in enumerate(sides):
            span = slice(side * count, (side + 1) * count)
            stats = stats_ref[span] + row_stats(rows_ref, own_ref, count)
            inverse = lax.rsqrt(stats[:, 0:1] / width + 1e-05)
            signs = signs_ref[:, pl.ds(core ^ side, 1)].reshape(count, lanes)
            filled = signs[:, lanes - 1 :]
            column = lax.broadcasted_iota(jnp.int32, stats.shape, 1)
            router = (column >= 1) & (column <= experts)
            margin = jnp.sum(jnp.where(router, stats * signs, 0.0), axis=1, keepdims=True)
            prob = jax.nn.sigmoid(margin * inverse).astype(jnp.bfloat16).astype(jnp.float32)
            scale_scratch[span] = inverse
            weight_scratch[span] = jnp.where(filled > 0.0, prob, 0.0)

    @pl.when(step < tiles)
    def _():
        start = pl.multiple_of(step * tile, tile)
        gate_all = gate_acc[...] + product(flat_scratch, gate_ref)
        up_all = up_acc[...] + product(flat_scratch, up_ref)
        first = jnp.minimum(step * per_step, experts - per_step)
        for j in range(per_step):
            turn(sides, first + j, turned_scratch, first + j)
        for side in range(2):
            span = slice(side * count, (side + 1) * count)
            inverse = scale_scratch[span]
            weight = weight_scratch[span]
            gate_pre = inverse * gate_all[span]
            up_pre = inverse * up_all[span]
            sig_gate = jax.nn.sigmoid(gate_pre)
            act_gate = gate_pre * sig_gate
            hidden = (weight * act_gate * up_pre).astype(jnp.bfloat16)
            hidden_out[:, pl.ds(core ^ side, 1)] = hidden.reshape(planes, 1, capacity, tile)
            cot = cot_ref[:, pl.ds(core ^ side, 1)].reshape(count, tile)
            d_pre = cot.astype(jnp.float32) * (weight * inverse)
            d_gate = d_pre * up_pre * sig_gate * (1.0 + gate_pre * (1.0 - sig_gate))
            d_gate_scratch[span, pl.ds(start, tile)] = d_gate.astype(jnp.bfloat16)
            d_up_scratch[span, pl.ds(start, tile)] = (d_pre * act_gate).astype(jnp.bfloat16)

    def gradients(turned):
        for t in range(tiles):
            span = slice(t * tile, (t + 1) * tile)
            for scratch, out in ((d_gate_scratch, grad_gate_out), (d_up_scratch, grad_up_out)):
                out[0, 0, :, span] = jnp.dot(
                    turned, scratch[:, span], preferred_element_type=jnp.float32
                ).astype(jnp.bfloat16)

    @pl.when((step >= tiles) & ((step - tiles) % 2 == 0))
    def _():
        gradients(turned_ref[0])

    @pl.when((step >= tiles) & ((step - tiles) % 2 == 1))
    def _():
        gradients(turned_scratch[(step - tiles) // 2])


def per_device(
    branch_wo,
    context,
    residual,
    norm_gain,
    router_w,
    gate_w,
    up_w,
    expert_ids,
    slot_ids,
    cot_hidden,
):
    experts = lax.axis_size("expert")
    blocks = lax.axis_size("fsdp")
    planes = blocks // 2
    expert = lax.axis_index("expert")
    block = lax.axis_index("fsdp")
    plane, core = block // 2, block % 2
    tokens, columns = context.shape
    width = columns * experts
    features = width // blocks
    capacity = cot_hidden.shape[1] // blocks
    units = cot_hidden.shape[2]
    part = columns // CHUNKS
    quarter = tokens // experts
    count = planes * capacity
    position = jnp.stack([expert, plane, core]).astype(jnp.int32)
    bits = bits_of(experts)

    lanes = experts + 2 + (-(experts + 2)) % 16
    extra = jnp.concatenate([norm_gain[None], router_w.T])
    extra = jnp.pad(extra, ((0, lanes - extra.shape[0]), (0, 0)))
    ids = jnp.concatenate([expert_ids, slot_ids], axis=1).T.astype(jnp.bfloat16)
    id_rows = ids.size // features
    ids = jnp.pad(ids.reshape(id_rows, features), ((0, -id_rows % 16), (0, 0)))

    shares = lax.all_to_all(
        context.reshape(experts, quarter, columns), "expert", split_axis=0, concat_axis=0, tiled=True
    )
    spread_shape = (blocks, quarter + ids.shape[0], features)
    to_blocks = pl.pallas_call(
        spread_kernel,
        out_shape=jax.ShapeDtypeStruct(spread_shape, jnp.bfloat16),
        in_specs=[whole(shares.shape), whole(ids.shape)],
        out_specs=whole(spread_shape),
        grid=(1,),
        compiler_params=params(),
        name="spread",
    )(shares, ids)
    from_blocks = lax.all_to_all(to_blocks, "fsdp", split_axis=0, concat_axis=0, tiled=True)
    ids_all = from_blocks[:, quarter : quarter + id_rows].astype(jnp.int32)
    ids_all = ids_all.reshape(blocks, 4, tokens)
    own_share = from_blocks[:, :quarter]
    pieces = [
        (exchange(own_share, "expert", k) if k else own_share).reshape(
            planes, 2, quarter, features
        )
        for k in range(experts)
    ]
    side_shape = (planes, experts, quarter, features)
    sides = pl.pallas_call(
        sides_kernel,
        out_shape=(jax.ShapeDtypeStruct(side_shape, jnp.bfloat16),) * 2,
        in_specs=[smem()] + [whole(piece.shape) for piece in pieces],
        out_specs=(whole(side_shape),) * 2,
        grid=(1,),
        compiler_params=params(),
        name="sides",
    )(position, *pieces)
    sides = [side.reshape(planes * tokens, features) for side in sides]

    signs = pl.pallas_call(
        functools.partial(signs_kernel, experts),
        out_shape=jax.ShapeDtypeStruct((blocks, capacity, lanes), jnp.float32),
        in_specs=[smem(), whole(ids_all.shape)],
        out_specs=whole((blocks, capacity, lanes)),
        grid=(1,),
        compiler_params=params(),
        name="signs",
    )(position, ids_all).reshape(planes, 2, capacity, lanes)

    branch = branch_wo[0]
    half = branch.shape[0] // 2
    weights = [1 << (bits - 1 - i) for i in range(bits)]
    own_bits = [(expert // weight) % 2 for weight in weights]

    def start_sum(c, h):
        def value(chosen):
            place = sum(weight * bit for weight, bit in zip(weights, chosen))
            corner = (h * half, (place * CHUNKS + c) * part)
            return lax.dynamic_slice(branch, corner, (half, part)).astype(jnp.float32)

        return value

    def joined(value, got, axis, rest):
        def total(chosen):
            chosen = [own_bits[axis] if i == axis else bit for i, bit in enumerate(chosen)]
            place = 0
            for i in rest:
                place = 2 * place + chosen[i]
            return value(chosen) + pick(got, place, 0).astype(jnp.float32)

        return total

    held = {(c, h): start_sum(c, h) for c in range(CHUNKS) for h in range(2)}
    orders = (list(range(bits))[::-1], list(range(bits)))
    for phase in range(bits):
        for c in range(CHUNKS):
            if phase == 0:
                sends = list(pack(position, branch, c, experts))
            else:
                sends = []
                for h, order in enumerate(orders):
                    rest = sorted(order[phase + 1 :])
                    stacked = []
                    for code in range(1 << len(rest)):
                        chosen = [own_bits[i] for i in range(bits)]
                        chosen[order[phase]] = 1 - own_bits[order[phase]]
                        for at, i in enumerate(rest):
                            chosen[i] = (code >> (len(rest) - 1 - at)) & 1
                        stacked.append(held[c, h](chosen).astype(jnp.bfloat16))
                    sends.append(stacked[0][None] if len(stacked) == 1 else jnp.stack(stacked))
            if phase == 0 and c > 0:
                sends = after(sends, from_blocks)
            got = [
                exchange(sends[h], "expert", weights[order[phase]])
                for h, order in enumerate(orders)
            ]
            if phase == 0 and c == 0:
                got = after(got, to_blocks)
            for h, order in enumerate(orders):
                held[c, h] = joined(held[c, h], got[h], order[phase], sorted(order[phase + 1 :]))
    held = {key: value(own_bits) for key, value in held.items()}

    gate_view = gate_w.reshape(experts, CHUNKS, part, units)
    up_view = up_w.reshape(experts, CHUNKS, part, units)
    tile = min(512, units)
    tiles = units // tile
    merged_parts = []
    for c in range(CHUNKS):
        merged = jnp.concatenate([held[c, 0], held[c, 1]]) / experts
        merged_parts.append(merged.astype(jnp.bfloat16))
    merged_out = pl.pallas_call(
        join_kernel,
        out_shape=jax.ShapeDtypeStruct((features, columns), jnp.bfloat16),
        in_specs=[whole((features, part))] * CHUNKS,
        out_specs=whole((features, columns)),
        grid=(1,),
        compiler_params=params(),
        name="join",
    )(*merged_parts)

    def attend(rows, c):
        out = jnp.dot(rows, merged_parts[c], preferred_element_type=jnp.float32)
        return out.reshape(planes, tokens, part)

    pairs = []
    for c in range(CHUNKS):
        swapped = exchange(attend(sides[1], c).astype(jnp.bfloat16), "fsdp", 1)
        pairs.append(attend(sides[0], c) + swapped.astype(jnp.float32))
    height = count + lanes
    slots = []
    scaled = None
    for c in range(CHUNKS):
        span = slice(c * part, (c + 1) * part)
        pair = pairs[c] if scaled is None else after(pairs[c], scaled)
        hstate = residual[:, span].astype(jnp.float32) + pick(pair, plane, 0)
        for k in range(1, planes):
            arrived = exchange(pick(pair, plane ^ k, 0).astype(jnp.bfloat16), "fsdp", 2 * k)
            hstate = hstate + arrived.astype(jnp.float32)
        scaled = (hstate * norm_gain[span].astype(jnp.float32)).astype(jnp.bfloat16)
        if slots:
            scaled = after(scaled, slots[-1])
        own_tokens = [exchange(scaled, "fsdp", 2 * k) if k else scaled for k in range(planes)]
        slots.append(
            pl.pallas_call(
                dispatch_kernel,
                out_shape=jax.ShapeDtypeStruct((experts, height, part), jnp.bfloat16),
                in_specs=[smem(), whole(ids_all.shape)]
                + [pl.BlockSpec((lanes, part), lambda i, c=c: (0, c))]
                + [whole((tokens, part))] * planes,
                out_specs=whole((experts, height, part)),
                grid=(1,),
                compiler_params=params(),
                name="dispatch",
            )(position, ids_all, extra, *own_tokens)
        )

    def to_experts(c):
        return lax.all_to_all(slots[c], "expert", split_axis=0, concat_axis=0, tiled=True)

    rows = after(to_experts(0), slots[-1], merged_out, signs)
    other = exchange(rows, "fsdp", 1)
    weight_spec = pl.BlockSpec((experts, 1, part, tile), lambda n: (0, 0, 0, n))
    sums = jax.ShapeDtypeStruct((2 * count, units), jnp.float32)
    sum_spec = pl.BlockSpec((2 * count, tile), lambda n: (0, n))
    per_step = max(1, experts // tiles)
    partial = pl.pallas_call(
        early_kernel,
        out_shape=(
            sums,
            sums,
            jax.ShapeDtypeStruct((2 * count, lanes), jnp.float32),
            jax.ShapeDtypeStruct((experts, part, 2 * count), jnp.bfloat16),
        ),
        in_specs=[whole(rows.shape)] * 2 + [weight_spec, weight_spec],
        out_specs=(
            sum_spec,
            sum_spec,
            whole((2 * count, lanes)),
            pl.BlockSpec(
                (per_step, part, 2 * count),
                lambda n: (jnp.minimum(n, experts // per_step - 1), 0, 0),
            ),
        ),
        grid=(tiles,),
        scratch_shapes=[pltpu.VMEM((2 * count, experts * part), jnp.bfloat16)],
        compiler_params=params(),
        cost_estimate=pl.CostEstimate(
            flops=8 * count * experts * part * units,
            bytes_accessed=4 * experts * part * units,
            transcendentals=0,
        ),
        name="early",
    )(rows, other, gate_view, up_view)
    rows = after(to_experts(1), partial)
    other = exchange(rows, "fsdp", 1)

    tile_of = lambda i: jnp.minimum(i, tiles - 1)
    place_of = lambda i: jnp.maximum(i - tiles, 0)
    weight_spec = pl.BlockSpec((experts, 1, part, tile), lambda i: (0, 1, 0, tile_of(i)))
    sum_spec = pl.BlockSpec((2 * count, tile), lambda i: (0, tile_of(i)))
    unit_spec = pl.BlockSpec((planes, 2, capacity, tile), lambda i: (0, 0, 0, tile_of(i)))
    grad_spec = pl.BlockSpec((1, 1, part, units), lambda i: (place_of(i) // 2, place_of(i) % 2, 0, 0))
    grad_shape = jax.ShapeDtypeStruct((experts, CHUNKS, part, units), jnp.bfloat16)
    gate_sums, up_sums, stats, turned = partial
    hidden, grad_gate, grad_up = pl.pallas_call(
        functools.partial(late_kernel, float(width), tiles),
        out_shape=(
            jax.ShapeDtypeStruct((planes, 2, capacity, units), jnp.bfloat16),
            grad_shape,
            grad_shape,
        ),
        in_specs=[smem(), whole(rows.shape), whole(rows.shape)]
        + [pl.BlockSpec((1, part, 2 * count), lambda i: (place_of(i) // 2, 0, 0))]
        + [weight_spec, weight_spec, sum_spec, sum_spec]
        + [whole(stats.shape), whole(signs.shape), unit_spec],
        out_specs=(unit_spec, grad_spec, grad_spec),
        grid=(tiles + experts * CHUNKS,),
        scratch_shapes=[
            pltpu.VMEM((2 * count, experts * part), jnp.bfloat16),
            pltpu.VMEM((2 * count, 1), jnp.float32),
            pltpu.VMEM((2 * count, 1), jnp.float32),
            pltpu.VMEM((2 * count, units), jnp.bfloat16),
            pltpu.VMEM((2 * count, units), jnp.bfloat16),
            pltpu.VMEM((experts, part, 2 * count), jnp.bfloat16),
        ],
        compiler_params=params(),
        name="late",
    )(
        position,
        rows,
        other,
        turned,
        gate_view,
        up_view,
        gate_sums,
        up_sums,
        stats,
        signs,
        cot_hidden.reshape(planes, 2, capacity, units),
    )
    return (
        merged_out,
        hidden.reshape(1, -1, units),
        grad_gate.reshape(1, width, units),
        grad_up.reshape(1, width, units),
    )


def solution(mesh):
    placed = (
        P("expert", "fsdp", None),
        P("fsdp", "expert"),
        P("fsdp", "expert"),
        P("expert"),
        P("expert", None),
        P("expert", None, "fsdp"),
        P("expert", None, "fsdp"),
        P("fsdp", None),
        P("fsdp", None),
        P("expert", None, "fsdp"),
    )
    return jax.shard_map(
        per_device,
        mesh=mesh,
        in_specs=placed,
        out_specs=(
            P("fsdp", "expert"),
            P("expert", None, "fsdp"),
            P("expert", None, "fsdp"),
            P("expert", None, "fsdp"),
        ),
        check_vma=False,
    )
```

```python
import functools

import jax
import jax.numpy as jnp
from jax import lax
from jax.experimental import pallas as pl
from jax.experimental.pallas import tpu as pltpu
from jax.sharding import PartitionSpec as P

CHUNKS = 2
VMEM_LIMIT = 56 * 1024 * 1024


def exchange(value, axis, offset):
    size = lax.axis_size(axis)
    return lax.ppermute(value, axis, [(i, i ^ offset) for i in range(size)])


def pick(value, index, axis):
    return lax.dynamic_index_in_dim(value, index, axis, keepdims=False)


def after(value, *others):
    return lax.optimization_barrier((value, others))[0]


def bits_of(size):
    return size.bit_length() - 1


def whole(shape):
    return pl.BlockSpec(shape, lambda *_: (0,) * len(shape))


def smem():
    return pl.BlockSpec(memory_space=pltpu.SMEM)


def params():
    return pltpu.CompilerParams(vmem_limit_bytes=VMEM_LIMIT)


def signs_kernel(experts, position_ref, ids_ref, out_ref):
    blocks, capacity, lanes = out_ref.shape
    tokens = ids_ref.shape[2]
    expert = position_ref[0]
    slots = lax.broadcasted_iota(jnp.int32, (capacity, tokens), 0)
    rows = lax.broadcasted_iota(jnp.int32, (lanes, tokens), 0)
    last = lax.broadcasted_iota(jnp.int32, (capacity, lanes), 1) == lanes - 1
    for b in range(blocks):
        ids = ids_ref[b]
        e0, e1, s0, s1 = ids[0:1], ids[1:2], ids[2:3], ids[3:4]
        hit0 = jnp.where((e0 == expert) & (s0 == slots), 1.0, 0.0)
        hit1 = jnp.where((e1 == expert) & (s1 == slots), 1.0, 0.0)
        table = jnp.where(e0 == rows - 1, 1.0, 0.0) - jnp.where(e1 == rows - 1, 1.0, 0.0)
        signs = lax.dot_general(
            (hit0 - hit1).astype(jnp.bfloat16),
            table.astype(jnp.bfloat16),
            (((1,), (1,)), ((), ())),
            preferred_element_type=jnp.float32,
        )
        filled = jnp.sum(hit0 + hit1, axis=1, keepdims=True)
        out_ref[b] = jnp.where(last, filled, signs)


def pack_kernel(position_ref, low_ref, high_ref, low_out, high_out):
    low_out[0] = low_ref[...]
    high_out[0] = high_ref[...]


def pack(position, branch, c, experts):
    half = branch.shape[0] // 2
    part = branch.shape[1] // experts // CHUNKS
    others = experts // 2

    def low(j, position_ref):
        return (0, (2 * j + 1 - position_ref[0] % 2) * CHUNKS + c)

    def high(j, position_ref):
        return (1, (j + others * (1 - position_ref[0] // others)) * CHUNKS + c)

    block = pl.BlockSpec((1, half, part), lambda j, position_ref: (j, 0, 0))
    shape = jax.ShapeDtypeStruct((others, half, part), jnp.bfloat16)
    return pl.pallas_call(
        pack_kernel,
        out_shape=(shape, shape),
        grid_spec=pltpu.PrefetchScalarGridSpec(
            num_scalar_prefetch=1,
            grid=(others,),
            in_specs=[pl.BlockSpec((half, part), low), pl.BlockSpec((half, part), high)],
            out_specs=(block, block),
        ),
        compiler_params=params(),
        name="pack",
    )(position, branch, branch)


def join_kernel(*refs):
    *part_refs, out_ref = refs
    part = part_refs[0].shape[1]
    for c, part_ref in enumerate(part_refs):
        out_ref[:, c * part : (c + 1) * part] = part_ref[...]


def spread_kernel(shares_ref, ids_ref, out_ref):
    experts, quarter, columns = shares_ref.shape
    blocks, _, features = out_ref.shape
    per_expert = blocks // experts
    for f in range(blocks):
        start = (f % per_expert) * features
        out_ref[f, :quarter] = shares_ref[f // per_expert, :, start : start + features]
        out_ref[f, quarter:] = ids_ref[...]


def sides_kernel(position_ref, *refs):
    *share_refs, own_ref, other_ref = refs
    for k, share_ref in enumerate(share_refs):
        place = position_ref[0] ^ k
        for side, out_ref in enumerate((own_ref, other_ref)):
            out_ref[:, place] = share_ref[:, position_ref[2] ^ side]


def dispatch_kernel(position_ref, ids_ref, extra_ref, *refs):
    *token_refs, out_ref = refs
    planes = len(token_refs)
    experts, _, part = out_ref.shape
    lanes = extra_ref.shape[0]
    count = out_ref.shape[1] - lanes
    capacity = count // planes
    tokens = ids_ref.shape[2]
    plane, core = position_ref[1], position_ref[2]
    slots = lax.broadcasted_iota(jnp.int32, (experts * capacity, tokens), 0)
    for k in range(planes):
        source = plane ^ k
        ids = ids_ref[source * 2 + core]
        code0 = ids[0:1] * capacity + ids[2:3]
        code1 = ids[1:2] * capacity + ids[3:4]
        one_hot = jnp.where((code0 == slots) | (code1 == slots), 1.0, 0.0).astype(jnp.bfloat16)
        picked = jnp.dot(one_hot, token_refs[k][...], preferred_element_type=jnp.float32)
        rows = pl.ds(pl.multiple_of(source * capacity, 16), capacity)
        out_ref[:, rows] = picked.reshape(experts, capacity, part).astype(jnp.bfloat16)
    for e in range(experts):
        out_ref[e, count:] = extra_ref[...]


def row_stats(flat_ref, side, aux_ref):
    count = flat_ref.shape[0] // 2
    experts, lanes, part = aux_ref.shape
    squares = jnp.zeros((count, part), jnp.float32)
    logits = jnp.zeros((count, lanes), jnp.float32)
    for e in range(experts):
        rows = flat_ref[side * count : (side + 1) * count, e * part : (e + 1) * part]
        aux = aux_ref[e]
        ratio = rows.astype(jnp.float32) * (1.0 / aux[0:1].astype(jnp.float32))
        squares = squares + ratio * ratio
        logits = logits + lax.dot_general(
            rows, aux, (((1,), (1,)), ((), ())), preferred_element_type=jnp.float32
        )
    total = jnp.sum(squares, axis=1, keepdims=True)
    return jnp.where(lax.broadcasted_iota(jnp.int32, logits.shape, 1) == 0, total, logits)


def row_copies(sides, flat_ref, aux_ref, sems):
    count = flat_ref.shape[0] // 2
    experts, _, part = aux_ref.shape
    copies = [
        pltpu.make_async_copy(sides[0].at[:, pl.ds(count, aux_ref.shape[1])], aux_ref, sems.at[0])
    ]
    for side, rows_ref in enumerate(sides):
        for e in range(experts):
            copies.append(
                pltpu.make_async_copy(
                    rows_ref.at[e, pl.ds(0, count)],
                    flat_ref.at[pl.ds(side * count, count), pl.ds(e * part, part)],
                    sems.at[1 + side * experts + e],
                )
            )
    return copies


def turned(flat_ref, e, part):
    return flat_ref[:, e * part : (e + 1) * part].T


def product(flat_ref, weight_ref):
    weight = weight_ref[...].reshape(flat_ref.shape[1], weight_ref.shape[3])
    return jnp.dot(flat_ref[...], weight, preferred_element_type=jnp.float32)


def shares_of(experts, tiles, t):
    return range(t * experts // tiles, (t + 1) * experts // tiles)


def early_kernel(
    tiles,
    own_ref,
    other_ref,
    gate_ref,
    up_ref,
    gate_out,
    up_out,
    stats_out,
    turned_out,
    flat_scratch,
    aux_scratch,
    sems,
):
    count = flat_scratch.shape[0] // 2
    experts, _, part = aux_scratch.shape

    for t in range(tiles):

        @pl.when(pl.program_id(0) == t)
        def _():
            if t == 0:
                copies = row_copies((own_ref, other_ref), flat_scratch, aux_scratch, sems)
                for copy in copies:
                    copy.start()
                for copy in copies:
                    copy.wait()
            gate_out[...] = product(flat_scratch, gate_ref)
            up_out[...] = product(flat_scratch, up_ref)
            for e in shares_of(experts, tiles, t):
                turned_out[e] = turned(flat_scratch, e, part)
            if t == tiles - 1:
                for side in range(2):
                    stats_out[side * count : (side + 1) * count] = row_stats(
                        flat_scratch, side, aux_scratch
                    )


def late_kernel(
    width,
    tiles,
    position_ref,
    own_ref,
    other_ref,
    turned_ref,
    gate_ref,
    up_ref,
    gate_acc,
    up_acc,
    stats_ref,
    signs_ref,
    cot_ref,
    hidden_out,
    grad_gate_out,
    grad_up_out,
    flat_scratch,
    aux_scratch,
    scale_scratch,
    weight_scratch,
    gate_scratch,
    up_scratch,
    d_gate_scratch,
    d_up_scratch,
    turned_scratch,
    sems,
):
    step = pl.program_id(0)
    core = position_ref[2]
    planes, _, capacity, tile = hidden_out.shape
    count = planes * capacity
    experts, _, part = aux_scratch.shape
    lanes = stats_ref.shape[1]
    turn_copy = pltpu.make_async_copy(
        turned_ref, turned_scratch.at[0], sems.at[1 + 2 * experts]
    )

    def scales():
        for side in range(2):
            span = slice(side * count, (side + 1) * count)
            stats = stats_ref[span] + row_stats(flat_scratch, side, aux_scratch)
            inverse = lax.rsqrt(stats[:, 0:1] / width + 1e-05)
            signs = signs_ref[:, pl.ds(core ^ side, 1)].reshape(count, lanes)
            filled = signs[:, lanes - 1 :]
            column = lax.broadcasted_iota(jnp.int32, stats.shape, 1)
            router = (column >= 1) & (column <= experts)
            margin = jnp.sum(jnp.where(router, stats * signs, 0.0), axis=1, keepdims=True)
            prob = jax.nn.sigmoid(margin * inverse).astype(jnp.bfloat16).astype(jnp.float32)
            scale_scratch[span] = inverse
            weight_scratch[span] = jnp.where(filled > 0.0, prob, 0.0)

    def units_of(t):
        for side in range(2):
            span = slice(side * count, (side + 1) * count)
            inverse = scale_scratch[span]
            weight = weight_scratch[span]
            gate_pre = inverse * gate_scratch[t % 2, span]
            up_pre = inverse * up_scratch[t % 2, span]
            sig_gate = jax.nn.sigmoid(gate_pre)
            act_gate = gate_pre * sig_gate
            hidden = (weight * act_gate * up_pre).astype(jnp.bfloat16)
            hidden_out[:, pl.ds(core ^ side, 1)] = hidden.reshape(planes, 1, capacity, tile)
            cot = cot_ref[:, pl.ds(core ^ side, 1)].reshape(count, tile)
            d_pre = cot.astype(jnp.float32) * (weight * inverse)
            d_gate = d_pre * up_pre * sig_gate * (1.0 + gate_pre * (1.0 - sig_gate))
            columns = slice(t * tile, (t + 1) * tile)
            d_gate_scratch[span, columns] = d_gate.astype(jnp.bfloat16)
            d_up_scratch[span, columns] = (d_pre * act_gate).astype(jnp.bfloat16)

    def gradients(stretch):
        e = (step - tiles) % experts
        stretch_units = grad_gate_out.shape[2]
        span = slice(stretch * stretch_units, (stretch + 1) * stretch_units)
        for c in range(CHUNKS):
            for scratch, out in ((d_gate_scratch, grad_gate_out), (d_up_scratch, grad_up_out)):
                out[0, c * part : (c + 1) * part] = jnp.dot(
                    turned_scratch[c, e], scratch[:, span], preferred_element_type=jnp.float32
                ).astype(jnp.bfloat16)

    for t in range(tiles):

        @pl.when(step == t)
        def _():
            if t == 0:
                copies = row_copies((own_ref, other_ref), flat_scratch, aux_scratch, sems)
                for copy in copies:
                    copy.start()
                turn_copy.start()
                for copy in copies:
                    copy.wait()
            gate_scratch[t % 2] = gate_acc[...] + product(flat_scratch, gate_ref)
            up_scratch[t % 2] = up_acc[...] + product(flat_scratch, up_ref)
            for e in shares_of(experts, tiles, t):
                turned_scratch[1, e] = turned(flat_scratch, e, part)
            if t == 0:
                scales()
            else:
                units_of(t - 1)

    @pl.when(step == tiles)
    def _():
        turn_copy.wait()
        units_of(tiles - 1)
        gradients(0)

    for stretch in range(tiles * tile // grad_gate_out.shape[2]):
        first = tiles + stretch * experts

        @pl.when((step >= first) & (step < first + experts) & (step > tiles))
        def _():
            gradients(stretch)


def per_device(
    branch_wo,
    context,
    residual,
    norm_gain,
    router_w,
    gate_w,
    up_w,
    expert_ids,
    slot_ids,
    cot_hidden,
):
    experts = lax.axis_size("expert")
    blocks = lax.axis_size("fsdp")
    planes = blocks // 2
    expert = lax.axis_index("expert")
    block = lax.axis_index("fsdp")
    plane, core = block // 2, block % 2
    tokens, columns = context.shape
    width = columns * experts
    features = width // blocks
    capacity = cot_hidden.shape[1] // blocks
    units = cot_hidden.shape[2]
    part = columns // CHUNKS
    quarter = tokens // experts
    count = planes * capacity
    position = jnp.stack([expert, plane, core]).astype(jnp.int32)
    bits = bits_of(experts)

    lanes = experts + 2 + (-(experts + 2)) % 16
    extra = jnp.concatenate([norm_gain[None], router_w.T])
    extra = jnp.pad(extra, ((0, lanes - extra.shape[0]), (0, 0)))
    ids = jnp.concatenate([expert_ids, slot_ids], axis=1).T.astype(jnp.bfloat16)
    id_rows = ids.size // features
    ids = jnp.pad(ids.reshape(id_rows, features), ((0, -id_rows % 16), (0, 0)))

    branch = branch_wo[0]
    half = branch.shape[0] // 2
    weights = [1 << (bits - 1 - i) for i in range(bits)]
    own_bits = [(expert // weight) % 2 for weight in weights]

    def start_sum(c, h):
        def value(chosen):
            place = sum(weight * bit for weight, bit in zip(weights, chosen))
            corner = (h * half, (place * CHUNKS + c) * part)
            return lax.dynamic_slice(branch, corner, (half, part)).astype(jnp.float32)

        return value

    def joined(value, got, axis, rest):
        def total(chosen):
            chosen = [own_bits[axis] if i == axis else bit for i, bit in enumerate(chosen)]
            place = 0
            for i in rest:
                place = 2 * place + chosen[i]
            return value(chosen) + pick(got, place, 0).astype(jnp.float32)

        return total

    held = {(c, h): start_sum(c, h) for c in range(CHUNKS) for h in range(2)}
    orders = (list(range(bits))[::-1], list(range(bits)))

    def branch_sends(phase, c):
        if phase == 0:
            return pack(position, branch, c, experts)
        sends = []
        for h, order in enumerate(orders):
            rest = sorted(order[phase + 1 :])
            stacked = []
            for code in range(1 << len(rest)):
                chosen = list(own_bits)
                chosen[order[phase]] = 1 - own_bits[order[phase]]
                for at, i in enumerate(rest):
                    chosen[i] = (code >> (len(rest) - 1 - at)) & 1
                stacked.append(held[c, h](chosen).astype(jnp.bfloat16))
            sends.append(stacked[0][None] if len(stacked) == 1 else jnp.stack(stacked))
        return tuple(sends)

    def branch_exchange(phase, sends):
        return tuple(
            exchange(sends[h], "expert", weights[order[phase]]) for h, order in enumerate(orders)
        )

    def branch_add(phase, c, got):
        for h, order in enumerate(orders):
            held[c, h] = joined(held[c, h], got[h], order[phase], sorted(order[phase + 1 :]))

    def merged_of(c):
        total = jnp.concatenate([held[c, 0](own_bits), held[c, 1](own_bits)])
        return (total / experts).astype(jnp.bfloat16)

    shares = lax.all_to_all(
        context.reshape(experts, quarter, columns), "expert", split_axis=0, concat_axis=0, tiled=True
    )
    got = branch_exchange(0, branch_sends(0, 0))
    shares, got = lax.optimization_barrier((shares, got))
    branch_add(0, 0, got)

    spread_shape = (blocks, quarter + ids.shape[0], features)
    to_blocks = pl.pallas_call(
        spread_kernel,
        out_shape=jax.ShapeDtypeStruct(spread_shape, jnp.bfloat16),
        in_specs=[whole(shares.shape), whole(ids.shape)],
        out_specs=whole(spread_shape),
        grid=(1,),
        compiler_params=params(),
        name="spread",
    )(shares, ids)
    from_blocks = lax.all_to_all(to_blocks, "fsdp", split_axis=0, concat_axis=0, tiled=True)
    for phase in range(1, bits):
        got = branch_exchange(phase, branch_sends(phase, 0))
        if phase == bits - 1:
            from_blocks, got = lax.optimization_barrier((from_blocks, got))
        branch_add(phase, 0, got)

    ids_all = from_blocks[:, quarter : quarter + id_rows].astype(jnp.int32)
    ids_all = ids_all.reshape(blocks, 4, tokens)
    own_share = from_blocks[:, :quarter]
    pieces = [exchange(own_share, "expert", k) if k else own_share for k in range(experts)]
    side_shape = (planes, experts, quarter, features)
    sides = pl.pallas_call(
        sides_kernel,
        out_shape=(jax.ShapeDtypeStruct(side_shape, jnp.bfloat16),) * 2,
        in_specs=[smem()] + [whole((planes, 2, quarter, features))] * experts,
        out_specs=(whole(side_shape),) * 2,
        grid=(1,),
        compiler_params=params(),
        name="sides",
    )(position, *[piece.reshape(planes, 2, quarter, features) for piece in pieces])
    sides = [side.reshape(planes * tokens, features) for side in sides]
    signs = pl.pallas_call(
        functools.partial(signs_kernel, experts),
        out_shape=jax.ShapeDtypeStruct((blocks, capacity, lanes), jnp.float32),
        in_specs=[smem(), whole(ids_all.shape)],
        out_specs=whole((blocks, capacity, lanes)),
        grid=(1,),
        compiler_params=params(),
        name="signs",
    )(position, ids_all).reshape(planes, 2, capacity, lanes)

    gate_view = gate_w.reshape(experts, CHUNKS, part, units)
    up_view = up_w.reshape(experts, CHUNKS, part, units)
    tile = min(256, units)
    stretch = min(512, units)
    tiles = units // tile
    def pair_of(merged):
        def attend(rows):
            out = jnp.dot(rows, merged, preferred_element_type=jnp.float32)
            return out.reshape(planes, tokens, part)

        swapped = exchange(attend(sides[1]).astype(jnp.bfloat16), "fsdp", 1)
        return attend(sides[0]) + swapped.astype(jnp.float32)

    def plane_sends(pair):
        return [pick(pair, plane ^ k, 0).astype(jnp.bfloat16) for k in range(1, planes)]

    def plane_exchange(sends):
        return [exchange(send, "fsdp", 2 * k) for k, send in enumerate(sends, 1)]

    def scaled_of(c, pair, arrived):
        span = slice(c * part, (c + 1) * part)
        hstate = residual[:, span].astype(jnp.float32) + pick(pair, plane, 0)
        for value in arrived:
            hstate = hstate + value.astype(jnp.float32)
        return (hstate * norm_gain[span].astype(jnp.float32)).astype(jnp.bfloat16)

    height = count + lanes

    def slots_of(c, own_tokens):
        return pl.pallas_call(
            dispatch_kernel,
            out_shape=jax.ShapeDtypeStruct((experts, height, part), jnp.bfloat16),
            in_specs=[smem(), whole(ids_all.shape)]
            + [pl.BlockSpec((lanes, part), lambda i, c=c: (0, c))]
            + [whole((tokens, part))] * planes,
            out_specs=whole((experts, height, part)),
            grid=(1,),
            compiler_params=params(),
            name="dispatch",
        )(position, ids_all, extra, *own_tokens)

    merged0 = merged_of(0)
    got = branch_exchange(0, after(branch_sends(0, 1), pieces))
    pair0 = pair_of(merged0)
    sends0 = plane_sends(pair0)
    branch_add(0, 1, after(got, sends0))
    arrived0 = plane_exchange(sends0)
    for phase in range(1, bits):
        got = branch_exchange(phase, branch_sends(phase, 1))
        if phase < bits - 1:
            branch_add(phase, 1, got)

    scaled0 = scaled_of(0, pair0, arrived0)
    tokens0 = [scaled0] + plane_exchange([scaled0] * (planes - 1))
    if bits > 1:
        branch_add(bits - 1, 1, after(got, scaled0))
    merged1 = merged_of(1)
    merged_out = pl.pallas_call(
        join_kernel,
        out_shape=jax.ShapeDtypeStruct((features, columns), jnp.bfloat16),
        in_specs=[whole((features, part))] * CHUNKS,
        out_specs=whole((features, columns)),
        grid=(1,),
        compiler_params=params(),
        name="join",
    )(merged0, merged1)
    pair1 = pair_of(merged1)
    arrived1 = plane_exchange(plane_sends(pair1))

    slots0 = slots_of(0, tokens0)
    scaled1 = scaled_of(1, pair1, after(arrived1, slots0))
    tokens1 = [scaled1] + plane_exchange([scaled1] * (planes - 1))
    slots1 = slots_of(1, tokens1)
    slots = (slots0, slots1)

    def to_experts(c):
        return lax.all_to_all(slots[c], "expert", split_axis=0, concat_axis=0, tiled=True)

    rows = after(to_experts(0), slots[-1], merged_out, signs)
    other = exchange(rows, "fsdp", 1)
    weight_spec = pl.BlockSpec((experts, 1, part, tile), lambda n: (0, 0, 0, n))
    sums = jax.ShapeDtypeStruct((2 * count, units), jnp.float32)
    sum_spec = pl.BlockSpec((2 * count, tile), lambda n: (0, n))
    any_spec = pl.BlockSpec(memory_space=pl.ANY)
    row_scratch = [
        pltpu.VMEM((2 * count, experts * part), jnp.bfloat16),
        pltpu.VMEM((experts, lanes, part), jnp.bfloat16),
    ]
    partial = pl.pallas_call(
        functools.partial(early_kernel, tiles),
        out_shape=(
            sums,
            sums,
            jax.ShapeDtypeStruct((2 * count, lanes), jnp.float32),
            jax.ShapeDtypeStruct((experts, part, 2 * count), jnp.bfloat16),
        ),
        in_specs=[any_spec, any_spec, weight_spec, weight_spec],
        out_specs=(
            sum_spec,
            sum_spec,
            whole((2 * count, lanes)),
            whole((experts, part, 2 * count)),
        ),
        grid=(tiles,),
        scratch_shapes=row_scratch + [pltpu.SemaphoreType.DMA((1 + 2 * experts,))],
        compiler_params=params(),
        cost_estimate=pl.CostEstimate(
            flops=8 * count * experts * part * units,
            bytes_accessed=4 * experts * part * units,
            transcendentals=0,
        ),
        name="early",
    )(rows, other, gate_view, up_view)
    rows = after(to_experts(1), partial)
    other = exchange(rows, "fsdp", 1)

    tile_of = lambda i: jnp.minimum(i, tiles - 1)
    behind = lambda i: jnp.clip(i - 1, 0, tiles - 1)
    place_of = lambda i: jnp.maximum(i - tiles, 0)
    weight_spec = pl.BlockSpec((experts, 1, part, tile), lambda i: (0, 1, 0, tile_of(i)))
    sum_spec = pl.BlockSpec((2 * count, tile), lambda i: (0, tile_of(i)))
    unit_spec = pl.BlockSpec((planes, 2, capacity, tile), lambda i: (0, 0, 0, behind(i)))
    grad_spec = pl.BlockSpec(
        (1, columns, stretch), lambda i: (place_of(i) % experts, 0, place_of(i) // experts)
    )
    grad_shape = jax.ShapeDtypeStruct((experts, columns, units), jnp.bfloat16)
    gate_sums, up_sums, stats, turned_rows = partial
    hidden, grad_gate, grad_up = pl.pallas_call(
        functools.partial(late_kernel, float(width), tiles),
        out_shape=(
            jax.ShapeDtypeStruct((planes, 2, capacity, units), jnp.bfloat16),
            grad_shape,
            grad_shape,
        ),
        in_specs=[smem(), any_spec, any_spec, any_spec]
        + [weight_spec, weight_spec, sum_spec, sum_spec]
        + [whole(stats.shape), whole(signs.shape), unit_spec],
        out_specs=(unit_spec, grad_spec, grad_spec),
        grid=(tiles + experts * (units // stretch),),
        scratch_shapes=row_scratch
        + [
            pltpu.VMEM((2 * count, 1), jnp.float32),
            pltpu.VMEM((2 * count, 1), jnp.float32),
            pltpu.VMEM((2, 2 * count, tile), jnp.float32),
            pltpu.VMEM((2, 2 * count, tile), jnp.float32),
            pltpu.VMEM((2 * count, units), jnp.bfloat16),
            pltpu.VMEM((2 * count, units), jnp.bfloat16),
            pltpu.VMEM((CHUNKS, experts, part, 2 * count), jnp.bfloat16),
            pltpu.SemaphoreType.DMA((2 + 2 * experts,)),
        ],
        compiler_params=params(),
        name="late",
    )(
        position,
        rows,
        other,
        turned_rows,
        gate_view,
        up_view,
        gate_sums,
        up_sums,
        stats,
        signs,
        cot_hidden.reshape(planes, 2, capacity, units),
    )
    return (
        merged_out,
        hidden.reshape(1, -1, units),
        grad_gate.reshape(1, width, units),
        grad_up.reshape(1, width, units),
    )


def solution(mesh):
    placed = (
        P("expert", "fsdp", None),
        P("fsdp", "expert"),
        P("fsdp", "expert"),
        P("expert"),
        P("expert", None),
        P("expert", None, "fsdp"),
        P("expert", None, "fsdp"),
        P("fsdp", None),
        P("fsdp", None),
        P("expert", None, "fsdp"),
    )
    return jax.shard_map(
        per_device,
        mesh=mesh,
        in_specs=placed,
        out_specs=(
            P("fsdp", "expert"),
            P("expert", None, "fsdp"),
            P("expert", None, "fsdp"),
            P("expert", None, "fsdp"),
        ),
        check_vma=False,
    )
```

```python
import functools

import jax
import jax.numpy as jnp
from jax import lax
from jax.experimental import pallas as pl
from jax.experimental.pallas import tpu as pltpu
from jax.sharding import PartitionSpec as P

CHUNKS = 2
MEBI = 1024 * 1024


def exchange(value, axis, offset):
    size = lax.axis_size(axis)
    return lax.ppermute(value, axis, [(i, i ^ offset) for i in range(size)])


def pick(value, index, axis):
    return lax.dynamic_index_in_dim(value, index, axis, keepdims=False)


def after(value, *others):
    return lax.optimization_barrier((value, others))[0]


def bits_of(size):
    return size.bit_length() - 1


def whole(shape):
    return pl.BlockSpec(shape, lambda *_: (0,) * len(shape))


def smem():
    return pl.BlockSpec(memory_space=pltpu.SMEM)


def params(mebi=16):
    return pltpu.CompilerParams(vmem_limit_bytes=mebi * MEBI)


def signs_kernel(experts, position_ref, ids_ref, out_ref):
    blocks, capacity, lanes = out_ref.shape
    tokens = ids_ref.shape[2]
    expert = position_ref[0]
    slots = lax.broadcasted_iota(jnp.int32, (capacity, tokens), 0)
    rows = lax.broadcasted_iota(jnp.int32, (lanes, tokens), 0)
    last = lax.broadcasted_iota(jnp.int32, (capacity, lanes), 1) == lanes - 1
    for b in range(blocks):
        ids = ids_ref[b]
        e0, e1, s0, s1 = ids[0:1], ids[1:2], ids[2:3], ids[3:4]
        hit0 = jnp.where((e0 == expert) & (s0 == slots), 1.0, 0.0)
        hit1 = jnp.where((e1 == expert) & (s1 == slots), 1.0, 0.0)
        table = jnp.where(e0 == rows - 1, 1.0, 0.0) - jnp.where(e1 == rows - 1, 1.0, 0.0)
        signs = lax.dot_general(
            (hit0 - hit1).astype(jnp.bfloat16),
            table.astype(jnp.bfloat16),
            (((1,), (1,)), ((), ())),
            preferred_element_type=jnp.float32,
        )
        filled = jnp.sum(hit0 + hit1, axis=1, keepdims=True)
        out_ref[b] = jnp.where(last, filled, signs)


def pack_kernel(position_ref, low_ref, high_ref, low_out, high_out):
    low_out[0] = low_ref[...]
    high_out[0] = high_ref[...]


def pack(position, branch, c, experts):
    half = branch.shape[0] // 2
    part = branch.shape[1] // experts // CHUNKS
    others = experts // 2

    def low(j, position_ref):
        return (0, (2 * j + 1 - position_ref[0] % 2) * CHUNKS + c)

    def high(j, position_ref):
        return (1, (j + others * (1 - position_ref[0] // others)) * CHUNKS + c)

    block = pl.BlockSpec((1, half, part), lambda j, position_ref: (j, 0, 0))
    shape = jax.ShapeDtypeStruct((others, half, part), jnp.bfloat16)
    return pl.pallas_call(
        pack_kernel,
        out_shape=(shape, shape),
        grid_spec=pltpu.PrefetchScalarGridSpec(
            num_scalar_prefetch=1,
            grid=(others,),
            in_specs=[pl.BlockSpec((half, part), low), pl.BlockSpec((half, part), high)],
            out_specs=(block, block),
        ),
        compiler_params=params(),
        name="pack",
    )(position, branch, branch)


def join_kernel(*refs):
    *part_refs, out_ref = refs
    part = part_refs[0].shape[1]
    for c, part_ref in enumerate(part_refs):
        out_ref[:, c * part : (c + 1) * part] = part_ref[...]


def spread_kernel(shares_ref, ids_ref, out_ref):
    experts, quarter, columns = shares_ref.shape
    blocks, _, features = out_ref.shape
    per_expert = blocks // experts
    for f in range(blocks):
        start = (f % per_expert) * features
        out_ref[f, :quarter] = shares_ref[f // per_expert, :, start : start + features]
        out_ref[f, quarter:] = ids_ref[...]


def sides_kernel(position_ref, *refs):
    *share_refs, own_ref, other_ref = refs
    for k, share_ref in enumerate(share_refs):
        place = position_ref[0] ^ k
        for side, out_ref in enumerate((own_ref, other_ref)):
            out_ref[:, place] = share_ref[:, position_ref[2] ^ side]


def dispatch_kernel(position_ref, ids_ref, extra_ref, *refs):
    *token_refs, out_ref = refs
    planes = len(token_refs)
    experts, _, part = out_ref.shape
    lanes = extra_ref.shape[0]
    count = out_ref.shape[1] - lanes
    capacity = count // planes
    tokens = ids_ref.shape[2]
    plane, core = position_ref[1], position_ref[2]
    slots = lax.broadcasted_iota(jnp.int32, (experts * capacity, tokens), 0)
    for k in range(planes):
        source = plane ^ k
        ids = ids_ref[source * 2 + core]
        code0 = ids[0:1] * capacity + ids[2:3]
        code1 = ids[1:2] * capacity + ids[3:4]
        one_hot = jnp.where((code0 == slots) | (code1 == slots), 1.0, 0.0).astype(jnp.bfloat16)
        picked = jnp.dot(one_hot, token_refs[k][...], preferred_element_type=jnp.float32)
        rows = pl.ds(pl.multiple_of(source * capacity, 16), capacity)
        out_ref[:, rows] = picked.reshape(experts, capacity, part).astype(jnp.bfloat16)
    for e in range(experts):
        out_ref[e, count:] = extra_ref[...]


def row_stats(flat_ref, side, aux_ref):
    count = flat_ref.shape[0] // 2
    experts, lanes, part = aux_ref.shape
    squares = jnp.zeros((count, part), jnp.float32)
    logits = jnp.zeros((count, lanes), jnp.float32)
    for e in range(experts):
        rows = flat_ref[side * count : (side + 1) * count, e * part : (e + 1) * part]
        aux = aux_ref[e]
        ratio = rows.astype(jnp.float32) * (1.0 / aux[0:1].astype(jnp.float32))
        squares = squares + ratio * ratio
        logits = logits + lax.dot_general(
            rows, aux, (((1,), (1,)), ((), ())), preferred_element_type=jnp.float32
        )
    total = jnp.sum(squares, axis=1, keepdims=True)
    return jnp.where(lax.broadcasted_iota(jnp.int32, logits.shape, 1) == 0, total, logits)


def row_copies(sides, flat_ref, aux_ref, sems):
    count = flat_ref.shape[0] // 2
    experts, _, part = aux_ref.shape
    copies = [
        pltpu.make_async_copy(sides[0].at[:, pl.ds(count, aux_ref.shape[1])], aux_ref, sems.at[0])
    ]
    for side, rows_ref in enumerate(sides):
        for e in range(experts):
            copies.append(
                pltpu.make_async_copy(
                    rows_ref.at[e, pl.ds(0, count)],
                    flat_ref.at[pl.ds(side * count, count), pl.ds(e * part, part)],
                    sems.at[1 + side * experts + e],
                )
            )
    return copies


def turned(flat_ref, e, part):
    return flat_ref[:, e * part : (e + 1) * part].T


def product(flat_ref, weight_ref):
    weight = weight_ref[...].reshape(flat_ref.shape[1], weight_ref.shape[3])
    return jnp.dot(flat_ref[...], weight, preferred_element_type=jnp.float32)


def shares_of(experts, tiles, t):
    return range(t * experts // tiles, (t + 1) * experts // tiles)


def early_kernel(
    tiles,
    own_ref,
    other_ref,
    gate_ref,
    up_ref,
    gate_out,
    up_out,
    stats_out,
    turned_out,
    flat_scratch,
    aux_scratch,
    sems,
):
    count = flat_scratch.shape[0] // 2
    experts, _, part = aux_scratch.shape

    for t in range(tiles):

        @pl.when(pl.program_id(0) == t)
        def _():
            if t == 0:
                copies = row_copies((own_ref, other_ref), flat_scratch, aux_scratch, sems)
                for copy in copies:
                    copy.start()
                for copy in copies:
                    copy.wait()
            gate_out[...] = product(flat_scratch, gate_ref)
            up_out[...] = product(flat_scratch, up_ref)
            for e in shares_of(experts, tiles, t):
                turned_out[e] = turned(flat_scratch, e, part)
            if t == tiles - 1:
                for side in range(2):
                    stats_out[side * count : (side + 1) * count] = row_stats(
                        flat_scratch, side, aux_scratch
                    )


def late_kernel(
    width,
    tiles,
    position_ref,
    own_ref,
    other_ref,
    turned_ref,
    gate_ref,
    up_ref,
    gate_acc,
    up_acc,
    stats_ref,
    signs_ref,
    cot_ref,
    hidden_out,
    grad_gate_out,
    grad_up_out,
    flat_scratch,
    aux_scratch,
    scale_scratch,
    weight_scratch,
    gate_scratch,
    up_scratch,
    d_gate_scratch,
    d_up_scratch,
    turned_scratch,
    sems,
):
    step = pl.program_id(0)
    core = position_ref[2]
    planes, _, capacity, tile = hidden_out.shape
    count = planes * capacity
    experts, _, part = aux_scratch.shape
    lanes = stats_ref.shape[1]
    turn_copy = pltpu.make_async_copy(
        turned_ref, turned_scratch.at[:, pl.ds(0, part)], sems.at[1 + 2 * experts]
    )

    def scales():
        for side in range(2):
            span = slice(side * count, (side + 1) * count)
            stats = stats_ref[span] + row_stats(flat_scratch, side, aux_scratch)
            inverse = lax.rsqrt(stats[:, 0:1] / width + 1e-05)
            signs = signs_ref[:, pl.ds(core ^ side, 1)].reshape(count, lanes)
            filled = signs[:, lanes - 1 :]
            column = lax.broadcasted_iota(jnp.int32, stats.shape, 1)
            router = (column >= 1) & (column <= experts)
            margin = jnp.sum(jnp.where(router, stats * signs, 0.0), axis=1, keepdims=True)
            prob = jax.nn.sigmoid(margin * inverse).astype(jnp.bfloat16).astype(jnp.float32)
            scale_scratch[span] = inverse
            weight_scratch[span] = jnp.where(filled > 0.0, prob, 0.0)

    def units_of(t):
        for side in range(2):
            span = slice(side * count, (side + 1) * count)
            inverse = scale_scratch[span]
            weight = weight_scratch[span]
            gate_pre = inverse * gate_scratch[t % 2, span]
            up_pre = inverse * up_scratch[t % 2, span]
            sig_gate = jax.nn.sigmoid(gate_pre)
            act_gate = gate_pre * sig_gate
            hidden = (weight * act_gate * up_pre).astype(jnp.bfloat16)
            hidden_out[:, pl.ds(core ^ side, 1)] = hidden.reshape(planes, 1, capacity, tile)
            cot = cot_ref[:, pl.ds(core ^ side, 1)].reshape(count, tile)
            d_pre = cot.astype(jnp.float32) * (weight * inverse)
            d_gate = d_pre * up_pre * sig_gate * (1.0 + gate_pre * (1.0 - sig_gate))
            columns = slice(t * tile, (t + 1) * tile)
            d_gate_scratch[span, columns] = d_gate.astype(jnp.bfloat16)
            d_up_scratch[span, columns] = (d_pre * act_gate).astype(jnp.bfloat16)

    def gradients(stretch):
        e = (step - tiles) % experts
        stretch_units = grad_gate_out.shape[2]
        span = slice(stretch * stretch_units, (stretch + 1) * stretch_units)
        for scratch, out in ((d_gate_scratch, grad_gate_out), (d_up_scratch, grad_up_out)):
            out[0] = jnp.dot(
                turned_scratch[e], scratch[:, span], preferred_element_type=jnp.float32
            ).astype(jnp.bfloat16)

    for t in range(tiles):

        @pl.when(step == t)
        def _():
            if t == 0:
                copies = row_copies((own_ref, other_ref), flat_scratch, aux_scratch, sems)
                for copy in copies:
                    copy.start()
                turn_copy.start()
                for copy in copies:
                    copy.wait()
            gate_scratch[t % 2] = gate_acc[...] + product(flat_scratch, gate_ref)
            up_scratch[t % 2] = up_acc[...] + product(flat_scratch, up_ref)
            for e in shares_of(experts, tiles, t):
                turned_scratch[e, part:] = turned(flat_scratch, e, part)
            if t == 0:
                scales()
            else:
                units_of(t - 1)

    @pl.when(step == tiles)
    def _():
        turn_copy.wait()
        units_of(tiles - 1)
        gradients(0)

    for stretch in range(tiles * tile // grad_gate_out.shape[2]):
        first = tiles + stretch * experts

        @pl.when((step >= first) & (step < first + experts) & (step > tiles))
        def _():
            gradients(stretch)


def per_device(
    branch_wo,
    context,
    residual,
    norm_gain,
    router_w,
    gate_w,
    up_w,
    expert_ids,
    slot_ids,
    cot_hidden,
):
    experts = lax.axis_size("expert")
    blocks = lax.axis_size("fsdp")
    planes = blocks // 2
    expert = lax.axis_index("expert")
    block = lax.axis_index("fsdp")
    plane, core = block // 2, block % 2
    tokens, columns = context.shape
    width = columns * experts
    features = width // blocks
    capacity = cot_hidden.shape[1] // blocks
    units = cot_hidden.shape[2]
    part = columns // CHUNKS
    quarter = tokens // experts
    count = planes * capacity
    position = jnp.stack([expert, plane, core]).astype(jnp.int32)
    bits = bits_of(experts)

    lanes = experts + 2 + (-(experts + 2)) % 16
    extra = jnp.concatenate([norm_gain[None], router_w.T])
    extra = jnp.pad(extra, ((0, lanes - extra.shape[0]), (0, 0)))
    ids = jnp.concatenate([expert_ids, slot_ids], axis=1).T.astype(jnp.bfloat16)
    id_rows = ids.size // features
    ids = jnp.pad(ids.reshape(id_rows, features), ((0, -id_rows % 16), (0, 0)))

    branch = branch_wo[0]
    half = branch.shape[0] // 2
    weights = [1 << (bits - 1 - i) for i in range(bits)]
    own_bits = [(expert // weight) % 2 for weight in weights]

    def start_sum(c, h):
        def value(chosen):
            place = sum(weight * bit for weight, bit in zip(weights, chosen))
            corner = (h * half, (place * CHUNKS + c) * part)
            return lax.dynamic_slice(branch, corner, (half, part)).astype(jnp.float32)

        return value

    def joined(value, got, axis, rest):
        def total(chosen):
            chosen = [own_bits[axis] if i == axis else bit for i, bit in enumerate(chosen)]
            place = 0
            for i in rest:
                place = 2 * place + chosen[i]
            return value(chosen) + pick(got, place, 0).astype(jnp.float32)

        return total

    held = {(c, h): start_sum(c, h) for c in range(CHUNKS) for h in range(2)}
    orders = (list(range(bits))[::-1], list(range(bits)))

    def branch_sends(phase, c):
        if phase == 0:
            return pack(position, branch, c, experts)
        sends = []
        for h, order in enumerate(orders):
            rest = sorted(order[phase + 1 :])
            stacked = []
            for code in range(1 << len(rest)):
                chosen = list(own_bits)
                chosen[order[phase]] = 1 - own_bits[order[phase]]
                for at, i in enumerate(rest):
                    chosen[i] = (code >> (len(rest) - 1 - at)) & 1
                stacked.append(held[c, h](chosen).astype(jnp.bfloat16))
            sends.append(stacked[0][None] if len(stacked) == 1 else jnp.stack(stacked))
        return tuple(sends)

    def branch_exchange(phase, sends):
        return tuple(
            exchange(sends[h], "expert", weights[order[phase]]) for h, order in enumerate(orders)
        )

    def branch_add(phase, c, got):
        for h, order in enumerate(orders):
            held[c, h] = joined(held[c, h], got[h], order[phase], sorted(order[phase + 1 :]))

    def merged_of(c):
        total = jnp.concatenate([held[c, 0](own_bits), held[c, 1](own_bits)])
        return (total / experts).astype(jnp.bfloat16)

    shares = lax.all_to_all(
        context.reshape(experts, quarter, columns), "expert", split_axis=0, concat_axis=0, tiled=True
    )

    spread_shape = (blocks, quarter + ids.shape[0], features)
    to_blocks = pl.pallas_call(
        spread_kernel,
        out_shape=jax.ShapeDtypeStruct(spread_shape, jnp.bfloat16),
        in_specs=[whole(shares.shape), whole(ids.shape)],
        out_specs=whole(spread_shape),
        grid=(1,),
        compiler_params=params(),
        name="spread",
    )(shares, ids)
    got = branch_exchange(0, pack(after(position, shares), branch, 0, experts))
    branch_add(0, 0, after(got, to_blocks))
    from_blocks = lax.all_to_all(to_blocks, "fsdp", split_axis=0, concat_axis=0, tiled=True)
    for phase in range(1, bits):
        got = branch_exchange(phase, branch_sends(phase, 0))
        if phase == bits - 1:
            from_blocks, got = lax.optimization_barrier((from_blocks, got))
        branch_add(phase, 0, got)

    ids_all = from_blocks[:, quarter : quarter + id_rows].astype(jnp.int32)
    ids_all = ids_all.reshape(blocks, 4, tokens)
    own_share = from_blocks[:, :quarter]
    packed1 = branch_sends(0, 1)
    pieces = [exchange(own_share, "expert", k) if k else own_share for k in range(experts)]
    pieces, packed1 = lax.optimization_barrier((pieces, packed1))
    side_shape = (planes, experts, quarter, features)
    sides = pl.pallas_call(
        sides_kernel,
        out_shape=(jax.ShapeDtypeStruct(side_shape, jnp.bfloat16),) * 2,
        in_specs=[smem()] + [whole((planes, 2, quarter, features))] * experts,
        out_specs=(whole(side_shape),) * 2,
        grid=(1,),
        compiler_params=params(),
        name="sides",
    )(position, *[piece.reshape(planes, 2, quarter, features) for piece in pieces])
    sides = [side.reshape(planes * tokens, features) for side in sides]
    signs = pl.pallas_call(
        functools.partial(signs_kernel, experts),
        out_shape=jax.ShapeDtypeStruct((blocks, capacity, lanes), jnp.float32),
        in_specs=[smem(), whole(ids_all.shape)],
        out_specs=whole((blocks, capacity, lanes)),
        grid=(1,),
        compiler_params=params(),
        name="signs",
    )(position, ids_all).reshape(planes, 2, capacity, lanes)

    gate_view = gate_w.reshape(experts, CHUNKS, part, units)
    up_view = up_w.reshape(experts, CHUNKS, part, units)
    tile = min(256, units)
    stretch = min(512, units)
    tiles = units // tile
    def pair_of(merged):
        def attend(rows):
            out = jnp.dot(rows, merged, preferred_element_type=jnp.float32)
            return out.reshape(planes, tokens, part)

        swapped = exchange(attend(sides[1]).astype(jnp.bfloat16), "fsdp", 1)
        return attend(sides[0]) + swapped.astype(jnp.float32)

    def plane_sends(pair):
        return [pick(pair, plane ^ k, 0).astype(jnp.bfloat16) for k in range(1, planes)]

    def plane_exchange(sends):
        return [exchange(send, "fsdp", 2 * k) for k, send in enumerate(sends, 1)]

    def scaled_of(c, pair, arrived):
        span = slice(c * part, (c + 1) * part)
        hstate = residual[:, span].astype(jnp.float32) + pick(pair, plane, 0)
        for value in arrived:
            hstate = hstate + value.astype(jnp.float32)
        return (hstate * norm_gain[span].astype(jnp.float32)).astype(jnp.bfloat16)

    height = count + lanes

    def slots_of(c, own_tokens):
        return pl.pallas_call(
            dispatch_kernel,
            out_shape=jax.ShapeDtypeStruct((experts, height, part), jnp.bfloat16),
            in_specs=[smem(), whole(ids_all.shape)]
            + [pl.BlockSpec((lanes, part), lambda i, c=c: (0, c))]
            + [whole((tokens, part))] * planes,
            out_specs=whole((experts, height, part)),
            grid=(1,),
            compiler_params=params(),
            name="dispatch",
        )(position, ids_all, extra, *own_tokens)

    merged0 = merged_of(0)
    got = branch_exchange(0, packed1)
    pair0 = pair_of(merged0)
    sends0 = plane_sends(pair0)
    branch_add(0, 1, after(got, sends0))
    arrived0 = plane_exchange(sends0)
    for phase in range(1, bits):
        got = branch_exchange(phase, branch_sends(phase, 1))
        if phase < bits - 1:
            branch_add(phase, 1, got)

    scaled0 = scaled_of(0, pair0, arrived0)
    tokens0 = [scaled0] + plane_exchange([scaled0] * (planes - 1))
    if bits > 1:
        branch_add(bits - 1, 1, after(got, scaled0))
    merged1 = merged_of(1)
    merged_out = pl.pallas_call(
        join_kernel,
        out_shape=jax.ShapeDtypeStruct((features, columns), jnp.bfloat16),
        in_specs=[whole((features, part))] * CHUNKS,
        out_specs=whole((features, columns)),
        grid=(1,),
        compiler_params=params(),
        name="join",
    )(merged0, merged1)
    pair1 = pair_of(merged1)
    sends1 = plane_sends(pair1)
    arrived1 = plane_exchange(sends1)

    slots0 = slots_of(0, after(tokens0, sends1))
    scaled1 = scaled_of(1, pair1, after(arrived1, slots0))
    tokens1 = [scaled1] + plane_exchange([scaled1] * (planes - 1))
    slots1 = slots_of(1, tokens1)
    slots = (slots0, slots1)

    def to_experts(c):
        return lax.all_to_all(slots[c], "expert", split_axis=0, concat_axis=0, tiled=True)

    rows = after(to_experts(0), slots[-1], merged_out, signs)
    other = exchange(rows, "fsdp", 1)
    weight_spec = pl.BlockSpec((experts, 1, part, tile), lambda n: (0, 0, 0, n))
    sums = jax.ShapeDtypeStruct((2 * count, units), jnp.float32)
    sum_spec = pl.BlockSpec((2 * count, tile), lambda n: (0, n))
    any_spec = pl.BlockSpec(memory_space=pl.ANY)
    row_scratch = [
        pltpu.VMEM((2 * count, experts * part), jnp.bfloat16),
        pltpu.VMEM((experts, lanes, part), jnp.bfloat16),
    ]
    partial = pl.pallas_call(
        functools.partial(early_kernel, tiles),
        out_shape=(
            sums,
            sums,
            jax.ShapeDtypeStruct((2 * count, lanes), jnp.float32),
            jax.ShapeDtypeStruct((experts, part, 2 * count), jnp.bfloat16),
        ),
        in_specs=[any_spec, any_spec, weight_spec, weight_spec],
        out_specs=(
            sum_spec,
            sum_spec,
            whole((2 * count, lanes)),
            whole((experts, part, 2 * count)),
        ),
        grid=(tiles,),
        scratch_shapes=row_scratch + [pltpu.SemaphoreType.DMA((1 + 2 * experts,))],
        compiler_params=params(32),
        cost_estimate=pl.CostEstimate(
            flops=8 * count * experts * part * units,
            bytes_accessed=4 * experts * part * units,
            transcendentals=0,
        ),
        name="early",
    )(rows, other, gate_view, up_view)
    rows = after(to_experts(1), partial)
    other = exchange(rows, "fsdp", 1)

    tile_of = lambda i: jnp.minimum(i, tiles - 1)
    behind = lambda i: jnp.clip(i - 1, 0, tiles - 1)
    place_of = lambda i: jnp.maximum(i - tiles, 0)
    weight_spec = pl.BlockSpec((experts, 1, part, tile), lambda i: (0, 1, 0, tile_of(i)))
    sum_spec = pl.BlockSpec((2 * count, tile), lambda i: (0, tile_of(i)))
    unit_spec = pl.BlockSpec((planes, 2, capacity, tile), lambda i: (0, 0, 0, behind(i)))
    grad_spec = pl.BlockSpec(
        (1, columns, stretch), lambda i: (place_of(i) % experts, 0, place_of(i) // experts)
    )
    grad_shape = jax.ShapeDtypeStruct((experts, columns, units), jnp.bfloat16)
    gate_sums, up_sums, stats, turned_rows = partial
    hidden, grad_gate, grad_up = pl.pallas_call(
        functools.partial(late_kernel, float(width), tiles),
        out_shape=(
            jax.ShapeDtypeStruct((planes, 2, capacity, units), jnp.bfloat16),
            grad_shape,
            grad_shape,
        ),
        in_specs=[smem(), any_spec, any_spec, any_spec]
        + [weight_spec, weight_spec, sum_spec, sum_spec]
        + [whole(stats.shape), whole(signs.shape), unit_spec],
        out_specs=(unit_spec, grad_spec, grad_spec),
        grid=(tiles + experts * (units // stretch),),
        scratch_shapes=row_scratch
        + [
            pltpu.VMEM((2 * count, 1), jnp.float32),
            pltpu.VMEM((2 * count, 1), jnp.float32),
            pltpu.VMEM((2, 2 * count, tile), jnp.float32),
            pltpu.VMEM((2, 2 * count, tile), jnp.float32),
            pltpu.VMEM((2 * count, units), jnp.bfloat16),
            pltpu.VMEM((2 * count, units), jnp.bfloat16),
            pltpu.VMEM((experts, columns, 2 * count), jnp.bfloat16),
            pltpu.SemaphoreType.DMA((2 + 2 * experts,)),
        ],
        compiler_params=params(48),
        name="late",
    )(
        position,
        rows,
        other,
        turned_rows,
        gate_view,
        up_view,
        gate_sums,
        up_sums,
        stats,
        signs,
        cot_hidden.reshape(planes, 2, capacity, units),
    )
    return (
        merged_out,
        hidden.reshape(1, -1, units),
        grad_gate.reshape(1, width, units),
        grad_up.reshape(1, width, units),
    )


def solution(mesh):
    placed = (
        P("expert", "fsdp", None),
        P("fsdp", "expert"),
        P("fsdp", "expert"),
        P("expert"),
        P("expert", None),
        P("expert", None, "fsdp"),
        P("expert", None, "fsdp"),
        P("fsdp", None),
        P("fsdp", None),
        P("expert", None, "fsdp"),
    )
    return jax.shard_map(
        per_device,
        mesh=mesh,
        in_specs=placed,
        out_specs=(
            P("fsdp", "expert"),
            P("expert", None, "fsdp"),
            P("expert", None, "fsdp"),
            P("expert", None, "fsdp"),
        ),
        check_vma=False,
    )
```

```python
import functools

import jax
import jax.numpy as jnp
from jax import lax
from jax.experimental import pallas as pl
from jax.experimental.pallas import tpu as pltpu
from jax.sharding import PartitionSpec as P

CHUNKS = 2
MEBI = 1024 * 1024


def exchange(value, axis, offset):
    size = lax.axis_size(axis)
    return lax.ppermute(value, axis, [(i, i ^ offset) for i in range(size)])


def pick(value, index, axis):
    return lax.dynamic_index_in_dim(value, index, axis, keepdims=False)


def after(value, *others):
    return lax.optimization_barrier((value, others))[0]


def bits_of(size):
    return size.bit_length() - 1


def whole(shape):
    return pl.BlockSpec(shape, lambda *_: (0,) * len(shape))


def smem():
    return pl.BlockSpec(memory_space=pltpu.SMEM)


def params(mebi=16):
    return pltpu.CompilerParams(vmem_limit_bytes=mebi * MEBI)


def signs_kernel(experts, position_ref, ids_ref, out_ref):
    blocks, capacity, lanes = out_ref.shape
    tokens = ids_ref.shape[2]
    expert = position_ref[0]
    slots = lax.broadcasted_iota(jnp.int32, (capacity, tokens), 0)
    rows = lax.broadcasted_iota(jnp.int32, (lanes, tokens), 0)
    last = lax.broadcasted_iota(jnp.int32, (capacity, lanes), 1) == lanes - 1
    for b in range(blocks):
        ids = ids_ref[b]
        e0, e1, s0, s1 = ids[0:1], ids[1:2], ids[2:3], ids[3:4]
        hit0 = jnp.where((e0 == expert) & (s0 == slots), 1.0, 0.0)
        hit1 = jnp.where((e1 == expert) & (s1 == slots), 1.0, 0.0)
        table = jnp.where(e0 == rows - 1, 1.0, 0.0) - jnp.where(e1 == rows - 1, 1.0, 0.0)
        signs = lax.dot_general(
            (hit0 - hit1).astype(jnp.bfloat16),
            table.astype(jnp.bfloat16),
            (((1,), (1,)), ((), ())),
            preferred_element_type=jnp.float32,
        )
        filled = jnp.sum(hit0 + hit1, axis=1, keepdims=True)
        out_ref[b] = jnp.where(last, filled, signs)


def pack_kernel(c, position_ref, branch_ref, low_out, high_out, sems):
    others, half, part = low_out.shape
    expert = position_ref[0]
    copies = []
    for j in range(others):
        low = 2 * j + 1 - expert % 2
        high = j + others * (1 - expert // others)
        for h, (place, out) in enumerate(((low, low_out), (high, high_out))):
            columns = pl.ds(pl.multiple_of((place * CHUNKS + c) * part, 128), part)
            source = branch_ref.at[pl.ds(h * half, half), columns]
            copies.append(pltpu.make_async_copy(source, out.at[j], sems.at[2 * j + h]))
    for copy in copies:
        copy.start()
    for copy in copies:
        copy.wait()


def pack(position, branch, c, experts):
    others = experts // 2
    shape = (others, branch.shape[0] // 2, branch.shape[1] // experts // CHUNKS)
    spec = pl.BlockSpec(memory_space=pltpu.HBM)
    return pl.pallas_call(
        functools.partial(pack_kernel, c),
        out_shape=(jax.ShapeDtypeStruct(shape, jnp.bfloat16),) * 2,
        in_specs=[smem(), spec],
        out_specs=(spec, spec),
        scratch_shapes=[pltpu.SemaphoreType.DMA((2 * others,))],
        compiler_params=params(),
        name="pack",
    )(position, branch)


def join_kernel(*refs):
    *part_refs, out_ref = refs
    part = part_refs[0].shape[1]
    for c, part_ref in enumerate(part_refs):
        out_ref[:, c * part : (c + 1) * part] = part_ref[...]


def spread_kernel(shares_ref, ids_ref, out_ref):
    experts, quarter, columns = shares_ref.shape
    blocks, _, features = out_ref.shape
    per_expert = blocks // experts
    for f in range(blocks):
        start = (f % per_expert) * features
        out_ref[f, :quarter] = shares_ref[f // per_expert, :, start : start + features]
        out_ref[f, quarter:] = ids_ref[...]


def sides_kernel(position_ref, *refs):
    *share_refs, own_ref, other_ref = refs
    for k, share_ref in enumerate(share_refs):
        place = position_ref[0] ^ k
        for side, out_ref in enumerate((own_ref, other_ref)):
            out_ref[:, place] = share_ref[:, position_ref[2] ^ side]


def dispatch_kernel(position_ref, ids_ref, extra_ref, *refs):
    *token_refs, out_ref = refs
    planes = len(token_refs)
    experts, _, part = out_ref.shape
    lanes = extra_ref.shape[0]
    count = out_ref.shape[1] - lanes
    capacity = count // planes
    tokens = ids_ref.shape[2]
    plane, core = position_ref[1], position_ref[2]
    slots = lax.broadcasted_iota(jnp.int32, (experts * capacity, tokens), 0)
    for k in range(planes):
        source = plane ^ k
        ids = ids_ref[source * 2 + core]
        code0 = ids[0:1] * capacity + ids[2:3]
        code1 = ids[1:2] * capacity + ids[3:4]
        one_hot = jnp.where((code0 == slots) | (code1 == slots), 1.0, 0.0).astype(jnp.bfloat16)
        picked = jnp.dot(one_hot, token_refs[k][...], preferred_element_type=jnp.float32)
        rows = pl.ds(pl.multiple_of(source * capacity, 16), capacity)
        out_ref[:, rows] = picked.reshape(experts, capacity, part).astype(jnp.bfloat16)
    for e in range(experts):
        out_ref[e, count:] = extra_ref[...]


def row_stats(flat_ref, side, aux_ref):
    count = flat_ref.shape[0] // 2
    experts, lanes, part = aux_ref.shape
    squares = jnp.zeros((count, part), jnp.float32)
    logits = jnp.zeros((count, lanes), jnp.float32)
    for e in range(experts):
        rows = flat_ref[side * count : (side + 1) * count, e * part : (e + 1) * part]
        aux = aux_ref[e]
        ratio = rows.astype(jnp.float32) * (1.0 / aux[0:1].astype(jnp.float32))
        squares = squares + ratio * ratio
        logits = logits + lax.dot_general(
            rows, aux, (((1,), (1,)), ((), ())), preferred_element_type=jnp.float32
        )
    total = jnp.sum(squares, axis=1, keepdims=True)
    return jnp.where(lax.broadcasted_iota(jnp.int32, logits.shape, 1) == 0, total, logits)


def row_copies(sides, flat_ref, aux_ref, sems):
    count = flat_ref.shape[0] // 2
    experts, _, part = aux_ref.shape
    copies = [
        pltpu.make_async_copy(sides[0].at[:, pl.ds(count, aux_ref.shape[1])], aux_ref, sems.at[0])
    ]
    for side, rows_ref in enumerate(sides):
        for e in range(experts):
            copies.append(
                pltpu.make_async_copy(
                    rows_ref.at[e, pl.ds(0, count)],
                    flat_ref.at[pl.ds(side * count, count), pl.ds(e * part, part)],
                    sems.at[1 + side * experts + e],
                )
            )
    return copies


def turned(flat_ref, e, part):
    return flat_ref[:, e * part : (e + 1) * part].T


def product(flat_ref, weight_ref):
    weight = weight_ref[...].reshape(flat_ref.shape[1], weight_ref.shape[3])
    return jnp.dot(flat_ref[...], weight, preferred_element_type=jnp.float32)


def shares_of(experts, tiles, t):
    return range(t * experts // tiles, (t + 1) * experts // tiles)


def early_kernel(
    tiles,
    own_ref,
    other_ref,
    gate_ref,
    up_ref,
    gate_out,
    up_out,
    stats_out,
    turned_out,
    flat_scratch,
    aux_scratch,
    sems,
):
    count = flat_scratch.shape[0] // 2
    experts, _, part = aux_scratch.shape

    for t in range(tiles):

        @pl.when(pl.program_id(0) == t)
        def _():
            if t == 0:
                copies = row_copies((own_ref, other_ref), flat_scratch, aux_scratch, sems)
                for copy in copies:
                    copy.start()
                for copy in copies:
                    copy.wait()
            gate_out[...] = product(flat_scratch, gate_ref)
            up_out[...] = product(flat_scratch, up_ref)
            for e in shares_of(experts, tiles, t):
                turned_out[e] = turned(flat_scratch, e, part)
            if t == tiles - 1:
                for side in range(2):
                    stats_out[side * count : (side + 1) * count] = row_stats(
                        flat_scratch, side, aux_scratch
                    )


def late_kernel(
    width,
    tiles,
    position_ref,
    own_ref,
    other_ref,
    turned_ref,
    gate_ref,
    up_ref,
    gate_acc,
    up_acc,
    stats_ref,
    signs_ref,
    cot_ref,
    hidden_out,
    grad_gate_out,
    grad_up_out,
    flat_scratch,
    aux_scratch,
    scale_scratch,
    weight_scratch,
    gate_scratch,
    up_scratch,
    d_gate_scratch,
    d_up_scratch,
    turned_scratch,
    sems,
):
    step = pl.program_id(0)
    core = position_ref[2]
    planes, _, capacity, tile = hidden_out.shape
    count = planes * capacity
    experts, _, part = aux_scratch.shape
    lanes = stats_ref.shape[1]
    turn_copy = pltpu.make_async_copy(
        turned_ref, turned_scratch.at[:, pl.ds(0, part)], sems.at[1 + 2 * experts]
    )

    def scales():
        for side in range(2):
            span = slice(side * count, (side + 1) * count)
            stats = stats_ref[span] + row_stats(flat_scratch, side, aux_scratch)
            inverse = lax.rsqrt(stats[:, 0:1] / width + 1e-05)
            signs = signs_ref[:, pl.ds(core ^ side, 1)].reshape(count, lanes)
            filled = signs[:, lanes - 1 :]
            column = lax.broadcasted_iota(jnp.int32, stats.shape, 1)
            router = (column >= 1) & (column <= experts)
            margin = jnp.sum(jnp.where(router, stats * signs, 0.0), axis=1, keepdims=True)
            prob = jax.nn.sigmoid(margin * inverse).astype(jnp.bfloat16).astype(jnp.float32)
            scale_scratch[span] = inverse
            weight_scratch[span] = jnp.where(filled > 0.0, prob, 0.0)

    def units_of(t):
        for side in range(2):
            span = slice(side * count, (side + 1) * count)
            inverse = scale_scratch[span]
            weight = weight_scratch[span]
            gate_pre = inverse * gate_scratch[t % 2, span]
            up_pre = inverse * up_scratch[t % 2, span]
            sig_gate = jax.nn.sigmoid(gate_pre)
            act_gate = gate_pre * sig_gate
            hidden = (weight * act_gate * up_pre).astype(jnp.bfloat16)
            hidden_out[:, pl.ds(core ^ side, 1)] = hidden.reshape(planes, 1, capacity, tile)
            cot = cot_ref[:, pl.ds(core ^ side, 1)].reshape(count, tile)
            d_pre = cot.astype(jnp.float32) * (weight * inverse)
            d_gate = d_pre * up_pre * sig_gate * (1.0 + gate_pre * (1.0 - sig_gate))
            columns = slice(t * tile, (t + 1) * tile)
            d_gate_scratch[span, columns] = d_gate.astype(jnp.bfloat16)
            d_up_scratch[span, columns] = (d_pre * act_gate).astype(jnp.bfloat16)

    def gradients(stretch):
        e = (step - tiles) % experts
        stretch_units = grad_gate_out.shape[2]
        span = slice(stretch * stretch_units, (stretch + 1) * stretch_units)
        for scratch, out in ((d_gate_scratch, grad_gate_out), (d_up_scratch, grad_up_out)):
            out[0] = jnp.dot(
                turned_scratch[e], scratch[:, span], preferred_element_type=jnp.float32
            ).astype(jnp.bfloat16)

    for t in range(tiles):

        @pl.when(step == t)
        def _():
            if t == 0:
                copies = row_copies((own_ref, other_ref), flat_scratch, aux_scratch, sems)
                for copy in copies:
                    copy.start()
                turn_copy.start()
                for copy in copies:
                    copy.wait()
            gate_scratch[t % 2] = gate_acc[...] + product(flat_scratch, gate_ref)
            up_scratch[t % 2] = up_acc[...] + product(flat_scratch, up_ref)
            for e in shares_of(experts, tiles, t):
                turned_scratch[e, part:] = turned(flat_scratch, e, part)
            if t == 0:
                scales()
            else:
                units_of(t - 1)

    @pl.when(step == tiles)
    def _():
        turn_copy.wait()
        units_of(tiles - 1)
        gradients(0)

    for stretch in range(tiles * tile // grad_gate_out.shape[2]):
        first = tiles + stretch * experts

        @pl.when((step >= first) & (step < first + experts) & (step > tiles))
        def _():
            gradients(stretch)


def per_device(
    branch_wo,
    context,
    residual,
    norm_gain,
    router_w,
    gate_w,
    up_w,
    expert_ids,
    slot_ids,
    cot_hidden,
):
    experts = lax.axis_size("expert")
    blocks = lax.axis_size("fsdp")
    planes = blocks // 2
    expert = lax.axis_index("expert")
    block = lax.axis_index("fsdp")
    plane, core = block // 2, block % 2
    tokens, columns = context.shape
    width = columns * experts
    features = width // blocks
    capacity = cot_hidden.shape[1] // blocks
    units = cot_hidden.shape[2]
    part = columns // CHUNKS
    quarter = tokens // experts
    count = planes * capacity
    position = jnp.stack([expert, plane, core]).astype(jnp.int32)
    bits = bits_of(experts)

    lanes = experts + 2 + (-(experts + 2)) % 16
    extra = jnp.concatenate([norm_gain[None], router_w.T])
    extra = jnp.pad(extra, ((0, lanes - extra.shape[0]), (0, 0)))
    ids = jnp.concatenate([expert_ids, slot_ids], axis=1).T.astype(jnp.bfloat16)
    id_rows = ids.size // features
    ids = jnp.pad(ids.reshape(id_rows, features), ((0, -id_rows % 16), (0, 0)))

    branch = branch_wo[0]
    half = branch.shape[0] // 2
    weights = [1 << (bits - 1 - i) for i in range(bits)]
    own_bits = [(expert // weight) % 2 for weight in weights]

    def start_sum(c, h):
        def value(chosen):
            place = sum(weight * bit for weight, bit in zip(weights, chosen))
            corner = (h * half, (place * CHUNKS + c) * part)
            return lax.dynamic_slice(branch, corner, (half, part)).astype(jnp.float32)

        return value

    def joined(value, got, axis, rest):
        def total(chosen):
            chosen = [own_bits[axis] if i == axis else bit for i, bit in enumerate(chosen)]
            place = 0
            for i in rest:
                place = 2 * place + chosen[i]
            return value(chosen) + pick(got, place, 0).astype(jnp.float32)

        return total

    held = {(c, h): start_sum(c, h) for c in range(CHUNKS) for h in range(2)}
    orders = (list(range(bits))[::-1], list(range(bits)))

    def branch_sends(phase, c):
        if phase == 0:
            return pack(position, branch, c, experts)
        sends = []
        for h, order in enumerate(orders):
            rest = sorted(order[phase + 1 :])
            stacked = []
            for code in range(1 << len(rest)):
                chosen = list(own_bits)
                chosen[order[phase]] = 1 - own_bits[order[phase]]
                for at, i in enumerate(rest):
                    chosen[i] = (code >> (len(rest) - 1 - at)) & 1
                stacked.append(held[c, h](chosen).astype(jnp.bfloat16))
            sends.append(stacked[0][None] if len(stacked) == 1 else jnp.stack(stacked))
        return tuple(sends)

    def branch_exchange(phase, sends):
        return tuple(
            exchange(sends[h], "expert", weights[order[phase]]) for h, order in enumerate(orders)
        )

    def branch_add(phase, c, got):
        for h, order in enumerate(orders):
            held[c, h] = joined(held[c, h], got[h], order[phase], sorted(order[phase + 1 :]))

    def merged_of(c):
        total = jnp.concatenate([held[c, 0](own_bits), held[c, 1](own_bits)])
        return (total / experts).astype(jnp.bfloat16)

    shares = lax.all_to_all(
        context.reshape(experts, quarter, columns), "expert", split_axis=0, concat_axis=0, tiled=True
    )

    spread_shape = (blocks, quarter + ids.shape[0], features)
    to_blocks = pl.pallas_call(
        spread_kernel,
        out_shape=jax.ShapeDtypeStruct(spread_shape, jnp.bfloat16),
        in_specs=[whole(shares.shape), whole(ids.shape)],
        out_specs=whole(spread_shape),
        grid=(1,),
        compiler_params=params(),
        name="spread",
    )(shares, ids)
    got = branch_exchange(0, pack(after(position, shares), branch, 0, experts))
    branch_add(0, 0, after(got, to_blocks))
    from_blocks = lax.all_to_all(to_blocks, "fsdp", split_axis=0, concat_axis=0, tiled=True)
    for phase in range(1, bits):
        got = branch_exchange(phase, branch_sends(phase, 0))
        if phase == bits - 1:
            from_blocks, got = lax.optimization_barrier((from_blocks, got))
        branch_add(phase, 0, got)

    ids_all = from_blocks[:, quarter : quarter + id_rows].astype(jnp.int32)
    ids_all = ids_all.reshape(blocks, 4, tokens)
    own_share = from_blocks[:, :quarter]
    packed1 = branch_sends(0, 1)
    pieces = [exchange(own_share, "expert", k) if k else own_share for k in range(experts)]
    pieces, packed1 = lax.optimization_barrier((pieces, packed1))
    side_shape = (planes, experts, quarter, features)
    sides = pl.pallas_call(
        sides_kernel,
        out_shape=(jax.ShapeDtypeStruct(side_shape, jnp.bfloat16),) * 2,
        in_specs=[smem()] + [whole((planes, 2, quarter, features))] * experts,
        out_specs=(whole(side_shape),) * 2,
        grid=(1,),
        compiler_params=params(),
        name="sides",
    )(position, *[piece.reshape(planes, 2, quarter, features) for piece in pieces])
    sides = [side.reshape(planes * tokens, features) for side in sides]
    signs = pl.pallas_call(
        functools.partial(signs_kernel, experts),
        out_shape=jax.ShapeDtypeStruct((blocks, capacity, lanes), jnp.float32),
        in_specs=[smem(), whole(ids_all.shape)],
        out_specs=whole((blocks, capacity, lanes)),
        grid=(1,),
        compiler_params=params(),
        name="signs",
    )(position, ids_all).reshape(planes, 2, capacity, lanes)

    gate_view = gate_w.reshape(experts, CHUNKS, part, units)
    up_view = up_w.reshape(experts, CHUNKS, part, units)
    tile = min(256, units)
    stretch = min(512, units)
    tiles = units // tile
    def pair_of(merged):
        def attend(rows):
            out = jnp.dot(rows, merged, preferred_element_type=jnp.float32)
            return out.reshape(planes, tokens, part)

        swapped = exchange(attend(sides[1]).astype(jnp.bfloat16), "fsdp", 1)
        return attend(sides[0]) + swapped.astype(jnp.float32)

    def plane_sends(pair):
        return [pick(pair, plane ^ k, 0).astype(jnp.bfloat16) for k in range(1, planes)]

    def plane_exchange(sends):
        return [exchange(send, "fsdp", 2 * k) for k, send in enumerate(sends, 1)]

    def scaled_of(c, pair, arrived):
        span = slice(c * part, (c + 1) * part)
        hstate = residual[:, span].astype(jnp.float32) + pick(pair, plane, 0)
        for value in arrived:
            hstate = hstate + value.astype(jnp.float32)
        return (hstate * norm_gain[span].astype(jnp.float32)).astype(jnp.bfloat16)

    height = count + lanes

    def slots_of(c, own_tokens):
        return pl.pallas_call(
            dispatch_kernel,
            out_shape=jax.ShapeDtypeStruct((experts, height, part), jnp.bfloat16),
            in_specs=[smem(), whole(ids_all.shape)]
            + [pl.BlockSpec((lanes, part), lambda i, c=c: (0, c))]
            + [whole((tokens, part))] * planes,
            out_specs=whole((experts, height, part)),
            grid=(1,),
            compiler_params=params(),
            name="dispatch",
        )(position, ids_all, extra, *own_tokens)

    merged0 = merged_of(0)
    got = branch_exchange(0, packed1)
    pair0 = pair_of(merged0)
    sends0 = plane_sends(pair0)
    branch_add(0, 1, after(got, sends0))
    arrived0 = plane_exchange(sends0)
    for phase in range(1, bits):
        got = branch_exchange(phase, branch_sends(phase, 1))
        if phase < bits - 1:
            branch_add(phase, 1, got)

    scaled0 = scaled_of(0, pair0, arrived0)
    tokens0 = [scaled0] + plane_exchange([scaled0] * (planes - 1))
    if bits > 1:
        branch_add(bits - 1, 1, after(got, tokens0[1]))
    merged1 = merged_of(1)
    merged_out = pl.pallas_call(
        join_kernel,
        out_shape=jax.ShapeDtypeStruct((features, columns), jnp.bfloat16),
        in_specs=[whole((features, part))] * CHUNKS,
        out_specs=whole((features, columns)),
        grid=(1,),
        compiler_params=params(),
        name="join",
    )(merged0, merged1)
    pair1 = pair_of(merged1)
    sends1 = plane_sends(pair1)
    arrived1 = plane_exchange(sends1)

    slots0 = slots_of(0, after(tokens0, arrived1[0]))
    scaled1 = scaled_of(1, pair1, after(arrived1, slots0))
    tokens1 = [scaled1] + plane_exchange([scaled1] * (planes - 1))
    slots1 = slots_of(1, tokens1)
    slots = (slots0, slots1)

    def to_experts(c):
        return lax.all_to_all(slots[c], "expert", split_axis=0, concat_axis=0, tiled=True)

    rows = after(to_experts(0), slots[-1], merged_out, signs)
    other = exchange(rows, "fsdp", 1)
    weight_spec = pl.BlockSpec((experts, 1, part, tile), lambda n: (0, 0, 0, n))
    sums = jax.ShapeDtypeStruct((2 * count, units), jnp.float32)
    sum_spec = pl.BlockSpec((2 * count, tile), lambda n: (0, n))
    any_spec = pl.BlockSpec(memory_space=pltpu.HBM)
    row_scratch = [
        pltpu.VMEM((2 * count, experts * part), jnp.bfloat16),
        pltpu.VMEM((experts, lanes, part), jnp.bfloat16),
    ]
    partial = pl.pallas_call(
        functools.partial(early_kernel, tiles),
        out_shape=(
            sums,
            sums,
            jax.ShapeDtypeStruct((2 * count, lanes), jnp.float32),
            jax.ShapeDtypeStruct((experts, part, 2 * count), jnp.bfloat16),
        ),
        in_specs=[any_spec, any_spec, weight_spec, weight_spec],
        out_specs=(
            sum_spec,
            sum_spec,
            whole((2 * count, lanes)),
            whole((experts, part, 2 * count)),
        ),
        grid=(tiles,),
        scratch_shapes=row_scratch + [pltpu.SemaphoreType.DMA((1 + 2 * experts,))],
        compiler_params=params(32),
        cost_estimate=pl.CostEstimate(
            flops=8 * count * experts * part * units,
            bytes_accessed=4 * experts * part * units,
            transcendentals=0,
        ),
        name="early",
    )(rows, other, gate_view, up_view)
    rows = after(to_experts(1), partial)
    other = exchange(rows, "fsdp", 1)

    tile_of = lambda i: jnp.minimum(i, tiles - 1)
    behind = lambda i: jnp.clip(i - 1, 0, tiles - 1)
    place_of = lambda i: jnp.maximum(i - tiles, 0)
    weight_spec = pl.BlockSpec((experts, 1, part, tile), lambda i: (0, 1, 0, tile_of(i)))
    sum_spec = pl.BlockSpec((2 * count, tile), lambda i: (0, tile_of(i)))
    unit_spec = pl.BlockSpec((planes, 2, capacity, tile), lambda i: (0, 0, 0, behind(i)))
    grad_spec = pl.BlockSpec(
        (1, columns, stretch), lambda i: (place_of(i) % experts, 0, place_of(i) // experts)
    )
    grad_shape = jax.ShapeDtypeStruct((experts, columns, units), jnp.bfloat16)
    gate_sums, up_sums, stats, turned_rows = partial
    hidden, grad_gate, grad_up = pl.pallas_call(
        functools.partial(late_kernel, float(width), tiles),
        out_shape=(
            jax.ShapeDtypeStruct((planes, 2, capacity, units), jnp.bfloat16),
            grad_shape,
            grad_shape,
        ),
        in_specs=[smem(), any_spec, any_spec, any_spec]
        + [weight_spec, weight_spec, sum_spec, sum_spec]
        + [whole(stats.shape), whole(signs.shape), unit_spec],
        out_specs=(unit_spec, grad_spec, grad_spec),
        grid=(tiles + experts * (units // stretch),),
        scratch_shapes=row_scratch
        + [
            pltpu.VMEM((2 * count, 1), jnp.float32),
            pltpu.VMEM((2 * count, 1), jnp.float32),
            pltpu.VMEM((2, 2 * count, tile), jnp.float32),
            pltpu.VMEM((2, 2 * count, tile), jnp.float32),
            pltpu.VMEM((2 * count, units), jnp.bfloat16),
            pltpu.VMEM((2 * count, units), jnp.bfloat16),
            pltpu.VMEM((experts, columns, 2 * count), jnp.bfloat16),
            pltpu.SemaphoreType.DMA((2 + 2 * experts,)),
        ],
        compiler_params=params(60),
        name="late",
    )(
        position,
        rows,
        other,
        turned_rows,
        gate_view,
        up_view,
        gate_sums,
        up_sums,
        stats,
        signs,
        cot_hidden.reshape(planes, 2, capacity, units),
    )
    return (
        merged_out,
        hidden.reshape(1, -1, units),
        grad_gate.reshape(1, width, units),
        grad_up.reshape(1, width, units),
    )


def solution(mesh):
    placed = (
        P("expert", "fsdp", None),
        P("fsdp", "expert"),
        P("fsdp", "expert"),
        P("expert"),
        P("expert", None),
        P("expert", None, "fsdp"),
        P("expert", None, "fsdp"),
        P("fsdp", None),
        P("fsdp", None),
        P("expert", None, "fsdp"),
    )
    return jax.shard_map(
        per_device,
        mesh=mesh,
        in_specs=placed,
        out_specs=(
            P("fsdp", "expert"),
            P("expert", None, "fsdp"),
            P("expert", None, "fsdp"),
            P("expert", None, "fsdp"),
        ),
        check_vma=False,
    )
```

```python
import functools

import jax
import jax.numpy as jnp
from jax import lax
from jax.experimental import pallas as pl
from jax.experimental.pallas import tpu as pltpu
from jax.sharding import PartitionSpec as P

CHUNKS = 2
MEBI = 1024 * 1024


def exchange(value, axis, offset):
    size = lax.axis_size(axis)
    return lax.ppermute(value, axis, [(i, i ^ offset) for i in range(size)])


def pick(value, index, axis):
    return lax.dynamic_index_in_dim(value, index, axis, keepdims=False)


def after(value, *others):
    return lax.optimization_barrier((value, others))[0]


def bits_of(size):
    return size.bit_length() - 1


def whole(shape):
    return pl.BlockSpec(shape, lambda *_: (0,) * len(shape))


def smem():
    return pl.BlockSpec(memory_space=pltpu.SMEM)


def params(mebi=16):
    return pltpu.CompilerParams(vmem_limit_bytes=mebi * MEBI)


def signs_kernel(experts, position_ref, ids_ref, out_ref):
    blocks, capacity, lanes = out_ref.shape
    tokens = ids_ref.shape[2]
    expert = position_ref[0]
    slots = lax.broadcasted_iota(jnp.int32, (capacity, tokens), 0)
    rows = lax.broadcasted_iota(jnp.int32, (lanes, tokens), 0)
    last = lax.broadcasted_iota(jnp.int32, (capacity, lanes), 1) == lanes - 1
    for b in range(blocks):
        ids = ids_ref[b]
        e0, e1, s0, s1 = ids[0:1], ids[1:2], ids[2:3], ids[3:4]
        hit0 = jnp.where((e0 == expert) & (s0 == slots), 1.0, 0.0)
        hit1 = jnp.where((e1 == expert) & (s1 == slots), 1.0, 0.0)
        table = jnp.where(e0 == rows - 1, 1.0, 0.0) - jnp.where(e1 == rows - 1, 1.0, 0.0)
        signs = lax.dot_general(
            (hit0 - hit1).astype(jnp.bfloat16),
            table.astype(jnp.bfloat16),
            (((1,), (1,)), ((), ())),
            preferred_element_type=jnp.float32,
        )
        filled = jnp.sum(hit0 + hit1, axis=1, keepdims=True)
        out_ref[b] = jnp.where(last, filled, signs)


def pack_kernel(c, flip, position_ref, branch_ref, low_out, high_out, sems):
    others, half, part = low_out.shape
    expert = position_ref[0]
    copies = []
    for j in range(others):
        low = 2 * j + (expert % 2 ^ flip)
        high = j + others * (expert // others ^ flip)
        for h, (place, out) in enumerate(((low, low_out), (high, high_out))):
            columns = pl.ds(pl.multiple_of((place * CHUNKS + c) * part, 128), part)
            source = branch_ref.at[pl.ds(h * half, half), columns]
            copies.append(pltpu.make_async_copy(source, out.at[j], sems.at[2 * j + h]))
    for copy in copies:
        copy.start()
    for copy in copies:
        copy.wait()


def pack(position, branch, c, flip, experts):
    others = experts // 2
    shape = (others, branch.shape[0] // 2, branch.shape[1] // experts // CHUNKS)
    source_spec = pl.BlockSpec(memory_space=pltpu.HBM)
    spec = pl.BlockSpec(memory_space=pl.ANY)
    return pl.pallas_call(
        functools.partial(pack_kernel, c, flip),
        out_shape=(jax.ShapeDtypeStruct(shape, jnp.bfloat16),) * 2,
        in_specs=[smem(), source_spec],
        out_specs=(spec, spec),
        scratch_shapes=[pltpu.SemaphoreType.DMA((2 * others,))],
        compiler_params=params(),
        name="pack",
    )(position, branch)


def join_kernel(*refs):
    *part_refs, out_ref = refs
    part = part_refs[0].shape[1]
    for c, part_ref in enumerate(part_refs):
        out_ref[:, c * part : (c + 1) * part] = part_ref[...]


def spread_kernel(shares_ref, ids_ref, out_ref):
    experts, quarter, columns = shares_ref.shape
    blocks, _, features = out_ref.shape
    per_expert = blocks // experts
    for f in range(blocks):
        start = (f % per_expert) * features
        out_ref[f, :quarter] = shares_ref[f // per_expert, :, start : start + features]
        out_ref[f, quarter:] = ids_ref[...]


def sides_kernel(position_ref, *refs):
    *share_refs, own_ref, other_ref = refs
    for k, share_ref in enumerate(share_refs):
        place = position_ref[0] ^ k
        for side, out_ref in enumerate((own_ref, other_ref)):
            out_ref[:, place] = share_ref[:, position_ref[2] ^ side]


def dispatch_kernel(position_ref, ids_ref, extra_ref, *refs):
    *token_refs, out_ref = refs
    planes = len(token_refs)
    experts, _, part = out_ref.shape
    lanes = extra_ref.shape[0]
    count = out_ref.shape[1] - lanes
    capacity = count // planes
    tokens = ids_ref.shape[2]
    plane, core = position_ref[1], position_ref[2]
    slots = lax.broadcasted_iota(jnp.int32, (experts * capacity, tokens), 0)
    for k in range(planes):
        source = plane ^ k
        ids = ids_ref[source * 2 + core]
        code0 = ids[0:1] * capacity + ids[2:3]
        code1 = ids[1:2] * capacity + ids[3:4]
        one_hot = jnp.where((code0 == slots) | (code1 == slots), 1.0, 0.0).astype(jnp.bfloat16)
        picked = jnp.dot(one_hot, token_refs[k][...], preferred_element_type=jnp.float32)
        rows = pl.ds(pl.multiple_of(source * capacity, 16), capacity)
        out_ref[:, rows] = picked.reshape(experts, capacity, part).astype(jnp.bfloat16)
    for e in range(experts):
        out_ref[e, count:] = extra_ref[...]


def row_stats(flat_ref, side, aux_ref):
    count = flat_ref.shape[0] // 2
    experts, lanes, part = aux_ref.shape
    squares = jnp.zeros((count, part), jnp.float32)
    logits = jnp.zeros((count, lanes), jnp.float32)
    for e in range(experts):
        rows = flat_ref[side * count : (side + 1) * count, e * part : (e + 1) * part]
        aux = aux_ref[e]
        ratio = rows.astype(jnp.float32) * (1.0 / aux[0:1].astype(jnp.float32))
        squares = squares + ratio * ratio
        logits = logits + lax.dot_general(
            rows, aux, (((1,), (1,)), ((), ())), preferred_element_type=jnp.float32
        )
    total = jnp.sum(squares, axis=1, keepdims=True)
    return jnp.where(lax.broadcasted_iota(jnp.int32, logits.shape, 1) == 0, total, logits)


def row_copies(sides, flat_ref, aux_ref, sems):
    count = flat_ref.shape[0] // 2
    experts, _, part = aux_ref.shape
    copies = [
        pltpu.make_async_copy(sides[0].at[:, pl.ds(count, aux_ref.shape[1])], aux_ref, sems.at[0])
    ]
    for side, rows_ref in enumerate(sides):
        for e in range(experts):
            copies.append(
                pltpu.make_async_copy(
                    rows_ref.at[e, pl.ds(0, count)],
                    flat_ref.at[pl.ds(side * count, count), pl.ds(e * part, part)],
                    sems.at[1 + side * experts + e],
                )
            )
    return copies


def turned(flat_ref, e, part):
    return flat_ref[:, e * part : (e + 1) * part].T


def product(flat_ref, weight_ref):
    weight = weight_ref[...].reshape(flat_ref.shape[1], weight_ref.shape[3])
    return jnp.dot(flat_ref[...], weight, preferred_element_type=jnp.float32)


def shares_of(experts, tiles, t):
    return range(t * experts // tiles, (t + 1) * experts // tiles)


def early_kernel(
    tiles,
    own_ref,
    other_ref,
    gate_ref,
    up_ref,
    gate_out,
    up_out,
    stats_out,
    turned_out,
    flat_scratch,
    aux_scratch,
    sems,
):
    count = flat_scratch.shape[0] // 2
    experts, _, part = aux_scratch.shape

    for t in range(tiles):

        @pl.when(pl.program_id(0) == t)
        def _():
            if t == 0:
                copies = row_copies((own_ref, other_ref), flat_scratch, aux_scratch, sems)
                for copy in copies:
                    copy.start()
                for copy in copies:
                    copy.wait()
            gate_out[...] = product(flat_scratch, gate_ref)
            up_out[...] = product(flat_scratch, up_ref)
            for e in shares_of(experts, tiles, t):
                turned_out[e] = turned(flat_scratch, e, part)
            if t == tiles - 1:
                for side in range(2):
                    stats_out[side * count : (side + 1) * count] = row_stats(
                        flat_scratch, side, aux_scratch
                    )


def late_kernel(
    width,
    tiles,
    position_ref,
    own_ref,
    other_ref,
    turned_ref,
    gate_ref,
    up_ref,
    gate_acc,
    up_acc,
    stats_ref,
    signs_ref,
    cot_ref,
    hidden_out,
    grad_gate_out,
    grad_up_out,
    flat_scratch,
    aux_scratch,
    scale_scratch,
    weight_scratch,
    gate_scratch,
    up_scratch,
    d_gate_scratch,
    d_up_scratch,
    turned_scratch,
    sems,
):
    step = pl.program_id(0)
    core = position_ref[2]
    planes, _, capacity, tile = hidden_out.shape
    count = planes * capacity
    experts, _, part = aux_scratch.shape
    lanes = stats_ref.shape[1]
    turn_copy = pltpu.make_async_copy(
        turned_ref, turned_scratch.at[:, pl.ds(0, part)], sems.at[1 + 2 * experts]
    )

    def scales():
        for side in range(2):
            span = slice(side * count, (side + 1) * count)
            stats = stats_ref[span] + row_stats(flat_scratch, side, aux_scratch)
            inverse = lax.rsqrt(stats[:, 0:1] / width + 1e-05)
            signs = signs_ref[:, pl.ds(core ^ side, 1)].reshape(count, lanes)
            filled = signs[:, lanes - 1 :]
            column = lax.broadcasted_iota(jnp.int32, stats.shape, 1)
            router = (column >= 1) & (column <= experts)
            margin = jnp.sum(jnp.where(router, stats * signs, 0.0), axis=1, keepdims=True)
            prob = jax.nn.sigmoid(margin * inverse).astype(jnp.bfloat16).astype(jnp.float32)
            scale_scratch[span] = inverse
            weight_scratch[span] = jnp.where(filled > 0.0, prob, 0.0)

    def units_of(t):
        for side in range(2):
            span = slice(side * count, (side + 1) * count)
            inverse = scale_scratch[span]
            weight = weight_scratch[span]
            gate_pre = inverse * gate_scratch[t % 2, span]
            up_pre = inverse * up_scratch[t % 2, span]
            sig_gate = jax.nn.sigmoid(gate_pre)
            act_gate = gate_pre * sig_gate
            hidden = (weight * act_gate * up_pre).astype(jnp.bfloat16)
            hidden_out[:, pl.ds(core ^ side, 1)] = hidden.reshape(planes, 1, capacity, tile)
            cot = cot_ref[:, pl.ds(core ^ side, 1)].reshape(count, tile)
            d_pre = cot.astype(jnp.float32) * (weight * inverse)
            d_gate = d_pre * up_pre * sig_gate * (1.0 + gate_pre * (1.0 - sig_gate))
            columns = slice(t * tile, (t + 1) * tile)
            d_gate_scratch[span, columns] = d_gate.astype(jnp.bfloat16)
            d_up_scratch[span, columns] = (d_pre * act_gate).astype(jnp.bfloat16)

    def gradients(stretch):
        e = (step - tiles) % experts
        stretch_units = grad_gate_out.shape[2]
        span = slice(stretch * stretch_units, (stretch + 1) * stretch_units)
        for scratch, out in ((d_gate_scratch, grad_gate_out), (d_up_scratch, grad_up_out)):
            out[0] = jnp.dot(
                turned_scratch[e], scratch[:, span], preferred_element_type=jnp.float32
            ).astype(jnp.bfloat16)

    for t in range(tiles):

        @pl.when(step == t)
        def _():
            if t == 0:
                copies = row_copies((own_ref, other_ref), flat_scratch, aux_scratch, sems)
                for copy in copies:
                    copy.start()
                turn_copy.start()
                for copy in copies:
                    copy.wait()
            gate_scratch[t % 2] = gate_acc[...] + product(flat_scratch, gate_ref)
            up_scratch[t % 2] = up_acc[...] + product(flat_scratch, up_ref)
            for e in shares_of(experts, tiles, t):
                turned_scratch[e, part:] = turned(flat_scratch, e, part)
            if t == 0:
                scales()
            else:
                units_of(t - 1)

    @pl.when(step == tiles)
    def _():
        turn_copy.wait()
        units_of(tiles - 1)
        gradients(0)

    for stretch in range(tiles * tile // grad_gate_out.shape[2]):
        first = tiles + stretch * experts

        @pl.when((step >= first) & (step < first + experts) & (step > tiles))
        def _():
            gradients(stretch)


def per_device(
    branch_wo,
    context,
    residual,
    norm_gain,
    router_w,
    gate_w,
    up_w,
    expert_ids,
    slot_ids,
    cot_hidden,
):
    experts = lax.axis_size("expert")
    blocks = lax.axis_size("fsdp")
    planes = blocks // 2
    expert = lax.axis_index("expert")
    block = lax.axis_index("fsdp")
    plane, core = block // 2, block % 2
    tokens, columns = context.shape
    width = columns * experts
    features = width // blocks
    capacity = cot_hidden.shape[1] // blocks
    units = cot_hidden.shape[2]
    part = columns // CHUNKS
    quarter = tokens // experts
    count = planes * capacity
    position = jnp.stack([expert, plane, core]).astype(jnp.int32)
    bits = bits_of(experts)

    lanes = experts + 2 + (-(experts + 2)) % 16
    extra = jnp.concatenate([norm_gain[None], router_w.T])
    extra = jnp.pad(extra, ((0, lanes - extra.shape[0]), (0, 0)))
    ids = jnp.concatenate([expert_ids, slot_ids], axis=1).T.astype(jnp.bfloat16)
    id_rows = ids.size // features
    ids = jnp.pad(ids.reshape(id_rows, features), ((0, -id_rows % 16), (0, 0)))

    branch = branch_wo[0]
    weights = [1 << (bits - 1 - i) for i in range(bits)]
    own_bits = [(expert // weight) % 2 for weight in weights]

    def start_sum(kept, first):
        def value(chosen):
            place = 0
            for i in range(bits):
                place = place if i == first else 2 * place + chosen[i]
            return pick(kept, place, 0).astype(jnp.float32)

        return value

    def joined(value, got, axis, rest):
        def total(chosen):
            chosen = [own_bits[axis] if i == axis else bit for i, bit in enumerate(chosen)]
            place = 0
            for i in rest:
                place = 2 * place + chosen[i]
            return value(chosen) + pick(got, place, 0).astype(jnp.float32)

        return total

    orders = (list(range(bits))[::-1], list(range(bits)))
    held = {}

    def keep(c, position):
        for h, kept in enumerate(pack(position, branch, c, 0, experts)):
            held[c, h] = start_sum(kept, orders[h][0])

    def branch_sends(phase, c):
        if phase == 0:
            return pack(position, branch, c, 1, experts)
        sends = []
        for h, order in enumerate(orders):
            rest = sorted(order[phase + 1 :])
            stacked = []
            for code in range(1 << len(rest)):
                chosen = list(own_bits)
                chosen[order[phase]] = 1 - own_bits[order[phase]]
                for at, i in enumerate(rest):
                    chosen[i] = (code >> (len(rest) - 1 - at)) & 1
                stacked.append(held[c, h](chosen).astype(jnp.bfloat16))
            sends.append(stacked[0][None] if len(stacked) == 1 else jnp.stack(stacked))
        return tuple(sends)

    def branch_exchange(phase, sends):
        return tuple(
            exchange(sends[h], "expert", weights[order[phase]]) for h, order in enumerate(orders)
        )

    def branch_add(phase, c, got):
        for h, order in enumerate(orders):
            held[c, h] = joined(held[c, h], got[h], order[phase], sorted(order[phase + 1 :]))

    def merged_of(c):
        total = jnp.concatenate([held[c, 0](own_bits), held[c, 1](own_bits)])
        return (total / experts).astype(jnp.bfloat16)

    shares = lax.all_to_all(
        context.reshape(experts, quarter, columns), "expert", split_axis=0, concat_axis=0, tiled=True
    )

    spread_shape = (blocks, quarter + ids.shape[0], features)
    to_blocks = pl.pallas_call(
        spread_kernel,
        out_shape=jax.ShapeDtypeStruct(spread_shape, jnp.bfloat16),
        in_specs=[whole(shares.shape), whole(ids.shape)],
        out_specs=whole(spread_shape),
        grid=(1,),
        compiler_params=params(),
        name="spread",
    )(shares, ids)
    got = branch_exchange(0, pack(after(position, shares), branch, 0, 1, experts))
    keep(0, after(position, to_blocks))
    branch_add(0, 0, after(got, to_blocks))
    from_blocks = lax.all_to_all(to_blocks, "fsdp", split_axis=0, concat_axis=0, tiled=True)
    for phase in range(1, bits):
        got = branch_exchange(phase, branch_sends(phase, 0))
        if phase == bits - 1:
            from_blocks, got = lax.optimization_barrier((from_blocks, got))
        branch_add(phase, 0, got)

    ids_all = from_blocks[:, quarter : quarter + id_rows].astype(jnp.int32)
    ids_all = ids_all.reshape(blocks, 4, tokens)
    own_share = from_blocks[:, :quarter]
    packed1 = branch_sends(0, 1)
    keep(1, after(position, packed1))
    pieces = [exchange(own_share, "expert", k) if k else own_share for k in range(experts)]
    pieces, packed1 = lax.optimization_barrier((pieces, packed1))
    side_shape = (planes, experts, quarter, features)
    sides = pl.pallas_call(
        sides_kernel,
        out_shape=(jax.ShapeDtypeStruct(side_shape, jnp.bfloat16),) * 2,
        in_specs=[smem()] + [whole((planes, 2, quarter, features))] * experts,
        out_specs=(whole(side_shape),) * 2,
        grid=(1,),
        compiler_params=params(),
        name="sides",
    )(position, *[piece.reshape(planes, 2, quarter, features) for piece in pieces])
    sides = [side.reshape(planes * tokens, features) for side in sides]
    signs = pl.pallas_call(
        functools.partial(signs_kernel, experts),
        out_shape=jax.ShapeDtypeStruct((blocks, capacity, lanes), jnp.float32),
        in_specs=[smem(), whole(ids_all.shape)],
        out_specs=whole((blocks, capacity, lanes)),
        grid=(1,),
        compiler_params=params(),
        name="signs",
    )(position, ids_all).reshape(planes, 2, capacity, lanes)

    gate_view = gate_w.reshape(experts, CHUNKS, part, units)
    up_view = up_w.reshape(experts, CHUNKS, part, units)
    tile = min(256, units)
    stretch = min(512, units)
    tiles = units // tile
    def pair_of(merged):
        def attend(rows):
            out = jnp.dot(rows, merged, preferred_element_type=jnp.float32)
            return out.reshape(planes, tokens, part)

        swapped = exchange(attend(sides[1]).astype(jnp.bfloat16), "fsdp", 1)
        return attend(sides[0]) + swapped.astype(jnp.float32)

    def plane_sends(pair):
        return [pick(pair, plane ^ k, 0).astype(jnp.bfloat16) for k in range(1, planes)]

    def plane_exchange(sends):
        return [exchange(send, "fsdp", 2 * k) for k, send in enumerate(sends, 1)]

    def scaled_of(c, pair, arrived):
        span = slice(c * part, (c + 1) * part)
        hstate = residual[:, span].astype(jnp.float32) + pick(pair, plane, 0)
        for value in arrived:
            hstate = hstate + value.astype(jnp.float32)
        return (hstate * norm_gain[span].astype(jnp.float32)).astype(jnp.bfloat16)

    height = count + lanes

    def slots_of(c, own_tokens):
        return pl.pallas_call(
            dispatch_kernel,
            out_shape=jax.ShapeDtypeStruct((experts, height, part), jnp.bfloat16),
            in_specs=[smem(), whole(ids_all.shape)]
            + [pl.BlockSpec((lanes, part), lambda i, c=c: (0, c))]
            + [whole((tokens, part))] * planes,
            out_specs=whole((experts, height, part)),
            grid=(1,),
            compiler_params=params(),
            name="dispatch",
        )(position, ids_all, extra, *own_tokens)

    merged0 = merged_of(0)
    got = branch_exchange(0, packed1)
    pair0 = pair_of(merged0)
    sends0 = plane_sends(pair0)
    branch_add(0, 1, after(got, sends0))
    arrived0 = plane_exchange(sends0)
    for phase in range(1, bits):
        got = branch_exchange(phase, branch_sends(phase, 1))
        if phase < bits - 1:
            branch_add(phase, 1, got)

    scaled0 = scaled_of(0, pair0, arrived0)
    tokens0 = [scaled0] + plane_exchange([scaled0] * (planes - 1))
    if bits > 1:
        branch_add(bits - 1, 1, after(got, scaled0))
    merged1 = merged_of(1)
    merged_out = pl.pallas_call(
        join_kernel,
        out_shape=jax.ShapeDtypeStruct((features, columns), jnp.bfloat16),
        in_specs=[whole((features, part))] * CHUNKS,
        out_specs=whole((features, columns)),
        grid=(1,),
        compiler_params=params(),
        name="join",
    )(merged0, merged1)
    pair1 = pair_of(merged1)
    sends1 = plane_sends(pair1)
    arrived1 = plane_exchange(sends1)

    scaled1 = scaled_of(1, pair1, arrived1)
    slots0 = slots_of(0, after(tokens0, scaled1))
    tokens1 = [scaled1] + plane_exchange([scaled1] * (planes - 1))
    slots1 = slots_of(1, tokens1)
    slots = (slots0, slots1)

    def to_experts(c):
        return lax.all_to_all(slots[c], "expert", split_axis=0, concat_axis=0, tiled=True)

    rows = after(to_experts(0), slots[-1], merged_out, signs)
    other = exchange(rows, "fsdp", 1)
    weight_spec = pl.BlockSpec((experts, 1, part, tile), lambda n: (0, 0, 0, n))
    sums = jax.ShapeDtypeStruct((2 * count, units), jnp.float32)
    sum_spec = pl.BlockSpec((2 * count, tile), lambda n: (0, n))
    any_spec = pl.BlockSpec(memory_space=pl.ANY)
    row_scratch = [
        pltpu.VMEM((2 * count, experts * part), jnp.bfloat16),
        pltpu.VMEM((experts, lanes, part), jnp.bfloat16),
    ]
    partial = pl.pallas_call(
        functools.partial(early_kernel, tiles),
        out_shape=(
            sums,
            sums,
            jax.ShapeDtypeStruct((2 * count, lanes), jnp.float32),
            jax.ShapeDtypeStruct((experts, part, 2 * count), jnp.bfloat16),
        ),
        in_specs=[any_spec, any_spec, weight_spec, weight_spec],
        out_specs=(
            sum_spec,
            sum_spec,
            whole((2 * count, lanes)),
            whole((experts, part, 2 * count)),
        ),
        grid=(tiles,),
        scratch_shapes=row_scratch + [pltpu.SemaphoreType.DMA((1 + 2 * experts,))],
        compiler_params=params(60),
        cost_estimate=pl.CostEstimate(
            flops=8 * count * experts * part * units,
            bytes_accessed=4 * experts * part * units,
            transcendentals=0,
        ),
        name="early",
    )(rows, other, gate_view, up_view)
    rows = after(to_experts(1), partial)
    other = exchange(rows, "fsdp", 1)

    tile_of = lambda i: jnp.minimum(i, tiles - 1)
    behind = lambda i: jnp.clip(i - 1, 0, tiles - 1)
    place_of = lambda i: jnp.maximum(i - tiles, 0)
    weight_spec = pl.BlockSpec((experts, 1, part, tile), lambda i: (0, 1, 0, tile_of(i)))
    sum_spec = pl.BlockSpec((2 * count, tile), lambda i: (0, tile_of(i)))
    unit_spec = pl.BlockSpec((planes, 2, capacity, tile), lambda i: (0, 0, 0, behind(i)))
    grad_spec = pl.BlockSpec(
        (1, columns, stretch), lambda i: (place_of(i) % experts, 0, place_of(i) // experts)
    )
    grad_shape = jax.ShapeDtypeStruct((experts, columns, units), jnp.bfloat16)
    gate_sums, up_sums, stats, turned_rows = partial
    hidden, grad_gate, grad_up = pl.pallas_call(
        functools.partial(late_kernel, float(width), tiles),
        out_shape=(
            jax.ShapeDtypeStruct((planes, 2, capacity, units), jnp.bfloat16),
            grad_shape,
            grad_shape,
        ),
        in_specs=[smem(), any_spec, any_spec, any_spec]
        + [weight_spec, weight_spec, sum_spec, sum_spec]
        + [whole(stats.shape), whole(signs.shape), unit_spec],
        out_specs=(unit_spec, grad_spec, grad_spec),
        grid=(tiles + experts * (units // stretch),),
        scratch_shapes=row_scratch
        + [
            pltpu.VMEM((2 * count, 1), jnp.float32),
            pltpu.VMEM((2 * count, 1), jnp.float32),
            pltpu.VMEM((2, 2 * count, tile), jnp.float32),
            pltpu.VMEM((2, 2 * count, tile), jnp.float32),
            pltpu.VMEM((2 * count, units), jnp.bfloat16),
            pltpu.VMEM((2 * count, units), jnp.bfloat16),
            pltpu.VMEM((experts, columns, 2 * count), jnp.bfloat16),
            pltpu.SemaphoreType.DMA((2 + 2 * experts,)),
        ],
        compiler_params=params(60),
        name="late",
    )(
        position,
        rows,
        other,
        turned_rows,
        gate_view,
        up_view,
        gate_sums,
        up_sums,
        stats,
        signs,
        cot_hidden.reshape(planes, 2, capacity, units),
    )
    return (
        merged_out,
        hidden.reshape(1, -1, units),
        grad_gate.reshape(1, width, units),
        grad_up.reshape(1, width, units),
    )


def solution(mesh):
    placed = (
        P("expert", "fsdp", None),
        P("fsdp", "expert"),
        P("fsdp", "expert"),
        P("expert"),
        P("expert", None),
        P("expert", None, "fsdp"),
        P("expert", None, "fsdp"),
        P("fsdp", None),
        P("fsdp", None),
        P("expert", None, "fsdp"),
    )
    return jax.shard_map(
        per_device,
        mesh=mesh,
        in_specs=placed,
        out_specs=(
            P("fsdp", "expert"),
            P("expert", None, "fsdp"),
            P("expert", None, "fsdp"),
            P("expert", None, "fsdp"),
        ),
        check_vma=False,
    )
```

```python
import functools

import jax
import jax.numpy as jnp
from jax import lax
from jax.experimental import pallas as pl
from jax.experimental.pallas import tpu as pltpu
from jax.sharding import PartitionSpec as P

CHUNKS = 2
MEBI = 1024 * 1024


def exchange(value, axis, offset):
    size = lax.axis_size(axis)
    return lax.ppermute(value, axis, [(i, i ^ offset) for i in range(size)])


def pick(value, index, axis):
    return lax.dynamic_index_in_dim(value, index, axis, keepdims=False)


def after(value, *others):
    return lax.optimization_barrier((value, others))[0]


def bits_of(size):
    return size.bit_length() - 1


def whole(shape):
    return pl.BlockSpec(shape, lambda *_: (0,) * len(shape))


def smem():
    return pl.BlockSpec(memory_space=pltpu.SMEM)


def params(mebi=16):
    return pltpu.CompilerParams(vmem_limit_bytes=mebi * MEBI)


def signs_kernel(experts, position_ref, ids_ref, out_ref):
    blocks, capacity, lanes = out_ref.shape
    tokens = ids_ref.shape[2]
    expert = position_ref[0]
    slots = lax.broadcasted_iota(jnp.int32, (capacity, tokens), 0)
    rows = lax.broadcasted_iota(jnp.int32, (lanes, tokens), 0)
    last = lax.broadcasted_iota(jnp.int32, (capacity, lanes), 1) == lanes - 1
    for b in range(blocks):
        ids = ids_ref[b]
        e0, e1, s0, s1 = ids[0:1], ids[1:2], ids[2:3], ids[3:4]
        hit0 = jnp.where((e0 == expert) & (s0 == slots), 1.0, 0.0)
        hit1 = jnp.where((e1 == expert) & (s1 == slots), 1.0, 0.0)
        table = jnp.where(e0 == rows - 1, 1.0, 0.0) - jnp.where(e1 == rows - 1, 1.0, 0.0)
        signs = lax.dot_general(
            (hit0 - hit1).astype(jnp.bfloat16),
            table.astype(jnp.bfloat16),
            (((1,), (1,)), ((), ())),
            preferred_element_type=jnp.float32,
        )
        filled = jnp.sum(hit0 + hit1, axis=1, keepdims=True)
        out_ref[b] = jnp.where(last, filled, signs)


def pack_kernel(c, flip, position_ref, branch_ref, low_out, high_out, sems):
    others, half, part = low_out.shape
    expert = position_ref[0]
    copies = []
    for j in range(others):
        low = 2 * j + (expert % 2 ^ flip)
        high = j + others * (expert // others ^ flip)
        for h, (place, out) in enumerate(((low, low_out), (high, high_out))):
            columns = pl.ds(pl.multiple_of((place * CHUNKS + c) * part, 128), part)
            source = branch_ref.at[pl.ds(h * half, half), columns]
            copies.append(pltpu.make_async_copy(source, out.at[j], sems.at[2 * j + h]))
    for copy in copies:
        copy.start()
    for copy in copies:
        copy.wait()


def pack(position, branch, c, flip, experts):
    others = experts // 2
    shape = (others, branch.shape[0] // 2, branch.shape[1] // experts // CHUNKS)
    source_spec = pl.BlockSpec(memory_space=pltpu.HBM)
    spec = pl.BlockSpec(memory_space=pl.ANY)
    return pl.pallas_call(
        functools.partial(pack_kernel, c, flip),
        out_shape=(jax.ShapeDtypeStruct(shape, jnp.bfloat16),) * 2,
        in_specs=[smem(), source_spec],
        out_specs=(spec, spec),
        scratch_shapes=[pltpu.SemaphoreType.DMA((2 * others,))],
        compiler_params=params(61),
        name="pack",
    )(position, branch)


def join_kernel(*refs):
    *part_refs, out_ref = refs
    part = part_refs[0].shape[1]
    for c, part_ref in enumerate(part_refs):
        out_ref[:, c * part : (c + 1) * part] = part_ref[...]


def spread_kernel(shares_ref, ids_ref, out_ref):
    experts, quarter, columns = shares_ref.shape
    blocks, _, features = out_ref.shape
    per_expert = blocks // experts
    for f in range(blocks):
        start = (f % per_expert) * features
        out_ref[f, :quarter] = shares_ref[f // per_expert, :, start : start + features]
        out_ref[f, quarter:] = ids_ref[...]


def sides_kernel(position_ref, *refs):
    *share_refs, own_ref, other_ref = refs
    for k, share_ref in enumerate(share_refs):
        place = position_ref[0] ^ k
        for side, out_ref in enumerate((own_ref, other_ref)):
            out_ref[:, place] = share_ref[:, position_ref[2] ^ side]


def dispatch_kernel(position_ref, ids_ref, extra_ref, *refs):
    *token_refs, out_ref = refs
    planes = len(token_refs)
    experts, _, part = out_ref.shape
    lanes = extra_ref.shape[0]
    count = out_ref.shape[1] - lanes
    capacity = count // planes
    tokens = ids_ref.shape[2]
    plane, core = position_ref[1], position_ref[2]
    slots = lax.broadcasted_iota(jnp.int32, (experts * capacity, tokens), 0)
    for k in range(planes):
        source = plane ^ k
        ids = ids_ref[source * 2 + core]
        code0 = ids[0:1] * capacity + ids[2:3]
        code1 = ids[1:2] * capacity + ids[3:4]
        one_hot = jnp.where((code0 == slots) | (code1 == slots), 1.0, 0.0).astype(jnp.bfloat16)
        picked = jnp.dot(one_hot, token_refs[k][...], preferred_element_type=jnp.float32)
        rows = pl.ds(pl.multiple_of(source * capacity, 16), capacity)
        out_ref[:, rows] = picked.reshape(experts, capacity, part).astype(jnp.bfloat16)
    for e in range(experts):
        out_ref[e, count:] = extra_ref[...]


def row_stats(flat_ref, side, aux_ref):
    count = flat_ref.shape[0] // 2
    experts, lanes, part = aux_ref.shape
    squares = jnp.zeros((count, part), jnp.float32)
    logits = jnp.zeros((count, lanes), jnp.float32)
    for e in range(experts):
        rows = flat_ref[side * count : (side + 1) * count, e * part : (e + 1) * part]
        aux = aux_ref[e]
        ratio = rows.astype(jnp.float32) * (1.0 / aux[0:1].astype(jnp.float32))
        squares = squares + ratio * ratio
        logits = logits + lax.dot_general(
            rows, aux, (((1,), (1,)), ((), ())), preferred_element_type=jnp.float32
        )
    total = jnp.sum(squares, axis=1, keepdims=True)
    return jnp.where(lax.broadcasted_iota(jnp.int32, logits.shape, 1) == 0, total, logits)


def row_copies(sides, flat_ref, aux_ref, sems):
    count = flat_ref.shape[0] // 2
    experts, _, part = aux_ref.shape
    copies = [
        pltpu.make_async_copy(sides[0].at[:, pl.ds(count, aux_ref.shape[1])], aux_ref, sems.at[0])
    ]
    for side, rows_ref in enumerate(sides):
        for e in range(experts):
            copies.append(
                pltpu.make_async_copy(
                    rows_ref.at[e, pl.ds(0, count)],
                    flat_ref.at[pl.ds(side * count, count), pl.ds(e * part, part)],
                    sems.at[1 + side * experts + e],
                )
            )
    return copies


def turned(flat_ref, e, part):
    return flat_ref[:, e * part : (e + 1) * part].T


def product(flat_ref, weight_ref):
    weight = weight_ref[...].reshape(flat_ref.shape[1], weight_ref.shape[3])
    return jnp.dot(flat_ref[...], weight, preferred_element_type=jnp.float32)


def shares_of(experts, tiles, t):
    return range(t * experts // tiles, (t + 1) * experts // tiles)


def early_kernel(
    tiles,
    own_ref,
    other_ref,
    gate_ref,
    up_ref,
    gate_out,
    up_out,
    stats_out,
    turned_out,
    flat_scratch,
    aux_scratch,
    sems,
):
    count = flat_scratch.shape[0] // 2
    experts, _, part = aux_scratch.shape

    for t in range(tiles):

        @pl.when(pl.program_id(0) == t)
        def _():
            if t == 0:
                copies = row_copies((own_ref, other_ref), flat_scratch, aux_scratch, sems)
                for copy in copies:
                    copy.start()
                for copy in copies:
                    copy.wait()
            gate_out[...] = product(flat_scratch, gate_ref)
            up_out[...] = product(flat_scratch, up_ref)
            for e in shares_of(experts, tiles, t):
                turned_out[e] = turned(flat_scratch, e, part)
            if t == tiles - 1:
                for side in range(2):
                    stats_out[side * count : (side + 1) * count] = row_stats(
                        flat_scratch, side, aux_scratch
                    )


def late_kernel(
    width,
    tiles,
    position_ref,
    own_ref,
    other_ref,
    turned_ref,
    gate_ref,
    up_ref,
    gate_acc,
    up_acc,
    stats_ref,
    signs_ref,
    cot_ref,
    hidden_out,
    grad_gate_out,
    grad_up_out,
    flat_scratch,
    aux_scratch,
    scale_scratch,
    weight_scratch,
    gate_scratch,
    up_scratch,
    d_gate_scratch,
    d_up_scratch,
    turned_scratch,
    sems,
):
    step = pl.program_id(0)
    core = position_ref[2]
    planes, _, capacity, tile = hidden_out.shape
    count = planes * capacity
    experts, _, part = aux_scratch.shape
    lanes = stats_ref.shape[1]
    turn_copy = pltpu.make_async_copy(
        turned_ref, turned_scratch.at[:, pl.ds(0, part)], sems.at[1 + 2 * experts]
    )

    def scales():
        for side in range(2):
            span = slice(side * count, (side + 1) * count)
            stats = stats_ref[span] + row_stats(flat_scratch, side, aux_scratch)
            inverse = lax.rsqrt(stats[:, 0:1] / width + 1e-05)
            signs = signs_ref[:, pl.ds(core ^ side, 1)].reshape(count, lanes)
            filled = signs[:, lanes - 1 :]
            column = lax.broadcasted_iota(jnp.int32, stats.shape, 1)
            router = (column >= 1) & (column <= experts)
            margin = jnp.sum(jnp.where(router, stats * signs, 0.0), axis=1, keepdims=True)
            prob = jax.nn.sigmoid(margin * inverse).astype(jnp.bfloat16).astype(jnp.float32)
            scale_scratch[span] = inverse
            weight_scratch[span] = jnp.where(filled > 0.0, prob, 0.0)

    def units_of(t):
        for side in range(2):
            span = slice(side * count, (side + 1) * count)
            inverse = scale_scratch[span]
            weight = weight_scratch[span]
            gate_pre = inverse * gate_scratch[t % 2, span]
            up_pre = inverse * up_scratch[t % 2, span]
            sig_gate = jax.nn.sigmoid(gate_pre)
            act_gate = gate_pre * sig_gate
            hidden = (weight * act_gate * up_pre).astype(jnp.bfloat16)
            hidden_out[:, pl.ds(core ^ side, 1)] = hidden.reshape(planes, 1, capacity, tile)
            cot = cot_ref[:, pl.ds(core ^ side, 1)].reshape(count, tile)
            d_pre = cot.astype(jnp.float32) * (weight * inverse)
            d_gate = d_pre * up_pre * sig_gate * (1.0 + gate_pre * (1.0 - sig_gate))
            columns = slice(t * tile, (t + 1) * tile)
            d_gate_scratch[span, columns] = d_gate.astype(jnp.bfloat16)
            d_up_scratch[span, columns] = (d_pre * act_gate).astype(jnp.bfloat16)

    def gradients(stretch):
        e = (step - tiles) % experts
        stretch_units = grad_gate_out.shape[2]
        span = slice(stretch * stretch_units, (stretch + 1) * stretch_units)
        for scratch, out in ((d_gate_scratch, grad_gate_out), (d_up_scratch, grad_up_out)):
            out[0] = jnp.dot(
                turned_scratch[e], scratch[:, span], preferred_element_type=jnp.float32
            ).astype(jnp.bfloat16)

    for t in range(tiles):

        @pl.when(step == t)
        def _():
            if t == 0:
                copies = row_copies((own_ref, other_ref), flat_scratch, aux_scratch, sems)
                for copy in copies:
                    copy.start()
                turn_copy.start()
                for copy in copies:
                    copy.wait()
            gate_scratch[t % 2] = gate_acc[...] + product(flat_scratch, gate_ref)
            up_scratch[t % 2] = up_acc[...] + product(flat_scratch, up_ref)
            for e in shares_of(experts, tiles, t):
                turned_scratch[e, part:] = turned(flat_scratch, e, part)
            if t == 0:
                scales()
            else:
                units_of(t - 1)

    @pl.when(step == tiles)
    def _():
        turn_copy.wait()
        units_of(tiles - 1)
        gradients(0)

    for stretch in range(tiles * tile // grad_gate_out.shape[2]):
        first = tiles + stretch * experts

        @pl.when((step >= first) & (step < first + experts) & (step > tiles))
        def _():
            gradients(stretch)


def per_device(
    branch_wo,
    context,
    residual,
    norm_gain,
    router_w,
    gate_w,
    up_w,
    expert_ids,
    slot_ids,
    cot_hidden,
):
    experts = lax.axis_size("expert")
    blocks = lax.axis_size("fsdp")
    planes = blocks // 2
    expert = lax.axis_index("expert")
    block = lax.axis_index("fsdp")
    plane, core = block // 2, block % 2
    tokens, columns = context.shape
    width = columns * experts
    features = width // blocks
    capacity = cot_hidden.shape[1] // blocks
    units = cot_hidden.shape[2]
    part = columns // CHUNKS
    quarter = tokens // experts
    count = planes * capacity
    position = jnp.stack([expert, plane, core]).astype(jnp.int32)
    bits = bits_of(experts)

    lanes = experts + 2 + (-(experts + 2)) % 16
    extra = jnp.concatenate([norm_gain[None], router_w.T])
    extra = jnp.pad(extra, ((0, lanes - extra.shape[0]), (0, 0)))
    ids = jnp.concatenate([expert_ids, slot_ids], axis=1).T.astype(jnp.bfloat16)
    id_rows = ids.size // features
    ids = jnp.pad(ids.reshape(id_rows, features), ((0, -id_rows % 16), (0, 0)))

    branch = branch_wo[0]
    weights = [1 << (bits - 1 - i) for i in range(bits)]
    own_bits = [(expert // weight) % 2 for weight in weights]

    def start_sum(kept, first):
        def value(chosen):
            place = 0
            for i in range(bits):
                place = place if i == first else 2 * place + chosen[i]
            return pick(kept, place, 0).astype(jnp.float32)

        return value

    def joined(value, got, axis, rest):
        def total(chosen):
            chosen = [own_bits[axis] if i == axis else bit for i, bit in enumerate(chosen)]
            place = 0
            for i in rest:
                place = 2 * place + chosen[i]
            return value(chosen) + pick(got, place, 0).astype(jnp.float32)

        return total

    orders = (list(range(bits))[::-1], list(range(bits)))
    held = {}

    def keep(c, position):
        for h, kept in enumerate(pack(position, branch, c, 0, experts)):
            held[c, h] = start_sum(kept, orders[h][0])

    def branch_sends(phase, c):
        if phase == 0:
            return pack(position, branch, c, 1, experts)
        sends = []
        for h, order in enumerate(orders):
            rest = sorted(order[phase + 1 :])
            stacked = []
            for code in range(1 << len(rest)):
                chosen = list(own_bits)
                chosen[order[phase]] = 1 - own_bits[order[phase]]
                for at, i in enumerate(rest):
                    chosen[i] = (code >> (len(rest) - 1 - at)) & 1
                stacked.append(held[c, h](chosen).astype(jnp.bfloat16))
            sends.append(stacked[0][None] if len(stacked) == 1 else jnp.stack(stacked))
        return tuple(sends)

    def branch_exchange(phase, sends):
        return tuple(
            exchange(sends[h], "expert", weights[order[phase]]) for h, order in enumerate(orders)
        )

    def branch_add(phase, c, got):
        for h, order in enumerate(orders):
            held[c, h] = joined(held[c, h], got[h], order[phase], sorted(order[phase + 1 :]))

    def merged_of(c):
        total = jnp.concatenate([held[c, 0](own_bits), held[c, 1](own_bits)])
        return (total / experts).astype(jnp.bfloat16)

    shares = lax.all_to_all(
        context.reshape(experts, quarter, columns), "expert", split_axis=0, concat_axis=0, tiled=True
    )

    spread_shape = (blocks, quarter + ids.shape[0], features)
    to_blocks = pl.pallas_call(
        spread_kernel,
        out_shape=jax.ShapeDtypeStruct(spread_shape, jnp.bfloat16),
        in_specs=[whole(shares.shape), whole(ids.shape)],
        out_specs=whole(spread_shape),
        grid=(1,),
        compiler_params=params(),
        name="spread",
    )(shares, ids)
    got = branch_exchange(0, pack(after(position, shares), branch, 0, 1, experts))
    keep(0, after(position, to_blocks))
    branch_add(0, 0, after(got, to_blocks))
    from_blocks = lax.all_to_all(to_blocks, "fsdp", split_axis=0, concat_axis=0, tiled=True)
    for phase in range(1, bits):
        got = branch_exchange(phase, branch_sends(phase, 0))
        if phase == bits - 1:
            from_blocks, got = lax.optimization_barrier((from_blocks, got))
        branch_add(phase, 0, got)

    ids_all = from_blocks[:, quarter : quarter + id_rows].astype(jnp.int32)
    ids_all = ids_all.reshape(blocks, 4, tokens)
    own_share = from_blocks[:, :quarter]
    packed1 = branch_sends(0, 1)
    keep(1, after(position, packed1))
    pieces = [exchange(own_share, "expert", k) if k else own_share for k in range(experts)]
    pieces, packed1 = lax.optimization_barrier((pieces, packed1))
    signs = pl.pallas_call(
        functools.partial(signs_kernel, experts),
        out_shape=jax.ShapeDtypeStruct((blocks, capacity, lanes), jnp.float32),
        in_specs=[smem(), whole(ids_all.shape)],
        out_specs=whole((blocks, capacity, lanes)),
        grid=(1,),
        compiler_params=params(),
        name="signs",
    )(position, ids_all).reshape(planes, 2, capacity, lanes)

    gate_view = gate_w.reshape(experts, CHUNKS, part, units)
    up_view = up_w.reshape(experts, CHUNKS, part, units)
    tile = min(256, units)
    stretch = min(512, units)
    tiles = units // tile
    pieces, signs = lax.optimization_barrier((pieces, signs))
    side_shape = (planes, experts, quarter, features)
    sides = pl.pallas_call(
        sides_kernel,
        out_shape=(jax.ShapeDtypeStruct(side_shape, jnp.bfloat16),) * 2,
        in_specs=[smem()] + [whole((planes, 2, quarter, features))] * experts,
        out_specs=(whole(side_shape),) * 2,
        grid=(1,),
        compiler_params=params(),
        name="sides",
    )(position, *[piece.reshape(planes, 2, quarter, features) for piece in pieces])
    sides = [side.reshape(planes * tokens, features) for side in sides]
    def pair_of(merged):
        def attend(rows):
            out = jnp.dot(rows, merged, preferred_element_type=jnp.float32)
            return out.reshape(planes, tokens, part)

        swapped = exchange(attend(sides[1]).astype(jnp.bfloat16), "fsdp", 1)
        return attend(sides[0]) + swapped.astype(jnp.float32)

    def plane_sends(pair):
        return [pick(pair, plane ^ k, 0).astype(jnp.bfloat16) for k in range(1, planes)]

    def plane_exchange(sends):
        return [exchange(send, "fsdp", 2 * k) for k, send in enumerate(sends, 1)]

    def scaled_of(c, pair, arrived):
        span = slice(c * part, (c + 1) * part)
        hstate = residual[:, span].astype(jnp.float32) + pick(pair, plane, 0)
        for value in arrived:
            hstate = hstate + value.astype(jnp.float32)
        return (hstate * norm_gain[span].astype(jnp.float32)).astype(jnp.bfloat16)

    height = count + lanes

    def slots_of(c, own_tokens):
        return pl.pallas_call(
            dispatch_kernel,
            out_shape=jax.ShapeDtypeStruct((experts, height, part), jnp.bfloat16),
            in_specs=[smem(), whole(ids_all.shape)]
            + [pl.BlockSpec((lanes, part), lambda i, c=c: (0, c))]
            + [whole((tokens, part))] * planes,
            out_specs=whole((experts, height, part)),
            grid=(1,),
            compiler_params=params(),
            name="dispatch",
        )(position, ids_all, extra, *own_tokens)

    merged0 = merged_of(0)
    got = branch_exchange(0, packed1)
    pair0 = pair_of(merged0)
    sends0 = plane_sends(pair0)
    branch_add(0, 1, after(got, sends0))
    arrived0 = plane_exchange(sends0)
    for phase in range(1, bits):
        got = branch_exchange(phase, branch_sends(phase, 1))
        if phase < bits - 1:
            branch_add(phase, 1, got)

    scaled0 = scaled_of(0, pair0, arrived0)
    tokens0 = [scaled0] + plane_exchange([scaled0] * (planes - 1))
    if bits > 1:
        branch_add(bits - 1, 1, after(got, scaled0))
    merged1 = merged_of(1)
    merged_out = pl.pallas_call(
        join_kernel,
        out_shape=jax.ShapeDtypeStruct((features, columns), jnp.bfloat16),
        in_specs=[whole((features, part))] * CHUNKS,
        out_specs=whole((features, columns)),
        grid=(1,),
        compiler_params=params(),
        name="join",
    )(merged0, merged1)
    pair1 = pair_of(merged1)
    sends1 = after(plane_sends(pair1), tokens0)
    arrived1 = plane_exchange(sends1)

    scaled1 = scaled_of(1, pair1, after(arrived1, merged_out))
    slots0 = slots_of(0, after(tokens0, scaled1))
    tokens1 = [scaled1] + plane_exchange([scaled1] * (planes - 1))
    slots1 = slots_of(1, tokens1)
    slots = (slots0, slots1)

    def to_experts(c):
        return lax.all_to_all(slots[c], "expert", split_axis=0, concat_axis=0, tiled=True)

    rows = after(to_experts(0), slots[-1], merged_out, signs)
    other = exchange(rows, "fsdp", 1)
    weight_spec = pl.BlockSpec((experts, 1, part, tile), lambda n: (0, 0, 0, n))
    sums = jax.ShapeDtypeStruct((2 * count, units), jnp.float32)
    sum_spec = pl.BlockSpec((2 * count, tile), lambda n: (0, n))
    any_spec = pl.BlockSpec(memory_space=pl.ANY)
    row_scratch = [
        pltpu.VMEM((2 * count, experts * part), jnp.bfloat16),
        pltpu.VMEM((experts, lanes, part), jnp.bfloat16),
    ]
    partial = pl.pallas_call(
        functools.partial(early_kernel, tiles),
        out_shape=(
            sums,
            sums,
            jax.ShapeDtypeStruct((2 * count, lanes), jnp.float32),
            jax.ShapeDtypeStruct((experts, part, 2 * count), jnp.bfloat16),
        ),
        in_specs=[any_spec, any_spec, weight_spec, weight_spec],
        out_specs=(
            sum_spec,
            sum_spec,
            whole((2 * count, lanes)),
            whole((experts, part, 2 * count)),
        ),
        grid=(tiles,),
        scratch_shapes=row_scratch + [pltpu.SemaphoreType.DMA((1 + 2 * experts,))],
        compiler_params=params(60),
        cost_estimate=pl.CostEstimate(
            flops=8 * count * experts * part * units,
            bytes_accessed=4 * experts * part * units,
            transcendentals=0,
        ),
        name="early",
    )(rows, other, gate_view, up_view)
    rows = after(to_experts(1), partial)
    other = exchange(rows, "fsdp", 1)

    tile_of = lambda i: jnp.minimum(i, tiles - 1)
    behind = lambda i: jnp.clip(i - 1, 0, tiles - 1)
    place_of = lambda i: jnp.maximum(i - tiles, 0)
    weight_spec = pl.BlockSpec((experts, 1, part, tile), lambda i: (0, 1, 0, tile_of(i)))
    sum_spec = pl.BlockSpec((2 * count, tile), lambda i: (0, tile_of(i)))
    unit_spec = pl.BlockSpec((planes, 2, capacity, tile), lambda i: (0, 0, 0, behind(i)))
    grad_spec = pl.BlockSpec(
        (1, columns, stretch), lambda i: (place_of(i) % experts, 0, place_of(i) // experts)
    )
    grad_shape = jax.ShapeDtypeStruct((experts, columns, units), jnp.bfloat16)
    gate_sums, up_sums, stats, turned_rows = partial
    hidden, grad_gate, grad_up = pl.pallas_call(
        functools.partial(late_kernel, float(width), tiles),
        out_shape=(
            jax.ShapeDtypeStruct((planes, 2, capacity, units), jnp.bfloat16),
            grad_shape,
            grad_shape,
        ),
        in_specs=[smem(), any_spec, any_spec, any_spec]
        + [weight_spec, weight_spec, sum_spec, sum_spec]
        + [whole(stats.shape), whole(signs.shape), unit_spec],
        out_specs=(unit_spec, grad_spec, grad_spec),
        grid=(tiles + experts * (units // stretch),),
        scratch_shapes=row_scratch
        + [
            pltpu.VMEM((2 * count, 1), jnp.float32),
            pltpu.VMEM((2 * count, 1), jnp.float32),
            pltpu.VMEM((2, 2 * count, tile), jnp.float32),
            pltpu.VMEM((2, 2 * count, tile), jnp.float32),
            pltpu.VMEM((2 * count, units), jnp.bfloat16),
            pltpu.VMEM((2 * count, units), jnp.bfloat16),
            pltpu.VMEM((experts, columns, 2 * count), jnp.bfloat16),
            pltpu.SemaphoreType.DMA((2 + 2 * experts,)),
        ],
        compiler_params=params(60),
        name="late",
    )(
        position,
        rows,
        other,
        turned_rows,
        gate_view,
        up_view,
        gate_sums,
        up_sums,
        stats,
        signs,
        cot_hidden.reshape(planes, 2, capacity, units),
    )
    return (
        merged_out,
        hidden.reshape(1, -1, units),
        grad_gate.reshape(1, width, units),
        grad_up.reshape(1, width, units),
    )


def solution(mesh):
    placed = (
        P("expert", "fsdp", None),
        P("fsdp", "expert"),
        P("fsdp", "expert"),
        P("expert"),
        P("expert", None),
        P("expert", None, "fsdp"),
        P("expert", None, "fsdp"),
        P("fsdp", None),
        P("fsdp", None),
        P("expert", None, "fsdp"),
    )
    return jax.shard_map(
        per_device,
        mesh=mesh,
        in_specs=placed,
        out_specs=(
            P("fsdp", "expert"),
            P("expert", None, "fsdp"),
            P("expert", None, "fsdp"),
            P("expert", None, "fsdp"),
        ),
        check_vma=False,
    )
```

```python
import functools

import jax
import jax.numpy as jnp
from jax import lax
from jax.experimental import pallas as pl
from jax.experimental.pallas import tpu as pltpu
from jax.sharding import PartitionSpec as P

CHUNKS = 2
MEBI = 1024 * 1024


def exchange(value, axis, offset):
    size = lax.axis_size(axis)
    return lax.ppermute(value, axis, [(i, i ^ offset) for i in range(size)])


def pick(value, index, axis):
    return lax.dynamic_index_in_dim(value, index, axis, keepdims=False)


def after(value, *others):
    return lax.optimization_barrier((value, others))[0]


def bits_of(size):
    return size.bit_length() - 1


def whole(shape):
    return pl.BlockSpec(shape, lambda *_: (0,) * len(shape))


def smem():
    return pl.BlockSpec(memory_space=pltpu.SMEM)


def params(mebi=16):
    return pltpu.CompilerParams(vmem_limit_bytes=mebi * MEBI)


def signs_kernel(experts, position_ref, ids_ref, out_ref):
    blocks, capacity, lanes = out_ref.shape
    tokens = ids_ref.shape[2]
    expert = position_ref[0]
    slots = lax.broadcasted_iota(jnp.int32, (capacity, tokens), 0)
    rows = lax.broadcasted_iota(jnp.int32, (lanes, tokens), 0)
    last = lax.broadcasted_iota(jnp.int32, (capacity, lanes), 1) == lanes - 1
    for b in range(blocks):
        ids = ids_ref[b]
        e0, e1, s0, s1 = ids[0:1], ids[1:2], ids[2:3], ids[3:4]
        hit0 = jnp.where((e0 == expert) & (s0 == slots), 1.0, 0.0)
        hit1 = jnp.where((e1 == expert) & (s1 == slots), 1.0, 0.0)
        table = jnp.where(e0 == rows - 1, 1.0, 0.0) - jnp.where(e1 == rows - 1, 1.0, 0.0)
        signs = lax.dot_general(
            (hit0 - hit1).astype(jnp.bfloat16),
            table.astype(jnp.bfloat16),
            (((1,), (1,)), ((), ())),
            preferred_element_type=jnp.float32,
        )
        filled = jnp.sum(hit0 + hit1, axis=1, keepdims=True)
        out_ref[b] = jnp.where(last, filled, signs)


def pack_kernel(position_ref, low_ref, high_ref, low_out, high_out):
    low_out[0] = low_ref[...]
    high_out[0] = high_ref[...]


def pack(position, branch, c, flip, experts):
    half = branch.shape[0] // 2
    part = branch.shape[1] // experts // CHUNKS
    others = experts // 2

    def low(j, position_ref):
        return (0, (2 * j + (position_ref[0] % 2 ^ flip)) * CHUNKS + c)

    def high(j, position_ref):
        return (1, (j + others * (position_ref[0] // others ^ flip)) * CHUNKS + c)

    block = pl.BlockSpec((1, half, part), lambda j, position_ref: (j, 0, 0))
    shape = jax.ShapeDtypeStruct((others, half, part), jnp.bfloat16)
    return pl.pallas_call(
        pack_kernel,
        out_shape=(shape, shape),
        grid_spec=pltpu.PrefetchScalarGridSpec(
            num_scalar_prefetch=1,
            grid=(others,),
            in_specs=[pl.BlockSpec((half, part), low), pl.BlockSpec((half, part), high)],
            out_specs=(block, block),
        ),
        compiler_params=params(61),
        name="pack",
    )(position, branch, branch)


def join_kernel(*refs):
    *part_refs, out_ref = refs
    part = part_refs[0].shape[1]
    for c, part_ref in enumerate(part_refs):
        out_ref[:, c * part : (c + 1) * part] = part_ref[...]


def spread_kernel(shares_ref, ids_ref, out_ref):
    experts, quarter, columns = shares_ref.shape
    blocks, _, features = out_ref.shape
    per_expert = blocks // experts
    for f in range(blocks):
        start = (f % per_expert) * features
        out_ref[f, :quarter] = shares_ref[f // per_expert, :, start : start + features]
        out_ref[f, quarter:] = ids_ref[...]


def sides_kernel(position_ref, *refs):
    *share_refs, own_ref, other_ref = refs
    for k, share_ref in enumerate(share_refs):
        place = position_ref[0] ^ k
        for side, out_ref in enumerate((own_ref, other_ref)):
            out_ref[:, place] = share_ref[:, position_ref[2] ^ side]


def dispatch_kernel(position_ref, ids_ref, extra_ref, *refs):
    *token_refs, out_ref = refs
    planes = len(token_refs)
    experts, _, part = out_ref.shape
    lanes = extra_ref.shape[0]
    count = out_ref.shape[1] - lanes
    capacity = count // planes
    tokens = ids_ref.shape[2]
    plane, core = position_ref[1], position_ref[2]
    slots = lax.broadcasted_iota(jnp.int32, (experts * capacity, tokens), 0)
    for k in range(planes):
        source = plane ^ k
        ids = ids_ref[source * 2 + core]
        code0 = ids[0:1] * capacity + ids[2:3]
        code1 = ids[1:2] * capacity + ids[3:4]
        one_hot = jnp.where((code0 == slots) | (code1 == slots), 1.0, 0.0).astype(jnp.bfloat16)
        picked = jnp.dot(one_hot, token_refs[k][...], preferred_element_type=jnp.float32)
        rows = pl.ds(pl.multiple_of(source * capacity, 16), capacity)
        out_ref[:, rows] = picked.reshape(experts, capacity, part).astype(jnp.bfloat16)
    for e in range(experts):
        out_ref[e, count:] = extra_ref[...]


def row_stats(flat_ref, side, aux_ref):
    count = flat_ref.shape[0] // 2
    experts, lanes, part = aux_ref.shape
    squares = jnp.zeros((count, part), jnp.float32)
    logits = jnp.zeros((count, lanes), jnp.float32)
    for e in range(experts):
        rows = flat_ref[side * count : (side + 1) * count, e * part : (e + 1) * part]
        aux = aux_ref[e]
        ratio = rows.astype(jnp.float32) * (1.0 / aux[0:1].astype(jnp.float32))
        squares = squares + ratio * ratio
        logits = logits + lax.dot_general(
            rows, aux, (((1,), (1,)), ((), ())), preferred_element_type=jnp.float32
        )
    total = jnp.sum(squares, axis=1, keepdims=True)
    return jnp.where(lax.broadcasted_iota(jnp.int32, logits.shape, 1) == 0, total, logits)


def row_copies(sides, flat_ref, aux_ref, sems):
    count = flat_ref.shape[0] // 2
    experts, _, part = aux_ref.shape
    copies = [
        pltpu.make_async_copy(sides[0].at[:, pl.ds(count, aux_ref.shape[1])], aux_ref, sems.at[0])
    ]
    for side, rows_ref in enumerate(sides):
        for e in range(experts):
            copies.append(
                pltpu.make_async_copy(
                    rows_ref.at[e, pl.ds(0, count)],
                    flat_ref.at[pl.ds(side * count, count), pl.ds(e * part, part)],
                    sems.at[1 + side * experts + e],
                )
            )
    return copies


def turned(flat_ref, e, part):
    return flat_ref[:, e * part : (e + 1) * part].T


def product(flat_ref, weight_ref):
    weight = weight_ref[...].reshape(flat_ref.shape[1], weight_ref.shape[3])
    return jnp.dot(flat_ref[...], weight, preferred_element_type=jnp.float32)


def shares_of(experts, tiles, t):
    return range(t * experts // tiles, (t + 1) * experts // tiles)


def early_kernel(
    tiles,
    own_ref,
    other_ref,
    gate_ref,
    up_ref,
    gate_out,
    up_out,
    stats_out,
    turned_out,
    flat_scratch,
    aux_scratch,
    sems,
):
    count = flat_scratch.shape[0] // 2
    experts, _, part = aux_scratch.shape

    for t in range(tiles):

        @pl.when(pl.program_id(0) == t)
        def _():
            if t == 0:
                copies = row_copies((own_ref, other_ref), flat_scratch, aux_scratch, sems)
                for copy in copies:
                    copy.start()
                for copy in copies:
                    copy.wait()
            gate_out[...] = product(flat_scratch, gate_ref)
            up_out[...] = product(flat_scratch, up_ref)
            for e in shares_of(experts, tiles, t):
                turned_out[e] = turned(flat_scratch, e, part)
            if t == tiles - 1:
                for side in range(2):
                    stats_out[side * count : (side + 1) * count] = row_stats(
                        flat_scratch, side, aux_scratch
                    )


def late_kernel(
    width,
    tiles,
    position_ref,
    own_ref,
    other_ref,
    turned_ref,
    gate_ref,
    up_ref,
    gate_acc,
    up_acc,
    stats_ref,
    signs_ref,
    cot_ref,
    hidden_out,
    grad_gate_out,
    grad_up_out,
    flat_scratch,
    aux_scratch,
    scale_scratch,
    weight_scratch,
    gate_scratch,
    up_scratch,
    d_gate_scratch,
    d_up_scratch,
    turned_scratch,
    sems,
):
    step = pl.program_id(0)
    core = position_ref[2]
    planes, _, capacity, tile = hidden_out.shape
    count = planes * capacity
    experts, _, part = aux_scratch.shape
    lanes = stats_ref.shape[1]
    turn_copy = pltpu.make_async_copy(
        turned_ref, turned_scratch.at[:, pl.ds(0, part)], sems.at[1 + 2 * experts]
    )

    def scales():
        for side in range(2):
            span = slice(side * count, (side + 1) * count)
            stats = stats_ref[span] + row_stats(flat_scratch, side, aux_scratch)
            inverse = lax.rsqrt(stats[:, 0:1] / width + 1e-05)
            signs = signs_ref[:, pl.ds(core ^ side, 1)].reshape(count, lanes)
            filled = signs[:, lanes - 1 :]
            column = lax.broadcasted_iota(jnp.int32, stats.shape, 1)
            router = (column >= 1) & (column <= experts)
            margin = jnp.sum(jnp.where(router, stats * signs, 0.0), axis=1, keepdims=True)
            prob = jax.nn.sigmoid(margin * inverse).astype(jnp.bfloat16).astype(jnp.float32)
            scale_scratch[span] = inverse
            weight_scratch[span] = jnp.where(filled > 0.0, prob, 0.0)

    def units_of(t):
        for side in range(2):
            span = slice(side * count, (side + 1) * count)
            inverse = scale_scratch[span]
            weight = weight_scratch[span]
            gate_pre = inverse * gate_scratch[t % 2, span]
            up_pre = inverse * up_scratch[t % 2, span]
            sig_gate = jax.nn.sigmoid(gate_pre)
            act_gate = gate_pre * sig_gate
            hidden = (weight * act_gate * up_pre).astype(jnp.bfloat16)
            hidden_out[:, pl.ds(core ^ side, 1)] = hidden.reshape(planes, 1, capacity, tile)
            cot = cot_ref[:, pl.ds(core ^ side, 1)].reshape(count, tile)
            d_pre = cot.astype(jnp.float32) * (weight * inverse)
            d_gate = d_pre * up_pre * sig_gate * (1.0 + gate_pre * (1.0 - sig_gate))
            columns = slice(t * tile, (t + 1) * tile)
            d_gate_scratch[span, columns] = d_gate.astype(jnp.bfloat16)
            d_up_scratch[span, columns] = (d_pre * act_gate).astype(jnp.bfloat16)

    def gradients(stretch):
        e = (step - tiles) % experts
        stretch_units = grad_gate_out.shape[2]
        span = slice(stretch * stretch_units, (stretch + 1) * stretch_units)
        for scratch, out in ((d_gate_scratch, grad_gate_out), (d_up_scratch, grad_up_out)):
            out[0] = jnp.dot(
                turned_scratch[e], scratch[:, span], preferred_element_type=jnp.float32
            ).astype(jnp.bfloat16)

    for t in range(tiles):

        @pl.when(step == t)
        def _():
            if t == 0:
                copies = row_copies((own_ref, other_ref), flat_scratch, aux_scratch, sems)
                for copy in copies:
                    copy.start()
                turn_copy.start()
                for copy in copies:
                    copy.wait()
            gate_scratch[t % 2] = gate_acc[...] + product(flat_scratch, gate_ref)
            up_scratch[t % 2] = up_acc[...] + product(flat_scratch, up_ref)
            for e in shares_of(experts, tiles, t):
                turned_scratch[e, part:] = turned(flat_scratch, e, part)
            if t == 0:
                scales()
            else:
                units_of(t - 1)

    @pl.when(step == tiles)
    def _():
        turn_copy.wait()
        units_of(tiles - 1)
        gradients(0)

    for stretch in range(tiles * tile // grad_gate_out.shape[2]):
        first = tiles + stretch * experts

        @pl.when((step >= first) & (step < first + experts) & (step > tiles))
        def _():
            gradients(stretch)


def per_device(
    branch_wo,
    context,
    residual,
    norm_gain,
    router_w,
    gate_w,
    up_w,
    expert_ids,
    slot_ids,
    cot_hidden,
):
    experts = lax.axis_size("expert")
    blocks = lax.axis_size("fsdp")
    planes = blocks // 2
    expert = lax.axis_index("expert")
    block = lax.axis_index("fsdp")
    plane, core = block // 2, block % 2
    tokens, columns = context.shape
    width = columns * experts
    features = width // blocks
    capacity = cot_hidden.shape[1] // blocks
    units = cot_hidden.shape[2]
    part = columns // CHUNKS
    quarter = tokens // experts
    count = planes * capacity
    position = jnp.stack([expert, plane, core]).astype(jnp.int32)
    bits = bits_of(experts)

    lanes = experts + 2 + (-(experts + 2)) % 16
    extra = jnp.concatenate([norm_gain[None], router_w.T])
    extra = jnp.pad(extra, ((0, lanes - extra.shape[0]), (0, 0)))
    ids = jnp.concatenate([expert_ids, slot_ids], axis=1).T.astype(jnp.bfloat16)
    id_rows = ids.size // features
    ids = jnp.pad(ids.reshape(id_rows, features), ((0, -id_rows % 16), (0, 0)))

    branch = branch_wo[0]
    weights = [1 << (bits - 1 - i) for i in range(bits)]
    own_bits = [(expert // weight) % 2 for weight in weights]

    def start_sum(kept, first):
        def value(chosen):
            place = 0
            for i in range(bits):
                place = place if i == first else 2 * place + chosen[i]
            return pick(kept, place, 0).astype(jnp.float32)

        return value

    def joined(value, got, axis, rest):
        def total(chosen):
            chosen = [own_bits[axis] if i == axis else bit for i, bit in enumerate(chosen)]
            place = 0
            for i in rest:
                place = 2 * place + chosen[i]
            return value(chosen) + pick(got, place, 0).astype(jnp.float32)

        return total

    orders = (list(range(bits))[::-1], list(range(bits)))
    held = {}

    def keep(c, position):
        for h, kept in enumerate(pack(position, branch, c, 0, experts)):
            held[c, h] = start_sum(kept, orders[h][0])

    def branch_sends(phase, c):
        if phase == 0:
            return pack(position, branch, c, 1, experts)
        sends = []
        for h, order in enumerate(orders):
            rest = sorted(order[phase + 1 :])
            stacked = []
            for code in range(1 << len(rest)):
                chosen = list(own_bits)
                chosen[order[phase]] = 1 - own_bits[order[phase]]
                for at, i in enumerate(rest):
                    chosen[i] = (code >> (len(rest) - 1 - at)) & 1
                stacked.append(held[c, h](chosen).astype(jnp.bfloat16))
            sends.append(stacked[0][None] if len(stacked) == 1 else jnp.stack(stacked))
        return tuple(sends)

    def branch_exchange(phase, sends):
        return tuple(
            exchange(sends[h], "expert", weights[order[phase]]) for h, order in enumerate(orders)
        )

    def branch_add(phase, c, got):
        for h, order in enumerate(orders):
            held[c, h] = joined(held[c, h], got[h], order[phase], sorted(order[phase + 1 :]))

    def merged_of(c):
        total = jnp.concatenate([held[c, 0](own_bits), held[c, 1](own_bits)])
        return (total / experts).astype(jnp.bfloat16)

    shares = lax.all_to_all(
        context.reshape(experts, quarter, columns), "expert", split_axis=0, concat_axis=0, tiled=True
    )

    spread_shape = (blocks, quarter + ids.shape[0], features)
    to_blocks = pl.pallas_call(
        spread_kernel,
        out_shape=jax.ShapeDtypeStruct(spread_shape, jnp.bfloat16),
        in_specs=[whole(shares.shape), whole(ids.shape)],
        out_specs=whole(spread_shape),
        grid=(1,),
        compiler_params=params(),
        name="spread",
    )(shares, ids)
    got = branch_exchange(0, pack(after(position, shares), branch, 0, 1, experts))
    keep(0, after(position, to_blocks))
    branch_add(0, 0, after(got, to_blocks))
    from_blocks = lax.all_to_all(to_blocks, "fsdp", split_axis=0, concat_axis=0, tiled=True)
    for phase in range(1, bits):
        got = branch_exchange(phase, branch_sends(phase, 0))
        if phase == bits - 1:
            from_blocks, got = lax.optimization_barrier((from_blocks, got))
        branch_add(phase, 0, got)

    ids_all = from_blocks[:, quarter : quarter + id_rows].astype(jnp.int32)
    ids_all = ids_all.reshape(blocks, 4, tokens)
    own_share = from_blocks[:, :quarter]
    packed1 = branch_sends(0, 1)
    keep(1, after(position, packed1))
    pieces = [exchange(own_share, "expert", k) if k else own_share for k in range(experts)]
    pieces, packed1 = lax.optimization_barrier((pieces, packed1))
    signs = pl.pallas_call(
        functools.partial(signs_kernel, experts),
        out_shape=jax.ShapeDtypeStruct((blocks, capacity, lanes), jnp.float32),
        in_specs=[smem(), whole(ids_all.shape)],
        out_specs=whole((blocks, capacity, lanes)),
        grid=(1,),
        compiler_params=params(),
        name="signs",
    )(position, ids_all).reshape(planes, 2, capacity, lanes)

    gate_view = gate_w.reshape(experts, CHUNKS, part, units)
    up_view = up_w.reshape(experts, CHUNKS, part, units)
    tile = min(256, units)
    stretch = min(512, units)
    tiles = units // tile
    pieces, signs = lax.optimization_barrier((pieces, signs))
    side_shape = (planes, experts, quarter, features)
    sides = pl.pallas_call(
        sides_kernel,
        out_shape=(jax.ShapeDtypeStruct(side_shape, jnp.bfloat16),) * 2,
        in_specs=[smem()] + [whole((planes, 2, quarter, features))] * experts,
        out_specs=(whole(side_shape),) * 2,
        grid=(1,),
        compiler_params=params(),
        name="sides",
    )(position, *[piece.reshape(planes, 2, quarter, features) for piece in pieces])
    sides = [side.reshape(planes * tokens, features) for side in sides]
    def pair_of(merged):
        def attend(rows):
            out = jnp.dot(rows, merged, preferred_element_type=jnp.float32)
            return out.reshape(planes, tokens, part)

        swapped = exchange(attend(sides[1]).astype(jnp.bfloat16), "fsdp", 1)
        return attend(sides[0]) + swapped.astype(jnp.float32)

    def plane_sends(pair):
        return [pick(pair, plane ^ k, 0).astype(jnp.bfloat16) for k in range(1, planes)]

    def plane_exchange(sends):
        return [exchange(send, "fsdp", 2 * k) for k, send in enumerate(sends, 1)]

    def scaled_of(c, pair, arrived):
        span = slice(c * part, (c + 1) * part)
        hstate = residual[:, span].astype(jnp.float32) + pick(pair, plane, 0)
        for value in arrived:
            hstate = hstate + value.astype(jnp.float32)
        return (hstate * norm_gain[span].astype(jnp.float32)).astype(jnp.bfloat16)

    height = count + lanes

    def slots_of(c, own_tokens):
        return pl.pallas_call(
            dispatch_kernel,
            out_shape=jax.ShapeDtypeStruct((experts, height, part), jnp.bfloat16),
            in_specs=[smem(), whole(ids_all.shape)]
            + [pl.BlockSpec((lanes, part), lambda i, c=c: (0, c))]
            + [whole((tokens, part))] * planes,
            out_specs=whole((experts, height, part)),
            grid=(1,),
            compiler_params=params(),
            name="dispatch",
        )(position, ids_all, extra, *own_tokens)

    merged0 = merged_of(0)
    got = branch_exchange(0, packed1)
    pair0 = pair_of(merged0)
    sends0 = plane_sends(pair0)
    branch_add(0, 1, after(got, sends0))
    arrived0 = plane_exchange(sends0)
    for phase in range(1, bits):
        got = branch_exchange(phase, branch_sends(phase, 1))
        if phase < bits - 1:
            branch_add(phase, 1, got)

    scaled0 = scaled_of(0, pair0, arrived0)
    tokens0 = [scaled0] + plane_exchange([scaled0] * (planes - 1))
    if bits > 1:
        branch_add(bits - 1, 1, after(got, scaled0))
    merged1 = merged_of(1)
    merged_out = pl.pallas_call(
        join_kernel,
        out_shape=jax.ShapeDtypeStruct((features, columns), jnp.bfloat16),
        in_specs=[whole((features, part))] * CHUNKS,
        out_specs=whole((features, columns)),
        grid=(1,),
        compiler_params=params(),
        name="join",
    )(merged0, merged1)
    pair1 = pair_of(merged1)
    sends1 = after(plane_sends(pair1), tokens0)
    arrived1 = plane_exchange(sends1)

    scaled1 = scaled_of(1, pair1, after(arrived1, merged_out))
    slots0 = slots_of(0, after(tokens0, scaled1))
    tokens1 = [scaled1] + plane_exchange([scaled1] * (planes - 1))
    slots1 = slots_of(1, tokens1)
    slots = (slots0, slots1)

    def to_experts(c):
        return lax.all_to_all(slots[c], "expert", split_axis=0, concat_axis=0, tiled=True)

    rows = after(to_experts(0), slots[-1], merged_out, signs)
    other = exchange(rows, "fsdp", 1)
    weight_spec = pl.BlockSpec((experts, 1, part, tile), lambda n: (0, 0, 0, n))
    sums = jax.ShapeDtypeStruct((2 * count, units), jnp.float32)
    sum_spec = pl.BlockSpec((2 * count, tile), lambda n: (0, n))
    any_spec = pl.BlockSpec(memory_space=pl.ANY)
    row_scratch = [
        pltpu.VMEM((2 * count, experts * part), jnp.bfloat16),
        pltpu.VMEM((experts, lanes, part), jnp.bfloat16),
    ]
    partial = pl.pallas_call(
        functools.partial(early_kernel, tiles),
        out_shape=(
            sums,
            sums,
            jax.ShapeDtypeStruct((2 * count, lanes), jnp.float32),
            jax.ShapeDtypeStruct((experts, part, 2 * count), jnp.bfloat16),
        ),
        in_specs=[any_spec, any_spec, weight_spec, weight_spec],
        out_specs=(
            sum_spec,
            sum_spec,
            whole((2 * count, lanes)),
            whole((experts, part, 2 * count)),
        ),
        grid=(tiles,),
        scratch_shapes=row_scratch + [pltpu.SemaphoreType.DMA((1 + 2 * experts,))],
        compiler_params=params(60),
        cost_estimate=pl.CostEstimate(
            flops=8 * count * experts * part * units,
            bytes_accessed=4 * experts * part * units,
            transcendentals=0,
        ),
        name="early",
    )(rows, other, gate_view, up_view)
    rows = after(to_experts(1), partial)
    other = exchange(rows, "fsdp", 1)

    tile_of = lambda i: jnp.minimum(i, tiles - 1)
    behind = lambda i: jnp.clip(i - 1, 0, tiles - 1)
    place_of = lambda i: jnp.maximum(i - tiles, 0)
    weight_spec = pl.BlockSpec((experts, 1, part, tile), lambda i: (0, 1, 0, tile_of(i)))
    sum_spec = pl.BlockSpec((2 * count, tile), lambda i: (0, tile_of(i)))
    unit_spec = pl.BlockSpec((planes, 2, capacity, tile), lambda i: (0, 0, 0, behind(i)))
    grad_spec = pl.BlockSpec(
        (1, columns, stretch), lambda i: (place_of(i) % experts, 0, place_of(i) // experts)
    )
    grad_shape = jax.ShapeDtypeStruct((experts, columns, units), jnp.bfloat16)
    gate_sums, up_sums, stats, turned_rows = partial
    hidden, grad_gate, grad_up = pl.pallas_call(
        functools.partial(late_kernel, float(width), tiles),
        out_shape=(
            jax.ShapeDtypeStruct((planes, 2, capacity, units), jnp.bfloat16),
            grad_shape,
            grad_shape,
        ),
        in_specs=[smem(), any_spec, any_spec, any_spec]
        + [weight_spec, weight_spec, sum_spec, sum_spec]
        + [whole(stats.shape), whole(signs.shape), unit_spec],
        out_specs=(unit_spec, grad_spec, grad_spec),
        grid=(tiles + experts * (units // stretch),),
        scratch_shapes=row_scratch
        + [
            pltpu.VMEM((2 * count, 1), jnp.float32),
            pltpu.VMEM((2 * count, 1), jnp.float32),
            pltpu.VMEM((2, 2 * count, tile), jnp.float32),
            pltpu.VMEM((2, 2 * count, tile), jnp.float32),
            pltpu.VMEM((2 * count, units), jnp.bfloat16),
            pltpu.VMEM((2 * count, units), jnp.bfloat16),
            pltpu.VMEM((experts, columns, 2 * count), jnp.bfloat16),
            pltpu.SemaphoreType.DMA((2 + 2 * experts,)),
        ],
        compiler_params=params(60),
        name="late",
    )(
        position,
        rows,
        other,
        turned_rows,
        gate_view,
        up_view,
        gate_sums,
        up_sums,
        stats,
        signs,
        cot_hidden.reshape(planes, 2, capacity, units),
    )
    return (
        merged_out,
        hidden.reshape(1, -1, units),
        grad_gate.reshape(1, width, units),
        grad_up.reshape(1, width, units),
    )


def solution(mesh):
    placed = (
        P("expert", "fsdp", None),
        P("fsdp", "expert"),
        P("fsdp", "expert"),
        P("expert"),
        P("expert", None),
        P("expert", None, "fsdp"),
        P("expert", None, "fsdp"),
        P("fsdp", None),
        P("fsdp", None),
        P("expert", None, "fsdp"),
    )
    return jax.shard_map(
        per_device,
        mesh=mesh,
        in_specs=placed,
        out_specs=(
            P("fsdp", "expert"),
            P("expert", None, "fsdp"),
            P("expert", None, "fsdp"),
            P("expert", None, "fsdp"),
        ),
        check_vma=False,
    )
```

```python
import functools

import jax
import jax.numpy as jnp
from jax import lax
from jax.experimental import pallas as pl
from jax.experimental.pallas import tpu as pltpu
from jax.sharding import PartitionSpec as P

CHUNKS = 2
MEBI = 1024 * 1024


def exchange(value, axis, offset):
    size = lax.axis_size(axis)
    return lax.ppermute(value, axis, [(i, i ^ offset) for i in range(size)])


def pick(value, index, axis):
    return lax.dynamic_index_in_dim(value, index, axis, keepdims=False)


def after(value, *others):
    return lax.optimization_barrier((value, others))[0]


def bits_of(size):
    return size.bit_length() - 1


def whole(shape):
    return pl.BlockSpec(shape, lambda *_: (0,) * len(shape))


def smem():
    return pl.BlockSpec(memory_space=pltpu.SMEM)


def params(mebi=16):
    return pltpu.CompilerParams(vmem_limit_bytes=mebi * MEBI)


def signs_kernel(experts, position_ref, ids_ref, out_ref):
    blocks, capacity, lanes = out_ref.shape
    tokens = ids_ref.shape[2]
    expert = position_ref[0]
    slots = lax.broadcasted_iota(jnp.int32, (capacity, tokens), 0)
    rows = lax.broadcasted_iota(jnp.int32, (lanes, tokens), 0)
    last = lax.broadcasted_iota(jnp.int32, (capacity, lanes), 1) == lanes - 1
    for b in range(blocks):
        ids = ids_ref[b]
        e0, e1, s0, s1 = ids[0:1], ids[1:2], ids[2:3], ids[3:4]
        hit0 = jnp.where((e0 == expert) & (s0 == slots), 1.0, 0.0)
        hit1 = jnp.where((e1 == expert) & (s1 == slots), 1.0, 0.0)
        table = jnp.where(e0 == rows - 1, 1.0, 0.0) - jnp.where(e1 == rows - 1, 1.0, 0.0)
        signs = lax.dot_general(
            (hit0 - hit1).astype(jnp.bfloat16),
            table.astype(jnp.bfloat16),
            (((1,), (1,)), ((), ())),
            preferred_element_type=jnp.float32,
        )
        filled = jnp.sum(hit0 + hit1, axis=1, keepdims=True)
        out_ref[b] = jnp.where(last, filled, signs)


def pack_kernel(position_ref, low_ref, high_ref, low_out, high_out):
    low_out[0] = low_ref[...]
    high_out[0] = high_ref[...]


def pack(position, branch, c, experts):
    half = branch.shape[0] // 2
    part = branch.shape[1] // experts // CHUNKS
    others = experts // 2

    def low(j, position_ref):
        return (0, (2 * j + 1 - position_ref[0] % 2) * CHUNKS + c)

    def high(j, position_ref):
        return (1, (j + others * (1 - position_ref[0] // others)) * CHUNKS + c)

    block = pl.BlockSpec((1, half, part), lambda j, position_ref: (j, 0, 0))
    shape = jax.ShapeDtypeStruct((others, half, part), jnp.bfloat16)
    return pl.pallas_call(
        pack_kernel,
        out_shape=(shape, shape),
        grid_spec=pltpu.PrefetchScalarGridSpec(
            num_scalar_prefetch=1,
            grid=(others,),
            in_specs=[pl.BlockSpec((half, part), low), pl.BlockSpec((half, part), high)],
            out_specs=(block, block),
        ),
        compiler_params=params(),
        name="pack",
    )(position, branch, branch)


def join_kernel(*refs):
    *part_refs, out_ref = refs
    part = part_refs[0].shape[1]
    for c, part_ref in enumerate(part_refs):
        out_ref[:, c * part : (c + 1) * part] = part_ref[...]


def spread_kernel(shares_ref, ids_ref, out_ref):
    experts, quarter, columns = shares_ref.shape
    blocks, _, features = out_ref.shape
    per_expert = blocks // experts
    for f in range(blocks):
        start = (f % per_expert) * features
        out_ref[f, :quarter] = shares_ref[f // per_expert, :, start : start + features]
        out_ref[f, quarter:] = ids_ref[...]


def sides_kernel(position_ref, *refs):
    *share_refs, own_ref, other_ref = refs
    for k, share_ref in enumerate(share_refs):
        place = position_ref[0] ^ k
        for side, out_ref in enumerate((own_ref, other_ref)):
            out_ref[:, place] = share_ref[:, position_ref[2] ^ side]


def dispatch_kernel(offsets, position_ref, ids_ref, extra_ref, *refs):
    *token_refs, out_ref = refs
    planes = len(offsets)
    experts, _, part = out_ref.shape
    lanes = extra_ref.shape[0]
    count = out_ref.shape[1] - lanes
    capacity = count // planes
    tokens = ids_ref.shape[2]
    plane, core = position_ref[1], position_ref[2]
    slots = lax.broadcasted_iota(jnp.int32, (experts * capacity, tokens), 0)
    for k, token_ref in zip(offsets, token_refs):
        source = plane ^ k
        ids = ids_ref[source * 2 + core]
        code0 = ids[0:1] * capacity + ids[2:3]
        code1 = ids[1:2] * capacity + ids[3:4]
        one_hot = jnp.where((code0 == slots) | (code1 == slots), 1.0, 0.0).astype(jnp.bfloat16)
        picked = jnp.dot(one_hot, token_ref[...], preferred_element_type=jnp.float32)
        rows = pl.ds(pl.multiple_of(source % planes * capacity, 16), capacity)
        out_ref[:, rows] = picked.reshape(experts, capacity, part).astype(jnp.bfloat16)
    for e in range(experts):
        out_ref[e, count:] = extra_ref[...]


def row_stats(flat_ref, group, groups, aux_ref):
    count = flat_ref.shape[0] // groups
    experts, lanes, part = aux_ref.shape
    squares = jnp.zeros((count, part), jnp.float32)
    logits = jnp.zeros((count, lanes), jnp.float32)
    for e in range(experts):
        rows = flat_ref[group * count : (group + 1) * count, e * part : (e + 1) * part]
        aux = aux_ref[e]
        ratio = rows.astype(jnp.float32) * (1.0 / aux[0:1].astype(jnp.float32))
        squares = squares + ratio * ratio
        logits = logits + lax.dot_general(
            rows, aux, (((1,), (1,)), ((), ())), preferred_element_type=jnp.float32
        )
    total = jnp.sum(squares, axis=1, keepdims=True)
    return jnp.where(lax.broadcasted_iota(jnp.int32, logits.shape, 1) == 0, total, logits)


def row_copies(sides, halves, flat_ref, aux_ref, sems):
    count = flat_ref.shape[0] // (2 * halves)
    experts, lanes, part = aux_ref.shape
    copies = [
        pltpu.make_async_copy(sides[0].at[:, pl.ds(halves * count, lanes)], aux_ref, sems.at[0])
    ]
    for half in range(halves):
        for side, rows_ref in enumerate(sides):
            for e in range(experts):
                group = half * 2 + side
                copies.append(
                    pltpu.make_async_copy(
                        rows_ref.at[e, pl.ds(half * count, count)],
                        flat_ref.at[pl.ds(group * count, count), pl.ds(e * part, part)],
                        sems.at[1 + group * experts + e],
                    )
                )
    return copies


def turned(flat_ref, half, halves, e, part):
    count = flat_ref.shape[0] // halves
    return flat_ref[half * count : (half + 1) * count, e * part : (e + 1) * part].T


def product(flat_ref, weight_ref):
    weight = weight_ref[...].reshape(flat_ref.shape[1], weight_ref.shape[3])
    return jnp.dot(flat_ref[...], weight, preferred_element_type=jnp.float32)


def shares_of(experts, tiles, t):
    return range(t * experts // tiles, (t + 1) * experts // tiles)


def early_kernel(
    tiles,
    own_ref,
    other_ref,
    gate_ref,
    up_ref,
    gate_out,
    up_out,
    stats_out,
    turned_out,
    flat_scratch,
    aux_scratch,
    sems,
):
    count = flat_scratch.shape[0] // 4
    experts, _, part = aux_scratch.shape

    for t in range(tiles):

        @pl.when(pl.program_id(0) == t)
        def _():
            if t == 0:
                copies = row_copies((own_ref, other_ref), 2, flat_scratch, aux_scratch, sems)
                for copy in copies:
                    copy.start()
                for copy in copies:
                    copy.wait()
            gate_out[...] = product(flat_scratch, gate_ref)
            up_out[...] = product(flat_scratch, up_ref)
            for e in shares_of(experts, tiles, t):
                for half in range(2):
                    turned_out[half, e] = turned(flat_scratch, half, 2, e, part)
            if t == tiles - 1:
                for group in range(4):
                    stats_out[group * count : (group + 1) * count] = row_stats(
                        flat_scratch, group, 4, aux_scratch
                    )


def late_kernel(
    width,
    tiles,
    which,
    position_ref,
    own_ref,
    other_ref,
    turned_ref,
    gate_ref,
    up_ref,
    gate_acc,
    up_acc,
    stats_ref,
    signs_ref,
    cot_ref,
    *refs,
):
    (
        hidden_out,
        grad_gate_out,
        grad_up_out,
        flat_scratch,
        aux_scratch,
        scale_scratch,
        weight_scratch,
        gate_scratch,
        up_scratch,
        d_gate_scratch,
        d_up_scratch,
        turned_scratch,
        sems,
    ) = refs[-13:]
    earlier = refs[1:3] if which else (None, None)
    step = pl.program_id(0)
    core = position_ref[2]
    planes, _, capacity, tile = hidden_out.shape
    count = planes * capacity
    experts, _, part = aux_scratch.shape
    lanes = stats_ref.shape[1]
    half = position_ref[1] // planes ^ which
    turn_copy = pltpu.make_async_copy(
        turned_ref.at[half], turned_scratch.at[:, pl.ds(0, part)], sems.at[1 + 2 * experts]
    )

    def scales():
        for side in range(2):
            span = slice(side * count, (side + 1) * count)
            stats = stats_ref[span] + row_stats(flat_scratch, side, 2, aux_scratch)
            inverse = lax.rsqrt(stats[:, 0:1] / width + 1e-05)
            signs = signs_ref[:, pl.ds(core ^ side, 1)].reshape(count, lanes)
            filled = signs[:, lanes - 1 :]
            column = lax.broadcasted_iota(jnp.int32, stats.shape, 1)
            router = (column >= 1) & (column <= experts)
            margin = jnp.sum(jnp.where(router, stats * signs, 0.0), axis=1, keepdims=True)
            prob = jax.nn.sigmoid(margin * inverse).astype(jnp.bfloat16).astype(jnp.float32)
            scale_scratch[span] = inverse
            weight_scratch[span] = jnp.where(filled > 0.0, prob, 0.0)

    def units_of(t):
        for side in range(2):
            span = slice(side * count, (side + 1) * count)
            inverse = scale_scratch[span]
            weight = weight_scratch[span]
            gate_pre = inverse * gate_scratch[t % 2, span]
            up_pre = inverse * up_scratch[t % 2, span]
            sig_gate = jax.nn.sigmoid(gate_pre)
            act_gate = gate_pre * sig_gate
            hidden = (weight * act_gate * up_pre).astype(jnp.bfloat16)
            hidden_out[:, pl.ds(core ^ side, 1)] = hidden.reshape(planes, 1, capacity, tile)
            cot = cot_ref[:, pl.ds(core ^ side, 1)].reshape(count, tile)
            d_pre = cot.astype(jnp.float32) * (weight * inverse)
            d_gate = d_pre * up_pre * sig_gate * (1.0 + gate_pre * (1.0 - sig_gate))
            columns = slice(t * tile, (t + 1) * tile)
            d_gate_scratch[span, columns] = d_gate.astype(jnp.bfloat16)
            d_up_scratch[span, columns] = (d_pre * act_gate).astype(jnp.bfloat16)

    def gradients(stretch):
        e = (step - tiles) % experts
        stretch_units = grad_gate_out.shape[2]
        span = slice(stretch * stretch_units, (stretch + 1) * stretch_units)
        for scratch, before, out in zip(
            (d_gate_scratch, d_up_scratch), earlier, (grad_gate_out, grad_up_out)
        ):
            total = jnp.dot(
                turned_scratch[e], scratch[:, span], preferred_element_type=jnp.float32
            )
            if before is not None:
                total = total + before[0].astype(jnp.float32)
            out[0] = total.astype(jnp.bfloat16)

    for t in range(tiles):

        @pl.when(step == t)
        def _():
            if t == 0:
                copies = row_copies((own_ref, other_ref), 1, flat_scratch, aux_scratch, sems)
                for copy in copies:
                    copy.start()
                turn_copy.start()
                for copy in copies:
                    copy.wait()
            gate_scratch[t % 2] = gate_acc[...] + product(flat_scratch, gate_ref)
            up_scratch[t % 2] = up_acc[...] + product(flat_scratch, up_ref)
            for e in shares_of(experts, tiles, t):
                turned_scratch[e, part:] = turned(flat_scratch, 0, 1, e, part)
            if t == 0:
                scales()
            else:
                units_of(t - 1)

    @pl.when(step == tiles)
    def _():
        turn_copy.wait()
        units_of(tiles - 1)
        gradients(0)

    for stretch in range(tiles * tile // grad_gate_out.shape[2]):
        first = tiles + stretch * experts

        @pl.when((step >= first) & (step < first + experts) & (step > tiles))
        def _():
            gradients(stretch)


def per_device(
    branch_wo,
    context,
    residual,
    norm_gain,
    router_w,
    gate_w,
    up_w,
    expert_ids,
    slot_ids,
    cot_hidden,
):
    experts = lax.axis_size("expert")
    blocks = lax.axis_size("fsdp")
    planes = blocks // 2
    expert = lax.axis_index("expert")
    block = lax.axis_index("fsdp")
    plane, core = block // 2, block % 2
    tokens, columns = context.shape
    width = columns * experts
    features = width // blocks
    capacity = cot_hidden.shape[1] // blocks
    units = cot_hidden.shape[2]
    part = columns // CHUNKS
    quarter = tokens // experts
    count = planes * capacity
    position = jnp.stack([expert, plane, core]).astype(jnp.int32)
    bits = bits_of(experts)

    lanes = experts + 2 + (-(experts + 2)) % 16
    extra = jnp.concatenate([norm_gain[None], router_w.T])
    extra = jnp.pad(extra, ((0, lanes - extra.shape[0]), (0, 0)))
    ids = jnp.concatenate([expert_ids, slot_ids], axis=1).T.astype(jnp.bfloat16)
    id_rows = ids.size // features
    ids = jnp.pad(ids.reshape(id_rows, features), ((0, -id_rows % 16), (0, 0)))

    branch = branch_wo[0]
    half = branch.shape[0] // 2
    weights = [1 << (bits - 1 - i) for i in range(bits)]
    own_bits = [(expert // weight) % 2 for weight in weights]

    def start_sum(c, h):
        def value(chosen):
            place = sum(weight * bit for weight, bit in zip(weights, chosen))
            corner = (h * half, (place * CHUNKS + c) * part)
            return lax.dynamic_slice(branch, corner, (half, part)).astype(jnp.float32)

        return value

    def joined(value, got, axis, rest):
        def total(chosen):
            chosen = [own_bits[axis] if i == axis else bit for i, bit in enumerate(chosen)]
            place = 0
            for i in rest:
                place = 2 * place + chosen[i]
            return value(chosen) + pick(got, place, 0).astype(jnp.float32)

        return total

    held = {(c, h): start_sum(c, h) for c in range(CHUNKS) for h in range(2)}
    orders = (list(range(bits))[::-1], list(range(bits)))

    def branch_sends(phase, c):
        if phase == 0:
            return pack(position, branch, c, experts)
        sends = []
        for h, order in enumerate(orders):
            rest = sorted(order[phase + 1 :])
            stacked = []
            for code in range(1 << len(rest)):
                chosen = list(own_bits)
                chosen[order[phase]] = 1 - own_bits[order[phase]]
                for at, i in enumerate(rest):
                    chosen[i] = (code >> (len(rest) - 1 - at)) & 1
                stacked.append(held[c, h](chosen).astype(jnp.bfloat16))
            sends.append(stacked[0][None] if len(stacked) == 1 else jnp.stack(stacked))
        return tuple(sends)

    def branch_exchange(phase, sends):
        return tuple(
            exchange(sends[h], "expert", weights[order[phase]]) for h, order in enumerate(orders)
        )

    def branch_add(phase, c, got):
        for h, order in enumerate(orders):
            held[c, h] = joined(held[c, h], got[h], order[phase], sorted(order[phase + 1 :]))

    def merged_of(c):
        total = jnp.concatenate([held[c, 0](own_bits), held[c, 1](own_bits)])
        return (total / experts).astype(jnp.bfloat16)

    shares = lax.all_to_all(
        context.reshape(experts, quarter, columns), "expert", split_axis=0, concat_axis=0, tiled=True
    )

    spread_shape = (blocks, quarter + ids.shape[0], features)
    to_blocks = pl.pallas_call(
        spread_kernel,
        out_shape=jax.ShapeDtypeStruct(spread_shape, jnp.bfloat16),
        in_specs=[whole(shares.shape), whole(ids.shape)],
        out_specs=whole(spread_shape),
        grid=(1,),
        compiler_params=params(),
        name="spread",
    )(shares, ids)
    got = branch_exchange(0, pack(after(position, shares), branch, 0, experts))
    branch_add(0, 0, after(got, to_blocks))
    from_blocks = lax.all_to_all(to_blocks, "fsdp", split_axis=0, concat_axis=0, tiled=True)
    for phase in range(1, bits):
        got = branch_exchange(phase, branch_sends(phase, 0))
        if phase == bits - 1:
            from_blocks, got = lax.optimization_barrier((from_blocks, got))
        branch_add(phase, 0, got)

    ids_all = from_blocks[:, quarter : quarter + id_rows].astype(jnp.int32)
    ids_all = ids_all.reshape(blocks, 4, tokens)
    own_share = from_blocks[:, :quarter]
    packed1 = branch_sends(0, 1)
    pieces = [exchange(own_share, "expert", k) if k else own_share for k in range(experts)]
    pieces, packed1 = lax.optimization_barrier((pieces, packed1))
    side_shape = (planes, experts, quarter, features)
    sides = pl.pallas_call(
        sides_kernel,
        out_shape=(jax.ShapeDtypeStruct(side_shape, jnp.bfloat16),) * 2,
        in_specs=[smem()] + [whole((planes, 2, quarter, features))] * experts,
        out_specs=(whole(side_shape),) * 2,
        grid=(1,),
        compiler_params=params(),
        name="sides",
    )(position, *[piece.reshape(planes, 2, quarter, features) for piece in pieces])
    sides = [side.reshape(planes * tokens, features) for side in sides]
    signs = pl.pallas_call(
        functools.partial(signs_kernel, experts),
        out_shape=jax.ShapeDtypeStruct((blocks, capacity, lanes), jnp.float32),
        in_specs=[smem(), whole(ids_all.shape)],
        out_specs=whole((blocks, capacity, lanes)),
        grid=(1,),
        compiler_params=params(),
        name="signs",
    )(position, ids_all).reshape(planes, 2, capacity, lanes)

    gate_view = gate_w.reshape(experts, CHUNKS, part, units)
    up_view = up_w.reshape(experts, CHUNKS, part, units)
    tile = min(256, units)
    stretch = min(512, units)
    tiles = units // tile
    def pair_of(merged):
        def attend(rows):
            out = jnp.dot(rows, merged, preferred_element_type=jnp.float32)
            return out.reshape(planes, tokens, part)

        swapped = exchange(attend(sides[1]).astype(jnp.bfloat16), "fsdp", 1)
        return attend(sides[0]) + swapped.astype(jnp.float32)

    def plane_sends(pair):
        return [pick(pair, plane ^ k, 0).astype(jnp.bfloat16) for k in range(1, planes)]

    def plane_exchange(sends):
        return [exchange(send, "fsdp", 2 * k) for k, send in enumerate(sends, 1)]

    def scaled_of(c, pair, arrived):
        span = slice(c * part, (c + 1) * part)
        hstate = residual[:, span].astype(jnp.float32) + pick(pair, plane, 0)
        for value in arrived:
            hstate = hstate + value.astype(jnp.float32)
        return (hstate * norm_gain[span].astype(jnp.float32)).astype(jnp.bfloat16)

    def slots_of(c, own_tokens, offsets):
        height = len(offsets) * capacity + lanes
        return pl.pallas_call(
            functools.partial(dispatch_kernel, tuple(offsets)),
            out_shape=jax.ShapeDtypeStruct((experts, height, part), jnp.bfloat16),
            in_specs=[smem(), whole(ids_all.shape)]
            + [pl.BlockSpec((lanes, part), lambda i, c=c: (0, c))]
            + [whole((tokens, part))] * len(offsets),
            out_specs=whole((experts, height, part)),
            grid=(1,),
            compiler_params=params(),
            name="dispatch",
        )(position, ids_all, extra, *[own_tokens[k] for k in offsets])

    merged0 = merged_of(0)
    got = branch_exchange(0, packed1)
    pair0 = pair_of(merged0)
    sends0 = plane_sends(pair0)
    branch_add(0, 1, after(got, sends0))
    arrived0 = plane_exchange(sends0)
    for phase in range(1, bits):
        got = branch_exchange(phase, branch_sends(phase, 1))
        if phase < bits - 1:
            branch_add(phase, 1, got)

    scaled0 = scaled_of(0, pair0, arrived0)
    tokens0 = [scaled0] + plane_exchange([scaled0] * (planes - 1))
    if bits > 1:
        branch_add(bits - 1, 1, after(got, scaled0))
    merged1 = merged_of(1)
    merged_out = pl.pallas_call(
        join_kernel,
        out_shape=jax.ShapeDtypeStruct((features, columns), jnp.bfloat16),
        in_specs=[whole((features, part))] * CHUNKS,
        out_specs=whole((features, columns)),
        grid=(1,),
        compiler_params=params(),
        name="join",
    )(merged0, merged1)
    pair1 = pair_of(merged1)
    sends1 = plane_sends(pair1)
    arrived1 = plane_exchange(sends1)

    slots0 = slots_of(0, after(tokens0, sends1), range(planes))
    scaled1 = scaled_of(1, pair1, after(arrived1, slots0))
    tokens1 = [scaled1] + plane_exchange([scaled1] * (planes - 1))
    near = slots_of(1, tokens1, range(planes // 2))
    far = slots_of(1, tokens1, range(planes // 2, planes))

    def to_experts(slots):
        return lax.all_to_all(slots, "expert", split_axis=0, concat_axis=0, tiled=True)

    rows = after(to_experts(slots0), far, merged_out, signs)
    other = exchange(rows, "fsdp", 1)
    weight_spec = pl.BlockSpec((experts, 1, part, tile), lambda n: (0, 0, 0, n))
    sums = jax.ShapeDtypeStruct((2 * count, units), jnp.float32)
    sum_spec = pl.BlockSpec((2 * count, tile), lambda n: (0, n))
    any_spec = pl.BlockSpec(memory_space=pl.ANY)
    row_scratch = [
        pltpu.VMEM((2 * count, experts * part), jnp.bfloat16),
        pltpu.VMEM((experts, lanes, part), jnp.bfloat16),
    ]
    partial = pl.pallas_call(
        functools.partial(early_kernel, tiles),
        out_shape=(
            sums,
            sums,
            jax.ShapeDtypeStruct((2 * count, lanes), jnp.float32),
            jax.ShapeDtypeStruct((2, experts, part, count), jnp.bfloat16),
        ),
        in_specs=[any_spec, any_spec, weight_spec, weight_spec],
        out_specs=(
            sum_spec,
            sum_spec,
            whole((2 * count, lanes)),
            whole((2, experts, part, count)),
        ),
        grid=(tiles,),
        scratch_shapes=row_scratch + [pltpu.SemaphoreType.DMA((1 + 4 * experts,))],
        compiler_params=params(32),
        cost_estimate=pl.CostEstimate(
            flops=8 * count * experts * part * units,
            bytes_accessed=4 * experts * part * units,
            transcendentals=0,
        ),
        name="early",
    )(rows, other, gate_view, up_view)
    tile_of = lambda i: jnp.minimum(i, tiles - 1)
    behind = lambda i: jnp.clip(i - 1, 0, tiles - 1)
    place_of = lambda i: jnp.maximum(i - tiles, 0)
    gate_sums, up_sums, stats, turned_rows = partial
    grad_shape = jax.ShapeDtypeStruct((experts, columns, units), jnp.bfloat16)
    half_planes = planes // 2
    near, far = to_experts(near), to_experts(far)
    near = after(near, partial)
    near_other = exchange(near, "fsdp", 1)
    far = after(far, near_other)
    far_other = exchange(far, "fsdp", 1)
    result = ()
    for which, (own_rows, other_rows) in enumerate(((near, near_other), (far, far_other))):

        def half_of(position_ref, which=which):
            return position_ref[1] // half_planes ^ which

        weight_spec = pl.BlockSpec(
            (experts, 1, part, tile), lambda i, position_ref: (0, 1, 0, tile_of(i))
        )
        sum_spec = pl.BlockSpec(
            (count, tile), lambda i, position_ref: (half_of(position_ref), tile_of(i))
        )
        stats_spec = pl.BlockSpec(
            (count, lanes), lambda i, position_ref: (half_of(position_ref), 0)
        )
        signs_spec = pl.BlockSpec(
            (half_planes, 2, capacity, lanes),
            lambda i, position_ref: (half_of(position_ref), 0, 0, 0),
        )
        unit_spec = pl.BlockSpec(
            (half_planes, 2, capacity, tile),
            lambda i, position_ref: (half_of(position_ref), 0, 0, behind(i)),
        )
        grad_spec = pl.BlockSpec(
            (1, columns, stretch),
            lambda i, position_ref: (place_of(i) % experts, 0, place_of(i) // experts),
        )
        result = pl.pallas_call(
            functools.partial(late_kernel, float(width), tiles, which),
            out_shape=(
                jax.ShapeDtypeStruct((planes, 2, capacity, units), jnp.bfloat16),
                grad_shape,
                grad_shape,
            ),
            grid_spec=pltpu.PrefetchScalarGridSpec(
                num_scalar_prefetch=1,
                grid=(tiles + experts * (units // stretch),),
                in_specs=[any_spec, any_spec, any_spec]
                + [weight_spec, weight_spec, sum_spec, sum_spec]
                + [stats_spec, signs_spec, unit_spec]
                + [any_spec, grad_spec, grad_spec][: len(result)],
                out_specs=(unit_spec, grad_spec, grad_spec),
                scratch_shapes=[
                    pltpu.VMEM((count, experts * part), jnp.bfloat16),
                    pltpu.VMEM((experts, lanes, part), jnp.bfloat16),
                    pltpu.VMEM((count, 1), jnp.float32),
                    pltpu.VMEM((count, 1), jnp.float32),
                    pltpu.VMEM((2, count, tile), jnp.float32),
                    pltpu.VMEM((2, count, tile), jnp.float32),
                    pltpu.VMEM((count, units), jnp.bfloat16),
                    pltpu.VMEM((count, units), jnp.bfloat16),
                    pltpu.VMEM((experts, columns, count), jnp.bfloat16),
                    pltpu.SemaphoreType.DMA((2 + 2 * experts,)),
                ],
            ),
            input_output_aliases={11: 0} if which else {},
            compiler_params=params(48),
            cost_estimate=pl.CostEstimate(
                flops=4 * count * experts * (part + columns) * units,
                bytes_accessed=8 * experts * columns * units,
                transcendentals=0,
            ),
            name="late" if which else "middle",
        )(
            position,
            own_rows,
            other_rows,
            turned_rows,
            gate_view,
            up_view,
            gate_sums,
            up_sums,
            stats,
            signs,
            cot_hidden.reshape(planes, 2, capacity, units),
            *result,
        )
    hidden, grad_gate, grad_up = result
    return (
        merged_out,
        hidden.reshape(1, -1, units),
        grad_gate.reshape(1, width, units),
        grad_up.reshape(1, width, units),
    )


def solution(mesh):
    placed = (
        P("expert", "fsdp", None),
        P("fsdp", "expert"),
        P("fsdp", "expert"),
        P("expert"),
        P("expert", None),
        P("expert", None, "fsdp"),
        P("expert", None, "fsdp"),
        P("fsdp", None),
        P("fsdp", None),
        P("expert", None, "fsdp"),
    )
    return jax.shard_map(
        per_device,
        mesh=mesh,
        in_specs=placed,
        out_specs=(
            P("fsdp", "expert"),
            P("expert", None, "fsdp"),
            P("expert", None, "fsdp"),
            P("expert", None, "fsdp"),
        ),
        check_vma=False,
    )
```

```python
import functools

import jax
import jax.numpy as jnp
from jax import lax
from jax.experimental import pallas as pl
from jax.experimental.pallas import tpu as pltpu
from jax.sharding import PartitionSpec as P

CHUNKS = 2
MEBI = 1024 * 1024


def exchange(value, axis, offset):
    size = lax.axis_size(axis)
    return lax.ppermute(value, axis, [(i, i ^ offset) for i in range(size)])


def pick(value, index, axis):
    return lax.dynamic_index_in_dim(value, index, axis, keepdims=False)


def after(value, *others):
    return lax.optimization_barrier((value, others))[0]


def bits_of(size):
    return size.bit_length() - 1


def whole(shape):
    return pl.BlockSpec(shape, lambda *_: (0,) * len(shape))


def smem():
    return pl.BlockSpec(memory_space=pltpu.SMEM)


def params(mebi=16):
    return pltpu.CompilerParams(vmem_limit_bytes=mebi * MEBI)


def signs_kernel(experts, position_ref, ids_ref, out_ref):
    blocks, capacity, lanes = out_ref.shape
    tokens = ids_ref.shape[2]
    expert = position_ref[0]
    slots = lax.broadcasted_iota(jnp.int32, (capacity, tokens), 0)
    rows = lax.broadcasted_iota(jnp.int32, (lanes, tokens), 0)
    last = lax.broadcasted_iota(jnp.int32, (capacity, lanes), 1) == lanes - 1
    for b in range(blocks):
        ids = ids_ref[b]
        e0, e1, s0, s1 = ids[0:1], ids[1:2], ids[2:3], ids[3:4]
        hit0 = jnp.where((e0 == expert) & (s0 == slots), 1.0, 0.0)
        hit1 = jnp.where((e1 == expert) & (s1 == slots), 1.0, 0.0)
        table = jnp.where(e0 == rows - 1, 1.0, 0.0) - jnp.where(e1 == rows - 1, 1.0, 0.0)
        signs = lax.dot_general(
            (hit0 - hit1).astype(jnp.bfloat16),
            table.astype(jnp.bfloat16),
            (((1,), (1,)), ((), ())),
            preferred_element_type=jnp.float32,
        )
        filled = jnp.sum(hit0 + hit1, axis=1, keepdims=True)
        out_ref[b] = jnp.where(last, filled, signs)


def pack_kernel(position_ref, low_ref, high_ref, low_out, high_out):
    low_out[0] = low_ref[...]
    high_out[0] = high_ref[...]


def pack(position, branch, c, experts):
    half = branch.shape[0] // 2
    part = branch.shape[1] // experts // CHUNKS
    others = experts // 2

    def low(j, position_ref):
        return (0, (2 * j + 1 - position_ref[0] % 2) * CHUNKS + c)

    def high(j, position_ref):
        return (1, (j + others * (1 - position_ref[0] // others)) * CHUNKS + c)

    block = pl.BlockSpec((1, half, part), lambda j, position_ref: (j, 0, 0))
    shape = jax.ShapeDtypeStruct((others, half, part), jnp.bfloat16)
    return pl.pallas_call(
        pack_kernel,
        out_shape=(shape, shape),
        grid_spec=pltpu.PrefetchScalarGridSpec(
            num_scalar_prefetch=1,
            grid=(others,),
            in_specs=[pl.BlockSpec((half, part), low), pl.BlockSpec((half, part), high)],
            out_specs=(block, block),
        ),
        compiler_params=params(),
        name="pack",
    )(position, branch, branch)


def join_kernel(*refs):
    *part_refs, out_ref = refs
    part = part_refs[0].shape[1]
    for c, part_ref in enumerate(part_refs):
        out_ref[:, c * part : (c + 1) * part] = part_ref[...]


def spread_kernel(shares_ref, ids_ref, out_ref):
    experts, quarter, columns = shares_ref.shape
    blocks, _, features = out_ref.shape
    per_expert = blocks // experts
    for f in range(blocks):
        start = (f % per_expert) * features
        out_ref[f, :quarter] = shares_ref[f // per_expert, :, start : start + features]
        out_ref[f, quarter:] = ids_ref[...]


def sides_kernel(position_ref, *refs):
    *share_refs, own_ref, other_ref = refs
    for k, share_ref in enumerate(share_refs):
        place = position_ref[0] ^ k
        for side, out_ref in enumerate((own_ref, other_ref)):
            out_ref[:, place] = share_ref[:, position_ref[2] ^ side]


def dispatch_kernel(position_ref, ids_ref, extra_ref, *refs):
    *token_refs, out_ref = refs
    planes = len(token_refs)
    experts, _, part = out_ref.shape
    lanes = extra_ref.shape[0]
    count = out_ref.shape[1] - lanes
    capacity = count // planes
    tokens = ids_ref.shape[2]
    plane, core = position_ref[1], position_ref[2]
    slots = lax.broadcasted_iota(jnp.int32, (experts * capacity, tokens), 0)
    for k in range(planes):
        source = plane ^ k
        ids = ids_ref[source * 2 + core]
        code0 = ids[0:1] * capacity + ids[2:3]
        code1 = ids[1:2] * capacity + ids[3:4]
        one_hot = jnp.where((code0 == slots) | (code1 == slots), 1.0, 0.0).astype(jnp.bfloat16)
        picked = jnp.dot(one_hot, token_refs[k][...], preferred_element_type=jnp.float32)
        rows = pl.ds(pl.multiple_of(source * capacity, 16), capacity)
        out_ref[:, rows] = picked.reshape(experts, capacity, part).astype(jnp.bfloat16)
    for e in range(experts):
        out_ref[e, count:] = extra_ref[...]


def row_stats(flat_ref, side, aux_ref):
    count = flat_ref.shape[0] // 2
    experts, lanes, part = aux_ref.shape
    squares = jnp.zeros((count, part), jnp.float32)
    logits = jnp.zeros((count, lanes), jnp.float32)
    for e in range(experts):
        rows = flat_ref[side * count : (side + 1) * count, e * part : (e + 1) * part]
        aux = aux_ref[e]
        ratio = rows.astype(jnp.float32) * (1.0 / aux[0:1].astype(jnp.float32))
        squares = squares + ratio * ratio
        logits = logits + lax.dot_general(
            rows, aux, (((1,), (1,)), ((), ())), preferred_element_type=jnp.float32
        )
    total = jnp.sum(squares, axis=1, keepdims=True)
    return jnp.where(lax.broadcasted_iota(jnp.int32, logits.shape, 1) == 0, total, logits)


def row_copies(sides, flat_ref, aux_ref, sems):
    count = flat_ref.shape[0] // 2
    experts, _, part = aux_ref.shape
    copies = [
        pltpu.make_async_copy(sides[0].at[:, pl.ds(count, aux_ref.shape[1])], aux_ref, sems.at[0])
    ]
    for side, rows_ref in enumerate(sides):
        for e in range(experts):
            copies.append(
                pltpu.make_async_copy(
                    rows_ref.at[e, pl.ds(0, count)],
                    flat_ref.at[pl.ds(side * count, count), pl.ds(e * part, part)],
                    sems.at[1 + side * experts + e],
                )
            )
    return copies


def turned(flat_ref, e, part):
    return flat_ref[:, e * part : (e + 1) * part].T


def product(flat_ref, weight_ref):
    weight = weight_ref[...].reshape(flat_ref.shape[1], weight_ref.shape[3])
    return jnp.dot(flat_ref[...], weight, preferred_element_type=jnp.float32)


def shares_of(experts, tiles, t):
    return range(t * experts // tiles, (t + 1) * experts // tiles)


def early_kernel(
    tiles,
    own_ref,
    other_ref,
    gate_ref,
    up_ref,
    gate_out,
    up_out,
    stats_out,
    turned_out,
    flat_scratch,
    aux_scratch,
    sems,
):
    count = flat_scratch.shape[0] // 2
    experts, _, part = aux_scratch.shape

    for t in range(tiles):

        @pl.when(pl.program_id(0) == t)
        def _():
            if t == 0:
                copies = row_copies((own_ref, other_ref), flat_scratch, aux_scratch, sems)
                for copy in copies:
                    copy.start()
                for copy in copies:
                    copy.wait()
            gate_out[...] = product(flat_scratch, gate_ref)
            up_out[...] = product(flat_scratch, up_ref)
            for e in shares_of(experts, tiles, t):
                turned_out[e] = turned(flat_scratch, e, part)
            if t == tiles - 1:
                for side in range(2):
                    stats_out[side * count : (side + 1) * count] = row_stats(
                        flat_scratch, side, aux_scratch
                    )


def late_kernel(
    width,
    tiles,
    position_ref,
    own_ref,
    other_ref,
    turned_ref,
    gate_ref,
    up_ref,
    gate_acc,
    up_acc,
    stats_ref,
    signs_ref,
    cot_ref,
    hidden_out,
    grad_gate_out,
    grad_up_out,
    flat_scratch,
    aux_scratch,
    scale_scratch,
    weight_scratch,
    gate_scratch,
    up_scratch,
    d_gate_scratch,
    d_up_scratch,
    turned_scratch,
    sems,
):
    step = pl.program_id(0)
    core = position_ref[2]
    planes, _, capacity, tile = hidden_out.shape
    count = planes * capacity
    experts, _, part = aux_scratch.shape
    lanes = stats_ref.shape[1]
    turn_copy = pltpu.make_async_copy(
        turned_ref, turned_scratch.at[:, pl.ds(0, part)], sems.at[1 + 2 * experts]
    )

    def scales():
        for side in range(2):
            span = slice(side * count, (side + 1) * count)
            stats = stats_ref[span] + row_stats(flat_scratch, side, aux_scratch)
            inverse = lax.rsqrt(stats[:, 0:1] / width + 1e-05)
            signs = signs_ref[:, pl.ds(core ^ side, 1)].reshape(count, lanes)
            filled = signs[:, lanes - 1 :]
            column = lax.broadcasted_iota(jnp.int32, stats.shape, 1)
            router = (column >= 1) & (column <= experts)
            margin = jnp.sum(jnp.where(router, stats * signs, 0.0), axis=1, keepdims=True)
            prob = jax.nn.sigmoid(margin * inverse).astype(jnp.bfloat16).astype(jnp.float32)
            scale_scratch[span] = inverse
            weight_scratch[span] = jnp.where(filled > 0.0, prob, 0.0)

    def units_of(t):
        for side in range(2):
            span = slice(side * count, (side + 1) * count)
            inverse = scale_scratch[span]
            weight = weight_scratch[span]
            gate_pre = inverse * gate_scratch[t % 2, span]
            up_pre = inverse * up_scratch[t % 2, span]
            sig_gate = jax.nn.sigmoid(gate_pre)
            act_gate = gate_pre * sig_gate
            hidden = (weight * act_gate * up_pre).astype(jnp.bfloat16)
            hidden_out[:, pl.ds(core ^ side, 1)] = hidden.reshape(planes, 1, capacity, tile)
            cot = cot_ref[:, pl.ds(core ^ side, 1)].reshape(count, tile)
            d_pre = cot.astype(jnp.float32) * (weight * inverse)
            d_gate = d_pre * up_pre * sig_gate * (1.0 + gate_pre * (1.0 - sig_gate))
            columns = slice(t * tile, (t + 1) * tile)
            d_gate_scratch[span, columns] = d_gate.astype(jnp.bfloat16)
            d_up_scratch[span, columns] = (d_pre * act_gate).astype(jnp.bfloat16)

    def gradients(stretch):
        e = (step - tiles) % experts
        stretch_units = grad_gate_out.shape[2]
        span = slice(stretch * stretch_units, (stretch + 1) * stretch_units)
        for scratch, out in ((d_gate_scratch, grad_gate_out), (d_up_scratch, grad_up_out)):
            out[0] = jnp.dot(
                turned_scratch[e], scratch[:, span], preferred_element_type=jnp.float32
            ).astype(jnp.bfloat16)

    for t in range(tiles):

        @pl.when(step == t)
        def _():
            if t == 0:
                copies = row_copies((own_ref, other_ref), flat_scratch, aux_scratch, sems)
                for copy in copies:
                    copy.start()
                turn_copy.start()
                for copy in copies:
                    copy.wait()
            gate_scratch[t % 2] = gate_acc[...] + product(flat_scratch, gate_ref)
            up_scratch[t % 2] = up_acc[...] + product(flat_scratch, up_ref)
            for e in shares_of(experts, tiles, t):
                turned_scratch[e, part:] = turned(flat_scratch, e, part)
            if t == 0:
                scales()
            else:
                units_of(t - 1)

    @pl.when(step == tiles)
    def _():
        turn_copy.wait()
        units_of(tiles - 1)
        gradients(0)

    for stretch in range(tiles * tile // grad_gate_out.shape[2]):
        first = tiles + stretch * experts

        @pl.when((step >= first) & (step < first + experts) & (step > tiles))
        def _():
            gradients(stretch)


def per_device(
    branch_wo,
    context,
    residual,
    norm_gain,
    router_w,
    gate_w,
    up_w,
    expert_ids,
    slot_ids,
    cot_hidden,
):
    experts = lax.axis_size("expert")
    blocks = lax.axis_size("fsdp")
    planes = blocks // 2
    expert = lax.axis_index("expert")
    block = lax.axis_index("fsdp")
    plane, core = block // 2, block % 2
    tokens, columns = context.shape
    width = columns * experts
    features = width // blocks
    capacity = cot_hidden.shape[1] // blocks
    units = cot_hidden.shape[2]
    part = columns // CHUNKS
    quarter = tokens // experts
    count = planes * capacity
    position = jnp.stack([expert, plane, core]).astype(jnp.int32)
    bits = bits_of(experts)

    lanes = experts + 2 + (-(experts + 2)) % 16
    extra = jnp.concatenate([norm_gain[None], router_w.T])
    extra = jnp.pad(extra, ((0, lanes - extra.shape[0]), (0, 0)))
    ids = jnp.concatenate([expert_ids, slot_ids], axis=1).T.astype(jnp.bfloat16)
    id_rows = ids.size // features
    ids = jnp.pad(ids.reshape(id_rows, features), ((0, -id_rows % 16), (0, 0)))

    branch = branch_wo[0]
    half = branch.shape[0] // 2
    weights = [1 << (bits - 1 - i) for i in range(bits)]
    own_bits = [(expert // weight) % 2 for weight in weights]

    def start_sum(c, h):
        def value(chosen):
            place = sum(weight * bit for weight, bit in zip(weights, chosen))
            corner = (h * half, (place * CHUNKS + c) * part)
            return lax.dynamic_slice(branch, corner, (half, part)).astype(jnp.float32)

        return value

    def joined(value, got, axis, rest):
        def total(chosen):
            chosen = [own_bits[axis] if i == axis else bit for i, bit in enumerate(chosen)]
            place = 0
            for i in rest:
                place = 2 * place + chosen[i]
            return value(chosen) + pick(got, place, 0).astype(jnp.float32)

        return total

    held = {(c, h): start_sum(c, h) for c in range(CHUNKS) for h in range(2)}
    orders = (list(range(bits))[::-1], list(range(bits)))

    def branch_sends(phase, c):
        if phase == 0:
            return pack(position, branch, c, experts)
        sends = []
        for h, order in enumerate(orders):
            rest = sorted(order[phase + 1 :])
            stacked = []
            for code in range(1 << len(rest)):
                chosen = list(own_bits)
                chosen[order[phase]] = 1 - own_bits[order[phase]]
                for at, i in enumerate(rest):
                    chosen[i] = (code >> (len(rest) - 1 - at)) & 1
                stacked.append(held[c, h](chosen).astype(jnp.bfloat16))
            sends.append(stacked[0][None] if len(stacked) == 1 else jnp.stack(stacked))
        return tuple(sends)

    def branch_exchange(phase, sends):
        return tuple(
            exchange(sends[h], "expert", weights[order[phase]]) for h, order in enumerate(orders)
        )

    def branch_add(phase, c, got):
        for h, order in enumerate(orders):
            held[c, h] = joined(held[c, h], got[h], order[phase], sorted(order[phase + 1 :]))

    def merged_of(c):
        total = jnp.concatenate([held[c, 0](own_bits), held[c, 1](own_bits)])
        return (total / experts).astype(jnp.bfloat16)

    shares = lax.all_to_all(
        context.reshape(experts, quarter, columns), "expert", split_axis=0, concat_axis=0, tiled=True
    )

    spread_shape = (blocks, quarter + ids.shape[0], features)
    to_blocks = pl.pallas_call(
        spread_kernel,
        out_shape=jax.ShapeDtypeStruct(spread_shape, jnp.bfloat16),
        in_specs=[whole(shares.shape), whole(ids.shape)],
        out_specs=whole(spread_shape),
        grid=(1,),
        compiler_params=params(),
        name="spread",
    )(shares, ids)
    got = branch_exchange(0, after(pack(position, branch, 0, experts), shares))
    branch_add(0, 0, after(got, to_blocks))
    from_blocks = lax.all_to_all(to_blocks, "fsdp", split_axis=0, concat_axis=0, tiled=True)
    for phase in range(1, bits):
        got = branch_exchange(phase, branch_sends(phase, 0))
        if phase == bits - 1:
            from_blocks, got = lax.optimization_barrier((from_blocks, got))
        branch_add(phase, 0, got)

    ids_all = from_blocks[:, quarter : quarter + id_rows].astype(jnp.int32)
    ids_all = ids_all.reshape(blocks, 4, tokens)
    own_share = from_blocks[:, :quarter]
    packed1 = branch_sends(0, 1)
    pieces = [exchange(own_share, "expert", k) if k else own_share for k in range(experts)]
    pieces, packed1 = lax.optimization_barrier((pieces, packed1))
    side_shape = (planes, experts, quarter, features)
    sides = pl.pallas_call(
        sides_kernel,
        out_shape=(jax.ShapeDtypeStruct(side_shape, jnp.bfloat16),) * 2,
        in_specs=[smem()] + [whole((planes, 2, quarter, features))] * experts,
        out_specs=(whole(side_shape),) * 2,
        grid=(1,),
        compiler_params=params(),
        name="sides",
    )(position, *[piece.reshape(planes, 2, quarter, features) for piece in pieces])
    sides = [side.reshape(planes * tokens, features) for side in sides]
    signs = pl.pallas_call(
        functools.partial(signs_kernel, experts),
        out_shape=jax.ShapeDtypeStruct((blocks, capacity, lanes), jnp.float32),
        in_specs=[smem(), whole(ids_all.shape)],
        out_specs=whole((blocks, capacity, lanes)),
        grid=(1,),
        compiler_params=params(),
        name="signs",
    )(position, ids_all).reshape(planes, 2, capacity, lanes)

    gate_view = gate_w.reshape(experts, CHUNKS, part, units)
    up_view = up_w.reshape(experts, CHUNKS, part, units)
    tile = min(256, units)
    stretch = min(512, units)
    tiles = units // tile
    def pair_of(merged):
        def attend(rows):
            out = jnp.dot(rows, merged, preferred_element_type=jnp.float32)
            return out.reshape(planes, tokens, part)

        swapped = exchange(attend(sides[1]).astype(jnp.bfloat16), "fsdp", 1)
        return attend(sides[0]) + swapped.astype(jnp.float32)

    def plane_sends(pair):
        return [pick(pair, plane ^ k, 0).astype(jnp.bfloat16) for k in range(1, planes)]

    def plane_exchange(sends):
        return [exchange(send, "fsdp", 2 * k) for k, send in enumerate(sends, 1)]

    def scaled_of(c, pair, arrived):
        span = slice(c * part, (c + 1) * part)
        hstate = residual[:, span].astype(jnp.float32) + pick(pair, plane, 0)
        for value in arrived:
            hstate = hstate + value.astype(jnp.float32)
        return (hstate * norm_gain[span].astype(jnp.float32)).astype(jnp.bfloat16)

    height = count + lanes

    def slots_of(c, own_tokens):
        return pl.pallas_call(
            dispatch_kernel,
            out_shape=jax.ShapeDtypeStruct((experts, height, part), jnp.bfloat16),
            in_specs=[smem(), whole(ids_all.shape)]
            + [pl.BlockSpec((lanes, part), lambda i, c=c: (0, c))]
            + [whole((tokens, part))] * planes,
            out_specs=whole((experts, height, part)),
            grid=(1,),
            compiler_params=params(),
            name="dispatch",
        )(position, ids_all, extra, *own_tokens)

    merged0 = merged_of(0)
    got = branch_exchange(0, packed1)
    pair0 = pair_of(merged0)
    sends0 = plane_sends(pair0)
    branch_add(0, 1, after(got, sends0))
    arrived0 = plane_exchange(sends0)
    for phase in range(1, bits):
        got = branch_exchange(phase, branch_sends(phase, 1))
        if phase < bits - 1:
            branch_add(phase, 1, got)

    scaled0 = scaled_of(0, pair0, arrived0)
    tokens0 = [scaled0] + plane_exchange([scaled0] * (planes - 1))
    if bits > 1:
        branch_add(bits - 1, 1, after(got, scaled0))
    merged1 = merged_of(1)
    merged_out = pl.pallas_call(
        join_kernel,
        out_shape=jax.ShapeDtypeStruct((features, columns), jnp.bfloat16),
        in_specs=[whole((features, part))] * CHUNKS,
        out_specs=whole((features, columns)),
        grid=(1,),
        compiler_params=params(),
        name="join",
    )(merged0, merged1)
    pair1 = pair_of(merged1)
    sends1 = plane_sends(pair1)
    arrived1 = plane_exchange(sends1)

    slots0 = slots_of(0, after(tokens0, sends1))
    scaled1 = scaled_of(1, pair1, after(arrived1, slots0))
    tokens1 = [scaled1] + plane_exchange([scaled1] * (planes - 1))
    slots1 = slots_of(1, tokens1)
    slots = (slots0, slots1)

    def to_experts(c):
        return lax.all_to_all(slots[c], "expert", split_axis=0, concat_axis=0, tiled=True)

    rows = after(to_experts(0), slots[-1], merged_out, signs)
    other = exchange(rows, "fsdp", 1)
    weight_spec = pl.BlockSpec((experts, 1, part, tile), lambda n: (0, 0, 0, n))
    sums = jax.ShapeDtypeStruct((2 * count, units), jnp.float32)
    sum_spec = pl.BlockSpec((2 * count, tile), lambda n: (0, n))
    any_spec = pl.BlockSpec(memory_space=pl.ANY)
    row_spec = pl.BlockSpec(memory_space=pltpu.HBM)
    row_scratch = [
        pltpu.VMEM((2 * count, experts * part), jnp.bfloat16),
        pltpu.VMEM((experts, lanes, part), jnp.bfloat16),
    ]
    partial = pl.pallas_call(
        functools.partial(early_kernel, tiles),
        out_shape=(
            sums,
            sums,
            jax.ShapeDtypeStruct((2 * count, lanes), jnp.float32),
            jax.ShapeDtypeStruct((experts, part, 2 * count), jnp.bfloat16),
        ),
        in_specs=[any_spec, any_spec, weight_spec, weight_spec],
        out_specs=(
            sum_spec,
            sum_spec,
            whole((2 * count, lanes)),
            whole((experts, part, 2 * count)),
        ),
        grid=(tiles,),
        scratch_shapes=row_scratch + [pltpu.SemaphoreType.DMA((1 + 2 * experts,))],
        compiler_params=params(32),
        cost_estimate=pl.CostEstimate(
            flops=8 * count * experts * part * units,
            bytes_accessed=4 * experts * part * units,
            transcendentals=0,
        ),
        name="early",
    )(rows, other, gate_view, up_view)
    rows = after(to_experts(1), partial)
    other = exchange(rows, "fsdp", 1)

    tile_of = lambda i: jnp.minimum(i, tiles - 1)
    behind = lambda i: jnp.clip(i - 1, 0, tiles - 1)
    place_of = lambda i: jnp.maximum(i - tiles, 0)
    weight_spec = pl.BlockSpec((experts, 1, part, tile), lambda i: (0, 1, 0, tile_of(i)))
    sum_spec = pl.BlockSpec((2 * count, tile), lambda i: (0, tile_of(i)))
    unit_spec = pl.BlockSpec((planes, 2, capacity, tile), lambda i: (0, 0, 0, behind(i)))
    grad_spec = pl.BlockSpec(
        (1, columns, stretch), lambda i: (place_of(i) % experts, 0, place_of(i) // experts)
    )
    grad_shape = jax.ShapeDtypeStruct((experts, columns, units), jnp.bfloat16)
    gate_sums, up_sums, stats, turned_rows = partial
    hidden, grad_gate, grad_up = pl.pallas_call(
        functools.partial(late_kernel, float(width), tiles),
        out_shape=(
            jax.ShapeDtypeStruct((planes, 2, capacity, units), jnp.bfloat16),
            grad_shape,
            grad_shape,
        ),
        in_specs=[smem(), row_spec, row_spec, any_spec]
        + [weight_spec, weight_spec, sum_spec, sum_spec]
        + [whole(stats.shape), whole(signs.shape), unit_spec],
        out_specs=(unit_spec, grad_spec, grad_spec),
        grid=(tiles + experts * (units // stretch),),
        scratch_shapes=row_scratch
        + [
            pltpu.VMEM((2 * count, 1), jnp.float32),
            pltpu.VMEM((2 * count, 1), jnp.float32),
            pltpu.VMEM((2, 2 * count, tile), jnp.float32),
            pltpu.VMEM((2, 2 * count, tile), jnp.float32),
            pltpu.VMEM((2 * count, units), jnp.bfloat16),
            pltpu.VMEM((2 * count, units), jnp.bfloat16),
            pltpu.VMEM((experts, columns, 2 * count), jnp.bfloat16),
            pltpu.SemaphoreType.DMA((2 + 2 * experts,)),
        ],
        compiler_params=params(48),
        name="late",
    )(
        position,
        rows,
        other,
        turned_rows,
        gate_view,
        up_view,
        gate_sums,
        up_sums,
        stats,
        signs,
        cot_hidden.reshape(planes, 2, capacity, units),
    )
    return (
        merged_out,
        hidden.reshape(1, -1, units),
        grad_gate.reshape(1, width, units),
        grad_up.reshape(1, width, units),
    )


def solution(mesh):
    placed = (
        P("expert", "fsdp", None),
        P("fsdp", "expert"),
        P("fsdp", "expert"),
        P("expert"),
        P("expert", None),
        P("expert", None, "fsdp"),
        P("expert", None, "fsdp"),
        P("fsdp", None),
        P("fsdp", None),
        P("expert", None, "fsdp"),
    )
    return jax.shard_map(
        per_device,
        mesh=mesh,
        in_specs=placed,
        out_specs=(
            P("fsdp", "expert"),
            P("expert", None, "fsdp"),
            P("expert", None, "fsdp"),
            P("expert", None, "fsdp"),
        ),
        check_vma=False,
    )
```

```python
import functools

import jax
import jax.numpy as jnp
from jax import lax
from jax.experimental import pallas as pl
from jax.experimental.pallas import tpu as pltpu
from jax.sharding import PartitionSpec as P

CHUNKS = 2
MEBI = 1024 * 1024


def exchange(value, axis, offset):
    size = lax.axis_size(axis)
    return lax.ppermute(value, axis, [(i, i ^ offset) for i in range(size)])


def pick(value, index, axis):
    return lax.dynamic_index_in_dim(value, index, axis, keepdims=False)


def after(value, *others):
    return lax.optimization_barrier((value, others))[0]


def bits_of(size):
    return size.bit_length() - 1


def whole(shape):
    return pl.BlockSpec(shape, lambda *_: (0,) * len(shape))


def smem():
    return pl.BlockSpec(memory_space=pltpu.SMEM)


def params(mebi=16):
    return pltpu.CompilerParams(vmem_limit_bytes=mebi * MEBI)


def signs_kernel(experts, position_ref, ids_ref, out_ref):
    blocks, capacity, lanes = out_ref.shape
    tokens = ids_ref.shape[2]
    expert = position_ref[0]
    slots = lax.broadcasted_iota(jnp.int32, (capacity, tokens), 0)
    rows = lax.broadcasted_iota(jnp.int32, (lanes, tokens), 0)
    last = lax.broadcasted_iota(jnp.int32, (capacity, lanes), 1) == lanes - 1
    for b in range(blocks):
        ids = ids_ref[b]
        e0, e1, s0, s1 = ids[0:1], ids[1:2], ids[2:3], ids[3:4]
        hit0 = jnp.where((e0 == expert) & (s0 == slots), 1.0, 0.0)
        hit1 = jnp.where((e1 == expert) & (s1 == slots), 1.0, 0.0)
        table = jnp.where(e0 == rows - 1, 1.0, 0.0) - jnp.where(e1 == rows - 1, 1.0, 0.0)
        signs = lax.dot_general(
            (hit0 - hit1).astype(jnp.bfloat16),
            table.astype(jnp.bfloat16),
            (((1,), (1,)), ((), ())),
            preferred_element_type=jnp.float32,
        )
        filled = jnp.sum(hit0 + hit1, axis=1, keepdims=True)
        out_ref[b] = jnp.where(last, filled, signs)


def pack_kernel(position_ref, low_ref, high_ref, low_out, high_out):
    low_out[0] = low_ref[...]
    high_out[0] = high_ref[...]


def pack(position, branch, c, experts):
    half = branch.shape[0] // 2
    part = branch.shape[1] // experts // CHUNKS
    others = experts // 2

    def low(j, position_ref):
        return (0, (2 * j + 1 - position_ref[0] % 2) * CHUNKS + c)

    def high(j, position_ref):
        return (1, (j + others * (1 - position_ref[0] // others)) * CHUNKS + c)

    block = pl.BlockSpec((1, half, part), lambda j, position_ref: (j, 0, 0))
    shape = jax.ShapeDtypeStruct((others, half, part), jnp.bfloat16)
    return pl.pallas_call(
        pack_kernel,
        out_shape=(shape, shape),
        grid_spec=pltpu.PrefetchScalarGridSpec(
            num_scalar_prefetch=1,
            grid=(others,),
            in_specs=[pl.BlockSpec((half, part), low), pl.BlockSpec((half, part), high)],
            out_specs=(block, block),
        ),
        compiler_params=params(),
        name="pack",
    )(position, branch, branch)


def join_kernel(*refs):
    *part_refs, out_ref = refs
    part = part_refs[0].shape[1]
    for c, part_ref in enumerate(part_refs):
        out_ref[:, c * part : (c + 1) * part] = part_ref[...]


def spread_kernel(shares_ref, ids_ref, out_ref):
    experts, quarter, columns = shares_ref.shape
    blocks, _, features = out_ref.shape
    per_expert = blocks // experts
    for f in range(blocks):
        start = (f % per_expert) * features
        out_ref[f, :quarter] = shares_ref[f // per_expert, :, start : start + features]
        out_ref[f, quarter:] = ids_ref[...]


def sides_kernel(position_ref, *refs):
    *share_refs, own_ref, other_ref = refs
    for k, share_ref in enumerate(share_refs):
        place = position_ref[0] ^ k
        for side, out_ref in enumerate((own_ref, other_ref)):
            out_ref[:, place] = share_ref[:, position_ref[2] ^ side]


def dispatch_kernel(position_ref, ids_ref, extra_ref, *refs):
    *token_refs, out_ref = refs
    planes = len(token_refs)
    experts, _, part = out_ref.shape
    lanes = extra_ref.shape[0]
    count = out_ref.shape[1] - lanes
    capacity = count // planes
    tokens = ids_ref.shape[2]
    plane, core = position_ref[1], position_ref[2]
    slots = lax.broadcasted_iota(jnp.int32, (experts * capacity, tokens), 0)
    for k in range(planes):
        source = plane ^ k
        ids = ids_ref[source * 2 + core]
        code0 = ids[0:1] * capacity + ids[2:3]
        code1 = ids[1:2] * capacity + ids[3:4]
        one_hot = jnp.where((code0 == slots) | (code1 == slots), 1.0, 0.0).astype(jnp.bfloat16)
        picked = jnp.dot(one_hot, token_refs[k][...], preferred_element_type=jnp.float32)
        rows = pl.ds(pl.multiple_of(source * capacity, 16), capacity)
        out_ref[:, rows] = picked.reshape(experts, capacity, part).astype(jnp.bfloat16)
    for e in range(experts):
        out_ref[e, count:] = extra_ref[...]


def row_stats(flat_ref, side, aux_ref):
    count = flat_ref.shape[0] // 2
    experts, lanes, part = aux_ref.shape
    squares = jnp.zeros((count, part), jnp.float32)
    logits = jnp.zeros((count, lanes), jnp.float32)
    for e in range(experts):
        rows = flat_ref[side * count : (side + 1) * count, e * part : (e + 1) * part]
        aux = aux_ref[e]
        ratio = rows.astype(jnp.float32) * (1.0 / aux[0:1].astype(jnp.float32))
        squares = squares + ratio * ratio
        logits = logits + lax.dot_general(
            rows, aux, (((1,), (1,)), ((), ())), preferred_element_type=jnp.float32
        )
    total = jnp.sum(squares, axis=1, keepdims=True)
    return jnp.where(lax.broadcasted_iota(jnp.int32, logits.shape, 1) == 0, total, logits)


def row_copies(sides, flat_ref, aux_ref, sems):
    count = flat_ref.shape[0] // 2
    experts, _, part = aux_ref.shape
    copies = [
        pltpu.make_async_copy(sides[0].at[:, pl.ds(count, aux_ref.shape[1])], aux_ref, sems.at[0])
    ]
    for side, rows_ref in enumerate(sides):
        for e in range(experts):
            copies.append(
                pltpu.make_async_copy(
                    rows_ref.at[e, pl.ds(0, count)],
                    flat_ref.at[pl.ds(side * count, count), pl.ds(e * part, part)],
                    sems.at[1 + side * experts + e],
                )
            )
    return copies


def turned(flat_ref, e, part):
    return flat_ref[:, e * part : (e + 1) * part].T


def product(flat_ref, weight_ref):
    weight = weight_ref[...].reshape(flat_ref.shape[1], weight_ref.shape[3])
    return jnp.dot(flat_ref[...], weight, preferred_element_type=jnp.float32)


def shares_of(experts, tiles, t):
    return range(t * experts // tiles, (t + 1) * experts // tiles)


def early_kernel(
    tiles,
    own_ref,
    other_ref,
    gate_ref,
    up_ref,
    gate_out,
    up_out,
    stats_out,
    turned_out,
    flat_scratch,
    aux_scratch,
    sems,
):
    count = flat_scratch.shape[0] // 2
    experts, _, part = aux_scratch.shape

    for t in range(tiles):

        @pl.when(pl.program_id(0) == t)
        def _():
            if t == 0:
                copies = row_copies((own_ref, other_ref), flat_scratch, aux_scratch, sems)
                for copy in copies:
                    copy.start()
                for copy in copies:
                    copy.wait()
            gate_out[...] = product(flat_scratch, gate_ref)
            up_out[...] = product(flat_scratch, up_ref)
            for e in shares_of(experts, tiles, t):
                turned_out[e] = turned(flat_scratch, e, part)
            if t == tiles - 1:
                for side in range(2):
                    stats_out[side * count : (side + 1) * count] = row_stats(
                        flat_scratch, side, aux_scratch
                    )


def late_kernel(
    width,
    tiles,
    position_ref,
    own_ref,
    other_ref,
    turned_ref,
    gate_ref,
    up_ref,
    gate_acc,
    up_acc,
    stats_hbm,
    signs_hbm,
    cot_hbm,
    hidden_out,
    grad_gate_out,
    grad_up_out,
    flat_scratch,
    aux_scratch,
    scale_scratch,
    weight_scratch,
    gate_scratch,
    up_scratch,
    d_gate_scratch,
    d_up_scratch,
    turned_scratch,
    stats_ref,
    signs_ref,
    cot_ref,
    sems,
):
    step = pl.program_id(0)
    core = position_ref[2]
    planes, _, capacity, tile = hidden_out.shape
    count = planes * capacity
    experts, _, part = aux_scratch.shape
    lanes = stats_ref.shape[1]
    turn_copy = pltpu.make_async_copy(
        turned_ref, turned_scratch.at[:, pl.ds(0, part)], sems.at[1 + 2 * experts]
    )

    stats_copy = pltpu.make_async_copy(stats_hbm, stats_ref, sems.at[2 + 2 * experts])
    signs_copy = pltpu.make_async_copy(signs_hbm, signs_ref, sems.at[3 + 2 * experts])
    cot_copy = pltpu.make_async_copy(cot_hbm, cot_ref, sems.at[4 + 2 * experts])

    def scales():
        stats_copy.wait()
        signs_copy.wait()
        for side in range(2):
            span = slice(side * count, (side + 1) * count)
            stats = stats_ref[span] + row_stats(flat_scratch, side, aux_scratch)
            inverse = lax.rsqrt(stats[:, 0:1] / width + 1e-05)
            signs = signs_ref[:, pl.ds(core ^ side, 1)].reshape(count, lanes)
            filled = signs[:, lanes - 1 :]
            column = lax.broadcasted_iota(jnp.int32, stats.shape, 1)
            router = (column >= 1) & (column <= experts)
            margin = jnp.sum(jnp.where(router, stats * signs, 0.0), axis=1, keepdims=True)
            prob = jax.nn.sigmoid(margin * inverse).astype(jnp.bfloat16).astype(jnp.float32)
            scale_scratch[span] = inverse
            weight_scratch[span] = jnp.where(filled > 0.0, prob, 0.0)

    def units_of(t):
        columns = slice(t * tile, (t + 1) * tile)
        if t == 0:
            cot_copy.wait()
        for side in range(2):
            span = slice(side * count, (side + 1) * count)
            inverse = scale_scratch[span]
            weight = weight_scratch[span]
            gate_pre = inverse * gate_scratch[t % 2, span]
            up_pre = inverse * up_scratch[t % 2, span]
            sig_gate = jax.nn.sigmoid(gate_pre)
            act_gate = gate_pre * sig_gate
            hidden = (weight * act_gate * up_pre).astype(jnp.bfloat16)
            hidden_out[:, pl.ds(core ^ side, 1)] = hidden.reshape(planes, 1, capacity, tile)
            cot = cot_ref[:, pl.ds(core ^ side, 1), :, columns].reshape(count, tile)
            d_pre = cot.astype(jnp.float32) * (weight * inverse)
            d_gate = d_pre * up_pre * sig_gate * (1.0 + gate_pre * (1.0 - sig_gate))
            d_gate_scratch[span, columns] = d_gate.astype(jnp.bfloat16)
            d_up_scratch[span, columns] = (d_pre * act_gate).astype(jnp.bfloat16)

    def gradients(stretch):
        e = (step - tiles) % experts
        stretch_units = grad_gate_out.shape[2]
        span = slice(stretch * stretch_units, (stretch + 1) * stretch_units)
        for scratch, out in ((d_gate_scratch, grad_gate_out), (d_up_scratch, grad_up_out)):
            out[0] = jnp.dot(
                turned_scratch[e], scratch[:, span], preferred_element_type=jnp.float32
            ).astype(jnp.bfloat16)

    for t in range(tiles):

        @pl.when(step == t)
        def _():
            if t == 0:
                copies = row_copies((own_ref, other_ref), flat_scratch, aux_scratch, sems)
                for copy in copies:
                    copy.start()
                for copy in (stats_copy, signs_copy, cot_copy, turn_copy):
                    copy.start()
                for copy in copies:
                    copy.wait()
            gate_scratch[t % 2] = gate_acc[...] + product(flat_scratch, gate_ref)
            up_scratch[t % 2] = up_acc[...] + product(flat_scratch, up_ref)
            for e in shares_of(experts, tiles, t):
                turned_scratch[e, part:] = turned(flat_scratch, e, part)
            if t == 0:
                scales()
            else:
                units_of(t - 1)

    @pl.when(step == tiles)
    def _():
        turn_copy.wait()
        units_of(tiles - 1)
        gradients(0)

    for stretch in range(tiles * tile // grad_gate_out.shape[2]):
        first = tiles + stretch * experts

        @pl.when((step >= first) & (step < first + experts) & (step > tiles))
        def _():
            gradients(stretch)


def per_device(
    branch_wo,
    context,
    residual,
    norm_gain,
    router_w,
    gate_w,
    up_w,
    expert_ids,
    slot_ids,
    cot_hidden,
):
    experts = lax.axis_size("expert")
    blocks = lax.axis_size("fsdp")
    planes = blocks // 2
    expert = lax.axis_index("expert")
    block = lax.axis_index("fsdp")
    plane, core = block // 2, block % 2
    tokens, columns = context.shape
    width = columns * experts
    features = width // blocks
    capacity = cot_hidden.shape[1] // blocks
    units = cot_hidden.shape[2]
    part = columns // CHUNKS
    quarter = tokens // experts
    count = planes * capacity
    position = jnp.stack([expert, plane, core]).astype(jnp.int32)
    bits = bits_of(experts)

    lanes = experts + 2 + (-(experts + 2)) % 16
    extra = jnp.concatenate([norm_gain[None], router_w.T])
    extra = jnp.pad(extra, ((0, lanes - extra.shape[0]), (0, 0)))
    ids = jnp.concatenate([expert_ids, slot_ids], axis=1).T.astype(jnp.bfloat16)
    id_rows = ids.size // features
    ids = jnp.pad(ids.reshape(id_rows, features), ((0, -id_rows % 16), (0, 0)))

    branch = branch_wo[0]
    half = branch.shape[0] // 2
    weights = [1 << (bits - 1 - i) for i in range(bits)]
    own_bits = [(expert // weight) % 2 for weight in weights]

    def start_sum(c, h):
        def value(chosen):
            place = sum(weight * bit for weight, bit in zip(weights, chosen))
            corner = (h * half, (place * CHUNKS + c) * part)
            return lax.dynamic_slice(branch, corner, (half, part)).astype(jnp.float32)

        return value

    def joined(value, got, axis, rest):
        def total(chosen):
            chosen = [own_bits[axis] if i == axis else bit for i, bit in enumerate(chosen)]
            place = 0
            for i in rest:
                place = 2 * place + chosen[i]
            return value(chosen) + pick(got, place, 0).astype(jnp.float32)

        return total

    held = {(c, h): start_sum(c, h) for c in range(CHUNKS) for h in range(2)}
    orders = (list(range(bits))[::-1], list(range(bits)))

    def branch_sends(phase, c):
        if phase == 0:
            return pack(position, branch, c, experts)
        sends = []
        for h, order in enumerate(orders):
            rest = sorted(order[phase + 1 :])
            stacked = []
            for code in range(1 << len(rest)):
                chosen = list(own_bits)
                chosen[order[phase]] = 1 - own_bits[order[phase]]
                for at, i in enumerate(rest):
                    chosen[i] = (code >> (len(rest) - 1 - at)) & 1
                stacked.append(held[c, h](chosen).astype(jnp.bfloat16))
            sends.append(stacked[0][None] if len(stacked) == 1 else jnp.stack(stacked))
        return tuple(sends)

    def branch_exchange(phase, sends):
        return tuple(
            exchange(sends[h], "expert", weights[order[phase]]) for h, order in enumerate(orders)
        )

    def branch_add(phase, c, got):
        for h, order in enumerate(orders):
            held[c, h] = joined(held[c, h], got[h], order[phase], sorted(order[phase + 1 :]))

    def merged_of(c):
        total = jnp.concatenate([held[c, 0](own_bits), held[c, 1](own_bits)])
        return (total / experts).astype(jnp.bfloat16)

    shares = lax.all_to_all(
        context.reshape(experts, quarter, columns), "expert", split_axis=0, concat_axis=0, tiled=True
    )

    spread_shape = (blocks, quarter + ids.shape[0], features)
    to_blocks = pl.pallas_call(
        spread_kernel,
        out_shape=jax.ShapeDtypeStruct(spread_shape, jnp.bfloat16),
        in_specs=[whole(shares.shape), whole(ids.shape)],
        out_specs=whole(spread_shape),
        grid=(1,),
        compiler_params=params(),
        name="spread",
    )(shares, ids)
    got = branch_exchange(0, after(pack(position, branch, 0, experts), shares))
    branch_add(0, 0, after(got, to_blocks))
    from_blocks = lax.all_to_all(to_blocks, "fsdp", split_axis=0, concat_axis=0, tiled=True)
    for phase in range(1, bits):
        got = branch_exchange(phase, branch_sends(phase, 0))
        if phase == bits - 1:
            from_blocks, got = lax.optimization_barrier((from_blocks, got))
        branch_add(phase, 0, got)

    ids_all = from_blocks[:, quarter : quarter + id_rows].astype(jnp.int32)
    ids_all = ids_all.reshape(blocks, 4, tokens)
    own_share = from_blocks[:, :quarter]
    packed1 = branch_sends(0, 1)
    pieces = [exchange(own_share, "expert", k) if k else own_share for k in range(experts)]
    pieces, packed1 = lax.optimization_barrier((pieces, packed1))
    side_shape = (planes, experts, quarter, features)
    sides = pl.pallas_call(
        sides_kernel,
        out_shape=(jax.ShapeDtypeStruct(side_shape, jnp.bfloat16),) * 2,
        in_specs=[smem()] + [whole((planes, 2, quarter, features))] * experts,
        out_specs=(whole(side_shape),) * 2,
        grid=(1,),
        compiler_params=params(),
        name="sides",
    )(position, *[piece.reshape(planes, 2, quarter, features) for piece in pieces])
    sides = [side.reshape(planes * tokens, features) for side in sides]
    signs = pl.pallas_call(
        functools.partial(signs_kernel, experts),
        out_shape=jax.ShapeDtypeStruct((blocks, capacity, lanes), jnp.float32),
        in_specs=[smem(), whole(ids_all.shape)],
        out_specs=whole((blocks, capacity, lanes)),
        grid=(1,),
        compiler_params=params(),
        name="signs",
    )(position, ids_all).reshape(planes, 2, capacity, lanes)

    gate_view = gate_w.reshape(experts, CHUNKS, part, units)
    up_view = up_w.reshape(experts, CHUNKS, part, units)
    tile = min(256, units)
    stretch = min(512, units)
    tiles = units // tile
    def pair_of(merged):
        def attend(rows):
            out = jnp.dot(rows, merged, preferred_element_type=jnp.float32)
            return out.reshape(planes, tokens, part)

        swapped = exchange(attend(sides[1]).astype(jnp.bfloat16), "fsdp", 1)
        return attend(sides[0]) + swapped.astype(jnp.float32)

    def plane_sends(pair):
        return [pick(pair, plane ^ k, 0).astype(jnp.bfloat16) for k in range(1, planes)]

    def plane_exchange(sends):
        return [exchange(send, "fsdp", 2 * k) for k, send in enumerate(sends, 1)]

    def scaled_of(c, pair, arrived):
        span = slice(c * part, (c + 1) * part)
        hstate = residual[:, span].astype(jnp.float32) + pick(pair, plane, 0)
        for value in arrived:
            hstate = hstate + value.astype(jnp.float32)
        return (hstate * norm_gain[span].astype(jnp.float32)).astype(jnp.bfloat16)

    height = count + lanes

    def slots_of(c, own_tokens):
        return pl.pallas_call(
            dispatch_kernel,
            out_shape=jax.ShapeDtypeStruct((experts, height, part), jnp.bfloat16),
            in_specs=[smem(), whole(ids_all.shape)]
            + [pl.BlockSpec((lanes, part), lambda i, c=c: (0, c))]
            + [whole((tokens, part))] * planes,
            out_specs=whole((experts, height, part)),
            grid=(1,),
            compiler_params=params(),
            name="dispatch",
        )(position, ids_all, extra, *own_tokens)

    merged0 = merged_of(0)
    got = branch_exchange(0, packed1)
    pair0 = pair_of(merged0)
    sends0 = plane_sends(pair0)
    branch_add(0, 1, after(got, sends0))
    arrived0 = plane_exchange(sends0)
    for phase in range(1, bits):
        got = branch_exchange(phase, branch_sends(phase, 1))
        if phase < bits - 1:
            branch_add(phase, 1, got)

    scaled0 = scaled_of(0, pair0, arrived0)
    tokens0 = [scaled0] + plane_exchange([scaled0] * (planes - 1))
    if bits > 1:
        branch_add(bits - 1, 1, after(got, scaled0))
    merged1 = merged_of(1)
    merged_out = pl.pallas_call(
        join_kernel,
        out_shape=jax.ShapeDtypeStruct((features, columns), jnp.bfloat16),
        in_specs=[whole((features, part))] * CHUNKS,
        out_specs=whole((features, columns)),
        grid=(1,),
        compiler_params=params(),
        name="join",
    )(merged0, merged1)
    pair1 = pair_of(merged1)
    sends1 = plane_sends(pair1)
    arrived1 = plane_exchange(sends1)

    slots0 = slots_of(0, after(tokens0, sends1))
    scaled1 = scaled_of(1, pair1, after(arrived1, slots0))
    tokens1 = [scaled1] + plane_exchange([scaled1] * (planes - 1))
    slots1 = slots_of(1, tokens1)
    slots = (slots0, slots1)

    def to_experts(c):
        return lax.all_to_all(slots[c], "expert", split_axis=0, concat_axis=0, tiled=True)

    rows = after(to_experts(0), slots[-1], merged_out, signs)
    other = exchange(rows, "fsdp", 1)
    weight_spec = pl.BlockSpec((experts, 1, part, tile), lambda n: (0, 0, 0, n))
    sums = jax.ShapeDtypeStruct((2 * count, units), jnp.float32)
    sum_spec = pl.BlockSpec((2 * count, tile), lambda n: (0, n))
    any_spec = pl.BlockSpec(memory_space=pl.ANY)
    row_spec = pl.BlockSpec(memory_space=pltpu.HBM)
    row_scratch = [
        pltpu.VMEM((2 * count, experts * part), jnp.bfloat16),
        pltpu.VMEM((experts, lanes, part), jnp.bfloat16),
    ]
    partial = pl.pallas_call(
        functools.partial(early_kernel, tiles),
        out_shape=(
            sums,
            sums,
            jax.ShapeDtypeStruct((2 * count, lanes), jnp.float32),
            jax.ShapeDtypeStruct((experts, part, 2 * count), jnp.bfloat16),
        ),
        in_specs=[any_spec, any_spec, weight_spec, weight_spec],
        out_specs=(
            sum_spec,
            sum_spec,
            whole((2 * count, lanes)),
            whole((experts, part, 2 * count)),
        ),
        grid=(tiles,),
        scratch_shapes=row_scratch + [pltpu.SemaphoreType.DMA((1 + 2 * experts,))],
        compiler_params=params(32),
        cost_estimate=pl.CostEstimate(
            flops=8 * count * experts * part * units,
            bytes_accessed=4 * experts * part * units,
            transcendentals=0,
        ),
        name="early",
    )(rows, other, gate_view, up_view)
    rows = after(to_experts(1), partial)
    other = exchange(rows, "fsdp", 1)

    tile_of = lambda i: jnp.minimum(i, tiles - 1)
    behind = lambda i: jnp.clip(i - 1, 0, tiles - 1)
    place_of = lambda i: jnp.maximum(i - tiles, 0)
    weight_spec = pl.BlockSpec((experts, 1, part, tile), lambda i: (0, 1, 0, tile_of(i)))
    sum_spec = pl.BlockSpec((2 * count, tile), lambda i: (0, tile_of(i)))
    unit_spec = pl.BlockSpec((planes, 2, capacity, tile), lambda i: (0, 0, 0, behind(i)))
    grad_spec = pl.BlockSpec(
        (1, columns, stretch), lambda i: (place_of(i) % experts, 0, place_of(i) // experts)
    )
    grad_shape = jax.ShapeDtypeStruct((experts, columns, units), jnp.bfloat16)
    gate_sums, up_sums, stats, turned_rows = partial
    hidden, grad_gate, grad_up = pl.pallas_call(
        functools.partial(late_kernel, float(width), tiles),
        out_shape=(
            jax.ShapeDtypeStruct((planes, 2, capacity, units), jnp.bfloat16),
            grad_shape,
            grad_shape,
        ),
        in_specs=[smem(), row_spec, row_spec, any_spec]
        + [weight_spec, weight_spec, sum_spec, sum_spec]
        + [row_spec] * 3,
        out_specs=(unit_spec, grad_spec, grad_spec),
        grid=(tiles + experts * (units // stretch),),
        scratch_shapes=row_scratch
        + [
            pltpu.VMEM((2 * count, 1), jnp.float32),
            pltpu.VMEM((2 * count, 1), jnp.float32),
            pltpu.VMEM((2, 2 * count, tile), jnp.float32),
            pltpu.VMEM((2, 2 * count, tile), jnp.float32),
            pltpu.VMEM((2 * count, units), jnp.bfloat16),
            pltpu.VMEM((2 * count, units), jnp.bfloat16),
            pltpu.VMEM((experts, columns, 2 * count), jnp.bfloat16),
            pltpu.VMEM((2 * count, lanes), jnp.float32),
            pltpu.VMEM(signs.shape, jnp.float32),
            pltpu.VMEM((planes, 2, capacity, units), jnp.bfloat16),
            pltpu.SemaphoreType.DMA((5 + 2 * experts,)),
        ],
        compiler_params=params(48),
        name="late",
    )(
        position,
        rows,
        other,
        turned_rows,
        gate_view,
        up_view,
        gate_sums,
        up_sums,
        stats,
        signs,
        cot_hidden.reshape(planes, 2, capacity, units),
    )
    return (
        merged_out,
        hidden.reshape(1, -1, units),
        grad_gate.reshape(1, width, units),
        grad_up.reshape(1, width, units),
    )


def solution(mesh):
    placed = (
        P("expert", "fsdp", None),
        P("fsdp", "expert"),
        P("fsdp", "expert"),
        P("expert"),
        P("expert", None),
        P("expert", None, "fsdp"),
        P("expert", None, "fsdp"),
        P("fsdp", None),
        P("fsdp", None),
        P("expert", None, "fsdp"),
    )
    return jax.shard_map(
        per_device,
        mesh=mesh,
        in_specs=placed,
        out_specs=(
            P("fsdp", "expert"),
            P("expert", None, "fsdp"),
            P("expert", None, "fsdp"),
            P("expert", None, "fsdp"),
        ),
        check_vma=False,
    )
```

```python
import functools

import jax
import jax.numpy as jnp
from jax import lax
from jax.experimental import pallas as pl
from jax.experimental.pallas import tpu as pltpu
from jax.sharding import PartitionSpec as P

CHUNKS = 2
MEBI = 1024 * 1024


def exchange(value, axis, offset):
    size = lax.axis_size(axis)
    return lax.ppermute(value, axis, [(i, i ^ offset) for i in range(size)])


def pick(value, index, axis):
    return lax.dynamic_index_in_dim(value, index, axis, keepdims=False)


def after(value, *others):
    return lax.optimization_barrier((value, others))[0]


def bits_of(size):
    return size.bit_length() - 1


def whole(shape):
    return pl.BlockSpec(shape, lambda *_: (0,) * len(shape))


def smem():
    return pl.BlockSpec(memory_space=pltpu.SMEM)


def params(mebi=16):
    return pltpu.CompilerParams(vmem_limit_bytes=mebi * MEBI)


def signs_kernel(experts, position_ref, ids_ref, out_ref):
    blocks, capacity, lanes = out_ref.shape
    tokens = ids_ref.shape[2]
    expert = position_ref[0]
    slots = lax.broadcasted_iota(jnp.int32, (capacity, tokens), 0)
    rows = lax.broadcasted_iota(jnp.int32, (lanes, tokens), 0)
    last = lax.broadcasted_iota(jnp.int32, (capacity, lanes), 1) == lanes - 1
    for b in range(blocks):
        ids = ids_ref[b]
        e0, e1, s0, s1 = ids[0:1], ids[1:2], ids[2:3], ids[3:4]
        hit0 = jnp.where((e0 == expert) & (s0 == slots), 1.0, 0.0)
        hit1 = jnp.where((e1 == expert) & (s1 == slots), 1.0, 0.0)
        table = jnp.where(e0 == rows - 1, 1.0, 0.0) - jnp.where(e1 == rows - 1, 1.0, 0.0)
        signs = lax.dot_general(
            (hit0 - hit1).astype(jnp.bfloat16),
            table.astype(jnp.bfloat16),
            (((1,), (1,)), ((), ())),
            preferred_element_type=jnp.float32,
        )
        filled = jnp.sum(hit0 + hit1, axis=1, keepdims=True)
        out_ref[b] = jnp.where(last, filled, signs)


def pack_kernel(position_ref, low_ref, high_ref, low_out, high_out):
    low_out[0] = low_ref[...]
    high_out[0] = high_ref[...]


def pack(position, branch, c, experts):
    half = branch.shape[0] // 2
    part = branch.shape[1] // experts // CHUNKS
    others = experts // 2

    def low(j, position_ref):
        return (0, (2 * j + 1 - position_ref[0] % 2) * CHUNKS + c)

    def high(j, position_ref):
        return (1, (j + others * (1 - position_ref[0] // others)) * CHUNKS + c)

    block = pl.BlockSpec((1, half, part), lambda j, position_ref: (j, 0, 0))
    shape = jax.ShapeDtypeStruct((others, half, part), jnp.bfloat16)
    return pl.pallas_call(
        pack_kernel,
        out_shape=(shape, shape),
        grid_spec=pltpu.PrefetchScalarGridSpec(
            num_scalar_prefetch=1,
            grid=(others,),
            in_specs=[pl.BlockSpec((half, part), low), pl.BlockSpec((half, part), high)],
            out_specs=(block, block),
        ),
        compiler_params=params(),
        name="pack",
    )(position, branch, branch)


def join_kernel(*refs):
    *part_refs, out_ref = refs
    part = part_refs[0].shape[1]
    for c, part_ref in enumerate(part_refs):
        out_ref[:, c * part : (c + 1) * part] = part_ref[...]


def spread_kernel(shares_ref, ids_ref, out_ref):
    experts, quarter, columns = shares_ref.shape
    blocks, _, features = out_ref.shape
    per_expert = blocks // experts
    for f in range(blocks):
        start = (f % per_expert) * features
        out_ref[f, :quarter] = shares_ref[f // per_expert, :, start : start + features]
        out_ref[f, quarter:] = ids_ref[...]


def sides_kernel(position_ref, *refs):
    *share_refs, own_ref, other_ref = refs
    for k, share_ref in enumerate(share_refs):
        place = position_ref[0] ^ k
        for side, out_ref in enumerate((own_ref, other_ref)):
            out_ref[:, place] = share_ref[:, position_ref[2] ^ side]


def dispatch_kernel(position_ref, ids_ref, extra_ref, *refs):
    *token_refs, out_ref = refs
    planes = len(token_refs)
    experts, _, part = out_ref.shape
    lanes = extra_ref.shape[0]
    count = out_ref.shape[1] - lanes
    capacity = count // planes
    tokens = ids_ref.shape[2]
    plane, core = position_ref[1], position_ref[2]
    slots = lax.broadcasted_iota(jnp.int32, (experts * capacity, tokens), 0)
    for k in range(planes):
        source = plane ^ k
        ids = ids_ref[source * 2 + core]
        code0 = ids[0:1] * capacity + ids[2:3]
        code1 = ids[1:2] * capacity + ids[3:4]
        one_hot = jnp.where((code0 == slots) | (code1 == slots), 1.0, 0.0).astype(jnp.bfloat16)
        picked = jnp.dot(one_hot, token_refs[k][...], preferred_element_type=jnp.float32)
        rows = pl.ds(pl.multiple_of(source * capacity, 16), capacity)
        out_ref[:, rows] = picked.reshape(experts, capacity, part).astype(jnp.bfloat16)
    for e in range(experts):
        out_ref[e, count:] = extra_ref[...]


def row_stats(flat_ref, side, aux_ref):
    count = flat_ref.shape[0] // 2
    experts, lanes, part = aux_ref.shape
    squares = jnp.zeros((count, part), jnp.float32)
    logits = jnp.zeros((count, lanes), jnp.float32)
    for e in range(experts):
        rows = flat_ref[side * count : (side + 1) * count, e * part : (e + 1) * part]
        aux = aux_ref[e]
        ratio = rows.astype(jnp.float32) * (1.0 / aux[0:1].astype(jnp.float32))
        squares = squares + ratio * ratio
        logits = logits + lax.dot_general(
            rows, aux, (((1,), (1,)), ((), ())), preferred_element_type=jnp.float32
        )
    total = jnp.sum(squares, axis=1, keepdims=True)
    return jnp.where(lax.broadcasted_iota(jnp.int32, logits.shape, 1) == 0, total, logits)


def row_copies(sides, flat_ref, aux_ref, sems):
    count = flat_ref.shape[0] // 2
    experts, _, part = aux_ref.shape
    copies = [
        pltpu.make_async_copy(sides[0].at[:, pl.ds(count, aux_ref.shape[1])], aux_ref, sems.at[0])
    ]
    for side, rows_ref in enumerate(sides):
        for e in range(experts):
            copies.append(
                pltpu.make_async_copy(
                    rows_ref.at[e, pl.ds(0, count)],
                    flat_ref.at[pl.ds(side * count, count), pl.ds(e * part, part)],
                    sems.at[1 + side * experts + e],
                )
            )
    return copies


def turned(flat_ref, e, part):
    return flat_ref[:, e * part : (e + 1) * part].T


def product(flat_ref, weight_ref):
    weight = weight_ref[...].reshape(flat_ref.shape[1], weight_ref.shape[3])
    return jnp.dot(flat_ref[...], weight, preferred_element_type=jnp.float32)


def shares_of(experts, tiles, t):
    return range(t * experts // tiles, (t + 1) * experts // tiles)


def early_kernel(
    tiles,
    own_ref,
    other_ref,
    gate_ref,
    up_ref,
    gate_out,
    up_out,
    stats_out,
    turned_out,
    flat_scratch,
    aux_scratch,
    sems,
):
    count = flat_scratch.shape[0] // 2
    experts, _, part = aux_scratch.shape

    for t in range(tiles):

        @pl.when(pl.program_id(0) == t)
        def _():
            if t == 0:
                copies = row_copies((own_ref, other_ref), flat_scratch, aux_scratch, sems)
                for copy in copies:
                    copy.start()
                for copy in copies:
                    copy.wait()
            gate_out[...] = product(flat_scratch, gate_ref)
            up_out[...] = product(flat_scratch, up_ref)
            for e in shares_of(experts, tiles, t):
                turned_out[e] = turned(flat_scratch, e, part)
            if t == tiles - 1:
                for side in range(2):
                    stats_out[side * count : (side + 1) * count] = row_stats(
                        flat_scratch, side, aux_scratch
                    )


def late_kernel(
    width,
    tiles,
    position_ref,
    own_ref,
    other_ref,
    turned_ref,
    gate_ref,
    up_ref,
    gate_acc,
    up_acc,
    stats_hbm,
    signs_hbm,
    cot_hbm,
    hidden_out,
    grad_gate_out,
    grad_up_out,
    flat_scratch,
    aux_scratch,
    scale_scratch,
    weight_scratch,
    gate_scratch,
    up_scratch,
    d_gate_scratch,
    d_up_scratch,
    turned_scratch,
    stats_ref,
    signs_ref,
    cot_ref,
    sems,
):
    step = pl.program_id(0)
    core = position_ref[2]
    planes, _, capacity, tile = hidden_out.shape
    count = planes * capacity
    experts, _, part = aux_scratch.shape
    lanes = stats_ref.shape[1]
    turn_copy = pltpu.make_async_copy(
        turned_ref, turned_scratch.at[:, pl.ds(0, part)], sems.at[1 + 2 * experts]
    )

    stats_copy = pltpu.make_async_copy(stats_hbm, stats_ref, sems.at[2 + 2 * experts])
    signs_copy = pltpu.make_async_copy(signs_hbm, signs_ref, sems.at[3 + 2 * experts])
    cot_copy = pltpu.make_async_copy(cot_hbm, cot_ref, sems.at[4 + 2 * experts])

    def scales():
        stats_copy.wait()
        signs_copy.wait()
        for side in range(2):
            span = slice(side * count, (side + 1) * count)
            stats = stats_ref[span] + row_stats(flat_scratch, side, aux_scratch)
            inverse = lax.rsqrt(stats[:, 0:1] / width + 1e-05)
            signs = signs_ref[:, pl.ds(core ^ side, 1)].reshape(count, lanes)
            filled = signs[:, lanes - 1 :]
            column = lax.broadcasted_iota(jnp.int32, stats.shape, 1)
            router = (column >= 1) & (column <= experts)
            margin = jnp.sum(jnp.where(router, stats * signs, 0.0), axis=1, keepdims=True)
            prob = jax.nn.sigmoid(margin * inverse).astype(jnp.bfloat16).astype(jnp.float32)
            scale_scratch[span] = inverse
            weight_scratch[span] = jnp.where(filled > 0.0, prob, 0.0)

    def units_of(t):
        columns = slice(t * tile, (t + 1) * tile)
        if t == 0:
            cot_copy.wait()
        for side in range(2):
            span = slice(side * count, (side + 1) * count)
            inverse = scale_scratch[span]
            weight = weight_scratch[span]
            gate_pre = inverse * gate_scratch[t % 2, span]
            up_pre = inverse * up_scratch[t % 2, span]
            sig_gate = jax.nn.sigmoid(gate_pre)
            act_gate = gate_pre * sig_gate
            hidden = (weight * act_gate * up_pre).astype(jnp.bfloat16)
            hidden_out[:, pl.ds(core ^ side, 1)] = hidden.reshape(planes, 1, capacity, tile)
            cot = cot_ref[:, pl.ds(core ^ side, 1), :, columns].reshape(count, tile)
            d_pre = cot.astype(jnp.float32) * (weight * inverse)
            d_gate = d_pre * up_pre * sig_gate * (1.0 + gate_pre * (1.0 - sig_gate))
            d_gate_scratch[span, columns] = d_gate.astype(jnp.bfloat16)
            d_up_scratch[span, columns] = (d_pre * act_gate).astype(jnp.bfloat16)

    def gradients(stretch):
        e = (step - tiles) % experts
        stretch_units = grad_gate_out.shape[2]
        span = slice(stretch * stretch_units, (stretch + 1) * stretch_units)
        for scratch, out in ((d_gate_scratch, grad_gate_out), (d_up_scratch, grad_up_out)):
            out[0] = jnp.dot(
                turned_scratch[e], scratch[:, span], preferred_element_type=jnp.float32
            ).astype(jnp.bfloat16)

    for t in range(tiles):

        @pl.when(step == t)
        def _():
            if t == 0:
                copies = row_copies((own_ref, other_ref), flat_scratch, aux_scratch, sems)
                for copy in copies:
                    copy.start()
                for copy in (stats_copy, signs_copy, cot_copy, turn_copy):
                    copy.start()
                for copy in copies:
                    copy.wait()
            gate_scratch[t % 2] = gate_acc[...] + product(flat_scratch, gate_ref)
            up_scratch[t % 2] = up_acc[...] + product(flat_scratch, up_ref)
            for e in shares_of(experts, tiles, t):
                turned_scratch[e, part:] = turned(flat_scratch, e, part)
            if t == 0:
                scales()
            else:
                units_of(t - 1)

    @pl.when(step == tiles)
    def _():
        turn_copy.wait()
        units_of(tiles - 1)
        gradients(0)

    for stretch in range(tiles * tile // grad_gate_out.shape[2]):
        first = tiles + stretch * experts

        @pl.when((step >= first) & (step < first + experts) & (step > tiles))
        def _():
            gradients(stretch)


def per_device(
    branch_wo,
    context,
    residual,
    norm_gain,
    router_w,
    gate_w,
    up_w,
    expert_ids,
    slot_ids,
    cot_hidden,
):
    experts = lax.axis_size("expert")
    blocks = lax.axis_size("fsdp")
    planes = blocks // 2
    expert = lax.axis_index("expert")
    block = lax.axis_index("fsdp")
    plane, core = block // 2, block % 2
    tokens, columns = context.shape
    width = columns * experts
    features = width // blocks
    capacity = cot_hidden.shape[1] // blocks
    units = cot_hidden.shape[2]
    part = columns // CHUNKS
    quarter = tokens // experts
    count = planes * capacity
    position = jnp.stack([expert, plane, core]).astype(jnp.int32)
    bits = bits_of(experts)

    lanes = experts + 2 + (-(experts + 2)) % 16
    extra = jnp.concatenate([norm_gain[None], router_w.T])
    extra = jnp.pad(extra, ((0, lanes - extra.shape[0]), (0, 0)))
    ids = jnp.concatenate([expert_ids, slot_ids], axis=1).T.astype(jnp.bfloat16)
    id_rows = ids.size // features
    ids = jnp.pad(ids.reshape(id_rows, features), ((0, -id_rows % 16), (0, 0)))

    branch = branch_wo[0]
    half = branch.shape[0] // 2
    weights = [1 << (bits - 1 - i) for i in range(bits)]
    own_bits = [(expert // weight) % 2 for weight in weights]

    def start_sum(c, h):
        def value(chosen):
            place = sum(weight * bit for weight, bit in zip(weights, chosen))
            corner = (h * half, (place * CHUNKS + c) * part)
            return lax.dynamic_slice(branch, corner, (half, part)).astype(jnp.float32)

        return value

    def joined(value, got, axis, rest):
        def total(chosen):
            chosen = [own_bits[axis] if i == axis else bit for i, bit in enumerate(chosen)]
            place = 0
            for i in rest:
                place = 2 * place + chosen[i]
            return value(chosen) + pick(got, place, 0).astype(jnp.float32)

        return total

    held = {(c, h): start_sum(c, h) for c in range(CHUNKS) for h in range(2)}
    orders = (list(range(bits))[::-1], list(range(bits)))

    def branch_sends(phase, c):
        if phase == 0:
            return pack(position, branch, c, experts)
        sends = []
        for h, order in enumerate(orders):
            rest = sorted(order[phase + 1 :])
            stacked = []
            for code in range(1 << len(rest)):
                chosen = list(own_bits)
                chosen[order[phase]] = 1 - own_bits[order[phase]]
                for at, i in enumerate(rest):
                    chosen[i] = (code >> (len(rest) - 1 - at)) & 1
                stacked.append(held[c, h](chosen).astype(jnp.bfloat16))
            sends.append(stacked[0][None] if len(stacked) == 1 else jnp.stack(stacked))
        return tuple(sends)

    def branch_exchange(phase, sends):
        return tuple(
            exchange(sends[h], "expert", weights[order[phase]]) for h, order in enumerate(orders)
        )

    def branch_add(phase, c, got):
        for h, order in enumerate(orders):
            held[c, h] = joined(held[c, h], got[h], order[phase], sorted(order[phase + 1 :]))

    def merged_of(c):
        total = jnp.concatenate([held[c, 0](own_bits), held[c, 1](own_bits)])
        return (total / experts).astype(jnp.bfloat16)

    shares = lax.all_to_all(
        context.reshape(experts, quarter, columns), "expert", split_axis=0, concat_axis=0, tiled=True
    )

    spread_shape = (blocks, quarter + ids.shape[0], features)
    to_blocks = pl.pallas_call(
        spread_kernel,
        out_shape=jax.ShapeDtypeStruct(spread_shape, jnp.bfloat16),
        in_specs=[whole(shares.shape), whole(ids.shape)],
        out_specs=whole(spread_shape),
        grid=(1,),
        compiler_params=params(),
        name="spread",
    )(shares, ids)
    got = branch_exchange(0, after(pack(position, branch, 0, experts), shares))
    branch_add(0, 0, after(got, to_blocks))
    from_blocks = lax.all_to_all(to_blocks, "fsdp", split_axis=0, concat_axis=0, tiled=True)
    for phase in range(1, bits):
        got = branch_exchange(phase, branch_sends(phase, 0))
        if phase == bits - 1:
            from_blocks, got = lax.optimization_barrier((from_blocks, got))
        branch_add(phase, 0, got)

    ids_all = from_blocks[:, quarter : quarter + id_rows].astype(jnp.int32)
    ids_all = ids_all.reshape(blocks, 4, tokens)
    own_share = from_blocks[:, :quarter]
    packed1 = branch_sends(0, 1)
    pieces = [exchange(own_share, "expert", k) if k else own_share for k in range(experts)]
    pieces, packed1 = lax.optimization_barrier((pieces, packed1))
    side_shape = (planes, experts, quarter, features)
    sides = pl.pallas_call(
        sides_kernel,
        out_shape=(jax.ShapeDtypeStruct(side_shape, jnp.bfloat16),) * 2,
        in_specs=[smem()] + [whole((planes, 2, quarter, features))] * experts,
        out_specs=(whole(side_shape),) * 2,
        grid=(1,),
        compiler_params=params(),
        name="sides",
    )(position, *[piece.reshape(planes, 2, quarter, features) for piece in pieces])
    sides = [side.reshape(planes * tokens, features) for side in sides]
    signs = pl.pallas_call(
        functools.partial(signs_kernel, experts),
        out_shape=jax.ShapeDtypeStruct((blocks, capacity, lanes), jnp.float32),
        in_specs=[smem(), whole(ids_all.shape)],
        out_specs=whole((blocks, capacity, lanes)),
        grid=(1,),
        compiler_params=params(),
        name="signs",
    )(position, ids_all).reshape(planes, 2, capacity, lanes)

    gate_view = gate_w.reshape(experts, CHUNKS, part, units)
    up_view = up_w.reshape(experts, CHUNKS, part, units)
    tile = min(256, units)
    stretch = min(512, units)
    tiles = units // tile
    def pair_of(merged):
        def attend(rows):
            out = jnp.dot(rows, merged, preferred_element_type=jnp.float32)
            return out.reshape(planes, tokens, part)

        swapped = exchange(attend(sides[1]).astype(jnp.bfloat16), "fsdp", 1)
        return attend(sides[0]) + swapped.astype(jnp.float32)

    def plane_sends(pair):
        return [pick(pair, plane ^ k, 0).astype(jnp.bfloat16) for k in range(1, planes)]

    def plane_exchange(sends):
        return [exchange(send, "fsdp", 2 * k) for k, send in enumerate(sends, 1)]

    def scaled_of(c, pair, arrived):
        span = slice(c * part, (c + 1) * part)
        hstate = residual[:, span].astype(jnp.float32) + pick(pair, plane, 0)
        for value in arrived:
            hstate = hstate + value.astype(jnp.float32)
        return (hstate * norm_gain[span].astype(jnp.float32)).astype(jnp.bfloat16)

    height = count + lanes

    def slots_of(c, own_tokens):
        return pl.pallas_call(
            dispatch_kernel,
            out_shape=jax.ShapeDtypeStruct((experts, height, part), jnp.bfloat16),
            in_specs=[smem(), whole(ids_all.shape)]
            + [pl.BlockSpec((lanes, part), lambda i, c=c: (0, c))]
            + [whole((tokens, part))] * planes,
            out_specs=whole((experts, height, part)),
            grid=(1,),
            compiler_params=params(),
            name="dispatch",
        )(position, ids_all, extra, *own_tokens)

    merged0 = merged_of(0)
    got = branch_exchange(0, packed1)
    pair0 = pair_of(merged0)
    sends0 = plane_sends(pair0)
    branch_add(0, 1, after(got, sends0))
    arrived0 = plane_exchange(sends0)
    for phase in range(1, bits):
        got = branch_exchange(phase, branch_sends(phase, 1))
        if phase < bits - 1:
            branch_add(phase, 1, got)

    scaled0 = scaled_of(0, pair0, arrived0)
    tokens0 = [scaled0] + plane_exchange([scaled0] * (planes - 1))
    if bits > 1:
        branch_add(bits - 1, 1, after(got, scaled0))
    merged1 = merged_of(1)
    merged_out = pl.pallas_call(
        join_kernel,
        out_shape=jax.ShapeDtypeStruct((features, columns), jnp.bfloat16),
        in_specs=[whole((features, part))] * CHUNKS,
        out_specs=whole((features, columns)),
        grid=(1,),
        compiler_params=params(),
        name="join",
    )(merged0, merged1)
    pair1 = pair_of(merged1)
    sends1 = plane_sends(pair1)
    arrived1 = plane_exchange(sends1)

    slots0 = slots_of(0, after(tokens0, sends1))
    scaled1 = scaled_of(1, pair1, after(arrived1, slots0))
    tokens1 = [scaled1] + plane_exchange([scaled1] * (planes - 1))
    slots1 = slots_of(1, tokens1)
    slots = (slots0, slots1)

    def to_experts(c):
        return lax.all_to_all(slots[c], "expert", split_axis=0, concat_axis=0, tiled=True)

    rows = after(to_experts(0), slots[-1], merged_out, signs)
    other = exchange(rows, "fsdp", 1)
    weight_spec = pl.BlockSpec((experts, 1, part, tile), lambda n: (0, 0, 0, n))
    sums = jax.ShapeDtypeStruct((2 * count, units), jnp.float32)
    sum_spec = pl.BlockSpec((2 * count, tile), lambda n: (0, n))
    any_spec = pl.BlockSpec(memory_space=pl.ANY)
    row_spec = pl.BlockSpec(memory_space=pltpu.HBM)
    row_scratch = [
        pltpu.VMEM((2 * count, experts * part), jnp.bfloat16),
        pltpu.VMEM((experts, lanes, part), jnp.bfloat16),
    ]
    partial = pl.pallas_call(
        functools.partial(early_kernel, tiles),
        out_shape=(
            sums,
            sums,
            jax.ShapeDtypeStruct((2 * count, lanes), jnp.float32),
            jax.ShapeDtypeStruct((experts, part, 2 * count), jnp.bfloat16),
        ),
        in_specs=[any_spec, any_spec, weight_spec, weight_spec],
        out_specs=(
            sum_spec,
            sum_spec,
            whole((2 * count, lanes)),
            whole((experts, part, 2 * count)),
        ),
        grid=(tiles,),
        scratch_shapes=row_scratch + [pltpu.SemaphoreType.DMA((1 + 2 * experts,))],
        compiler_params=params(32),
        cost_estimate=pl.CostEstimate(
            flops=8 * count * experts * part * units,
            bytes_accessed=4 * experts * part * units,
            transcendentals=0,
        ),
        name="early",
    )(rows, other, gate_view, up_view)
    rows = after(to_experts(1), partial)
    other = exchange(rows, "fsdp", 1)

    tile_of = lambda i: jnp.minimum(i, tiles - 1)
    behind = lambda i: jnp.clip(i - 1, 0, tiles - 1)
    place_of = lambda i: jnp.maximum(i - tiles, 0)
    weight_spec = pl.BlockSpec((experts, 1, part, tile), lambda i: (0, 1, 0, tile_of(i)))
    sum_spec = pl.BlockSpec((2 * count, tile), lambda i: (0, tile_of(i)))
    unit_spec = pl.BlockSpec((planes, 2, capacity, tile), lambda i: (0, 0, 0, behind(i)))
    grad_spec = pl.BlockSpec(
        (1, columns, stretch), lambda i: (place_of(i) % experts, 0, place_of(i) // experts)
    )
    grad_shape = jax.ShapeDtypeStruct((experts, columns, units), jnp.bfloat16)
    gate_sums, up_sums, stats, turned_rows = partial
    hidden, grad_gate, grad_up = pl.pallas_call(
        functools.partial(late_kernel, float(width), tiles),
        out_shape=(
            jax.ShapeDtypeStruct((planes, 2, capacity, units), jnp.bfloat16),
            grad_shape,
            grad_shape,
        ),
        in_specs=[smem(), row_spec, row_spec, any_spec]
        + [weight_spec, weight_spec, sum_spec, sum_spec]
        + [row_spec] * 3,
        out_specs=(unit_spec, grad_spec, grad_spec),
        grid=(tiles + experts * (units // stretch),),
        scratch_shapes=row_scratch
        + [
            pltpu.VMEM((2 * count, 1), jnp.float32),
            pltpu.VMEM((2 * count, 1), jnp.float32),
            pltpu.VMEM((2, 2 * count, tile), jnp.float32),
            pltpu.VMEM((2, 2 * count, tile), jnp.float32),
            pltpu.VMEM((2 * count, units), jnp.bfloat16),
            pltpu.VMEM((2 * count, units), jnp.bfloat16),
            pltpu.VMEM((experts, columns, 2 * count), jnp.bfloat16),
            pltpu.VMEM((2 * count, lanes), jnp.float32),
            pltpu.VMEM(signs.shape, jnp.float32),
            pltpu.VMEM((planes, 2, capacity, units), jnp.bfloat16),
            pltpu.SemaphoreType.DMA((5 + 2 * experts,)),
        ],
        compiler_params=params(60),
        name="late",
    )(
        position,
        rows,
        other,
        turned_rows,
        gate_view,
        up_view,
        gate_sums,
        up_sums,
        stats,
        signs,
        cot_hidden.reshape(planes, 2, capacity, units),
    )
    return (
        merged_out,
        hidden.reshape(1, -1, units),
        grad_gate.reshape(1, width, units),
        grad_up.reshape(1, width, units),
    )


def solution(mesh):
    placed = (
        P("expert", "fsdp", None),
        P("fsdp", "expert"),
        P("fsdp", "expert"),
        P("expert"),
        P("expert", None),
        P("expert", None, "fsdp"),
        P("expert", None, "fsdp"),
        P("fsdp", None),
        P("fsdp", None),
        P("expert", None, "fsdp"),
    )
    return jax.shard_map(
        per_device,
        mesh=mesh,
        in_specs=placed,
        out_specs=(
            P("fsdp", "expert"),
            P("expert", None, "fsdp"),
            P("expert", None, "fsdp"),
            P("expert", None, "fsdp"),
        ),
        check_vma=False,
    )
```
